256 devices in a mesh: lat: 16 (over z, x_lo), lon: 16 (over x_hi, y, core).
Axes of the slice: x: 4 (x_hi: 2, x_lo: 2; x = x_hi * 2 + x_lo), y: 4, z: 8, core: 2. Of those that a mesh axis runs over, the one named last changes fastest.
Arguments:
- tokens: bfloat16 [2, 384, 384, 512], P(None, 'lat', 'lon'), may hold values from -6 to 6
- norm_gain: float32 [512], replicated, may hold values from 0.25 to 1.75
- qkv_weight: bfloat16 [512, 1536], replicated, may hold values from -0.25 to 0.25
- out_weight: bfloat16 [512, 512], replicated, may hold values from -0.25 to 0.25
- bias_table: float32 [759, 8], replicated, may hold values from -4 to 320
- bias_index: int32 [144, 144], replicated, may hold values from 0 to 758
- cotangent: bfloat16 [2, 384, 384, 512], P(None, 'lat', 'lon'), may hold values from -6 to 6
Outputs:
- grad_tokens: bfloat16 [2, 384, 384, 512], P(None, 'lat', 'lon')
- grad_qkv: float32 [512, 1536], replicated
- grad_out: float32 [512, 512], replicated
- grad_bias: float32 [759, 8], replicated
- grad_gain: float32 [512], replicated
The draws below stay inside these ranges and needn't reach their ends.
All inputs are finite; a program needn't handle non-finite values.
Results may differ from the reference program's by a relative error of at most 0.015.
Values may be sent and summed in bfloat16 or wider, within the bound.
No kernel may reach another device: no remote copies, remote signals or barrier semaphores. Data moves between devices by JAX's collectives and lax.ppermute only.
A program may use at most 128 MiB of HBM per device.

```python
import jax
import jax.numpy as jnp
from jax import lax

D = 512
HEADS = 8
WZ = 2
WH = 6
WW = 12
SH = 3
SW = 6
WIN = 144
BIAS_ROWS = 759
NH = 384
NW = 384


def draw_bias_table(key, part):
    key = jax.random.fold_in(key, 7)
    base = jnp.clip(jax.random.normal(key, (BIAS_ROWS, HEADS), jnp.float32), -4.0, 4.0)
    return base


def plant(result, own_key, smallest, largest):
    longest = result.shape.index(max(result.shape))
    spots = []
    for shift in (0, 1):
        where = [jax.random.randint(jax.random.fold_in(own_key, axis), (), 0, length) for axis, length in enumerate(result.shape)]
        where[longest] = (where[longest] + shift) % result.shape[longest]
        spots.append(tuple(where))
    return result.at[spots[0]].set(smallest).at[spots[1]].set(largest)


def block_scale(stream_key, dims, cuts, least, top_value):
    factor_of, own = 1.0, jax.random.fold_in(stream_key, 6)
    for position, blocks in cuts:
        heights = jnp.exp(jax.random.uniform(jax.random.fold_in(own, position), (blocks,), jnp.float32, least / len(cuts), top_value / len(cuts)))
        factor_of = factor_of * jnp.repeat(heights, dims[position] // blocks).reshape([-1 if axis == position else 1 for axis in range(len(dims))])
    return factor_of


def noise(own_key, shape, scale, bound, shards=(), kind=jnp.bfloat16):
    result = jax.random.normal(own_key, shape, jnp.float32) * scale
    if len(shards) > 0:
        result = block_scale(own_key, shape, shards, -0.22, 0.18) * result
    return jnp.clip(result, min=-bound, max=bound).astype(kind)


def setup_inputs(seed: int = 0) -> dict:
    key_list = jax.random.split(jax.random.key(seed), 8)
    tokens = noise(key_list[0], (WZ, NH, NW, D), 1.0, 6.0, ((1, 16), (2, 16)))
    norm_gain = jnp.clip(1.0 + 0.15 * jax.random.normal(key_list[1], (D,), jnp.float32), 0.25, 1.75)
    qkv_weight = noise(key_list[2], (D, 3 * D), D ** -0.5, 0.25)
    out_weight = noise(key_list[3], (D, D), D ** -0.5, 0.25)
    bias_table = draw_bias_table(jax.random.fold_in(key_list[7], 71), 0)
    bias_index = plant(jax.random.randint(key_list[5], (WIN, WIN), 0, BIAS_ROWS), jax.random.fold_in(key_list[5], 1), 0, BIAS_ROWS - 1).astype(jnp.int32)
    cotangent = noise(key_list[6], (WZ, NH, NW, D), 1.0, 6.0, ((1, 16), (2, 16)))
    return dict(tokens=tokens, norm_gain=norm_gain, qkv_weight=qkv_weight, out_weight=out_weight, bias_table=bias_table, bias_index=bias_index, cotangent=cotangent)


def to_windows(grid):
    depth, rows_lat, cols_lon, chans = grid.shape
    parts = grid.reshape(depth, rows_lat // WH, WH, cols_lon // WW, WW, chans)
    return parts.transpose(1, 3, 0, 2, 4, 5).reshape(-1, depth * WH * WW, chans)

def from_windows(windows, depth, rows_lat, cols_lon):
    chans = windows.shape[-1]
    parts = windows.reshape(rows_lat // WH, cols_lon // WW, depth, WH, WW, chans)
    return parts.transpose(2, 0, 3, 1, 4, 5).reshape(depth, rows_lat, cols_lon, chans)

def reference(tokens, norm_gain, qkv_weight, out_weight, bias_table, bias_index, cotangent):
    depth, rows_lat, cols_lon, width = tokens.shape
    heads = bias_table.shape[1]
    head_size = width // heads
    window = bias_index.shape[0]
    scale = head_size ** (-0.5)
    floats = tokens.astype(jnp.float32)
    centred = floats - lax.optimization_barrier(jnp.mean(floats, axis=-1, keepdims=True))
    inverse_std = lax.rsqrt(lax.optimization_barrier(jnp.mean(centred * centred, axis=-1, keepdims=True)) + 1e-05)
    normalised = centred * inverse_std
    normed = (normalised * norm_gain).astype(jnp.bfloat16)
    rolled_grid = jnp.roll(normed, (-SH, -SW), axis=(1, 2))
    rolled_cgrid = jnp.roll(cotangent, (-SH, -SW), axis=(1, 2))
    rolled_in = to_windows(rolled_grid)
    rolled_cot = to_windows(rolled_cgrid)
    flat_in = rolled_in.reshape(-1, width)
    flat_cot = rolled_cot.reshape(-1, width)
    projected = jnp.dot(flat_in, qkv_weight, preferred_element_type=jnp.float32).astype(jnp.bfloat16)
    projected = projected.reshape(-1, window, 3, heads, head_size)
    grad_attn = jnp.dot(flat_cot, out_weight.T, preferred_element_type=jnp.float32).astype(jnp.bfloat16)
    grad_attn = grad_attn.reshape(-1, window, heads, head_size)
    lat_rows = lax.broadcasted_iota(jnp.int32, (depth, rows_lat, cols_lon, 1), 1)
    polar = (lat_rows >= rows_lat - SH).astype(jnp.int32)
    labels = to_windows(polar)[..., 0]
    bias = jnp.transpose(bias_table[bias_index], (2, 0, 1)).astype(jnp.float32)
    count = projected.shape[0]
    group = 4 if count % 4 == 0 else 2 if count % 2 == 0 else 1

    def blocks(array):
        return array.reshape((count // group, group) + array.shape[1:])

    def step(carry, block):
        queries, keys_win, values_win, grad_block, label_block = block
        qf = queries.astype(jnp.float32)
        kf = keys_win.astype(jnp.float32)
        vf = values_win.astype(jnp.float32)
        gf = grad_block.astype(jnp.float32)
        scores = jnp.einsum('gqhd,gkhd->ghqk', qf, kf) * scale + bias[None]
        same = label_block[:, None, :, None] == label_block[:, None, None, :]
        scores = jnp.where(same, scores, jnp.float32(-1e+30))
        probs = jax.nn.softmax(scores, axis=-1)
        probs_low = probs.astype(jnp.bfloat16)
        plf = probs_low.astype(jnp.float32)
        attended = jnp.einsum('ghqk,gkhd->gqhd', plf, vf).astype(jnp.bfloat16)
        grad_probs = jnp.einsum('gqhd,gkhd->ghqk', gf, vf)
        grad_scores = probs * (grad_probs - lax.optimization_barrier(jnp.sum(probs * grad_probs, axis=-1, keepdims=True)))
        scores_low = grad_scores.astype(jnp.bfloat16).astype(jnp.float32)
        grad_values = jnp.einsum('ghqk,gqhd->gkhd', plf, gf).astype(jnp.bfloat16)
        grad_query = (jnp.einsum('ghqk,gkhd->gqhd', scores_low, kf) * scale).astype(jnp.bfloat16)
        grad_key = (jnp.einsum('ghqk,gqhd->gkhd', scores_low, qf) * scale).astype(jnp.bfloat16)
        stacked = jnp.stack([grad_query, grad_key, grad_values], axis=2)
        return (carry + lax.optimization_barrier(jnp.sum(grad_scores, axis=0)), (attended, stacked))
    inputs = (blocks(projected[:, :, 0]), blocks(projected[:, :, 1]), blocks(projected[:, :, 2]), blocks(grad_attn), blocks(labels))
    bias_sum, outputs = lax.scan(step, jnp.zeros((heads, window, window), jnp.float32), inputs)
    attended = outputs[0].reshape(-1, width)
    grad_proj = outputs[1].reshape(-1, 3 * width)
    grad_out = jnp.dot(attended.T, flat_cot, preferred_element_type=jnp.float32)
    grad_qkv = jnp.dot(flat_in.T, grad_proj, preferred_element_type=jnp.float32)
    grad_bias = jax.ops.segment_sum(jnp.transpose(bias_sum, (1, 2, 0)).reshape(window * window, heads), bias_index.reshape(-1).astype(jnp.int32), num_segments=bias_table.shape[0])
    back_proj = jnp.dot(grad_proj, qkv_weight.T, preferred_element_type=jnp.float32).astype(jnp.bfloat16)
    back_grid = from_windows(back_proj.reshape(count, window, width), depth, rows_lat, cols_lon)
    grad_normed = jnp.roll(back_grid, (SH, SW), axis=(1, 2))
    grad_floats = grad_normed.astype(jnp.float32)
    grad_gain = lax.optimization_barrier(jnp.sum(grad_floats * normalised, axis=(0, 1, 2)))
    grad_hat = grad_floats * norm_gain
    centre_term = lax.optimization_barrier(jnp.mean(grad_hat, axis=-1, keepdims=True))
    slope_term = lax.optimization_barrier(jnp.mean(grad_hat * normalised, axis=-1, keepdims=True))
    grad_tokens = cotangent.astype(jnp.float32) + inverse_std * (grad_hat - centre_term - normalised * slope_term)
    return (grad_tokens.astype(jnp.bfloat16), grad_qkv, grad_out, grad_bias, grad_gain)
```

```python
import jax
import jax.numpy as jnp
from jax import lax
from jax.experimental import pallas as pl
from jax.experimental.pallas import tpu as pltpu
from jax.sharding import PartitionSpec as P

WH = 6
WW = 12
SH = 3
SW = 6
F32 = jnp.float32
BF16 = jnp.bfloat16
MIB = 1024 * 1024

LAST, CORE, X, Y = range(4)

NT = (((1,), (1,)), ((), ()))


def dot(a, b):
    return jnp.dot(a, b, preferred_element_type=F32)


def dot_nt(a, b):
    return lax.dot_general(a, b, NT, preferred_element_type=F32)


class Geometry:
    def __init__(self, depth, rows, cols):
        self.depth, self.rows, self.cols = depth, rows, cols
        self.cells = depth * rows * cols
        self.win = depth * WH * WW
        self.nwin = self.cells // self.win
        self.wins_lon = cols // WW
        self.wins_lat = rows // WH
        self.n_rows = depth * SH * (cols - SW)
        self.n_cols = depth * (rows - SH) * SW
        self.n_corner = depth * SH * SW

    def local(self, z, r, c):
        return (z * self.rows + r) * self.cols + c

    def rim_row(self, z, r):
        return (z * SH + r) * (self.cols - SW)

    def rim_col(self, z, r):
        return (z * (self.rows - SH) + r) * SW

    def corner(self, z, r):
        return (z * SH + r) * SW

    def cell(self, z, r, c):
        window = (r // WH) * self.wins_lon + c // WW
        return window * self.win + (z * WH + r % WH) * WW + c % WW


def pad16(n):
    return (n + 15) // 16 * 16


def forward_pieces(geo, z, r):
    own = geo.cols - SW
    if r < geo.rows - SH:
        first = ("local", geo.local(z, r + SH, SW), 0, own)
        second = ("cols", geo.rim_col(z, r), own, SW)
    else:
        first = ("rows", geo.rim_row(z, r - geo.rows + SH), 0, own)
        second = ("corner", geo.corner(z, r - geo.rows + SH), own, SW)
    return (first, second)


def window_cuts(start, length):
    at = start
    while at < start + length:
        stop = min(start + length, (at // WW + 1) * WW)
        yield at, stop - at
        at = stop


def pack_kernel(geo, tok_ref, cot_ref, rows_ref, cols_ref, corner_ref, top, left, wide, slim, buf, sems):
    n_rows, n_cols, n_corner = geo.n_rows, geo.n_cols, geo.n_corner
    base_cols = pad16(2 * n_rows)
    base_corner = base_cols + pad16(2 * n_cols)
    own = geo.cols - SW
    copies = []
    for which, ref in enumerate((tok_ref, cot_ref)):
        for part, (src, dst) in enumerate(
            (
                (ref.at[:, 0:SH], top.at[which]),
                (ref.at[:, SH : geo.rows, 0:16], left.at[which]),
            )
        ):
            copy = pltpu.make_async_copy(src, dst, sems.at[which, part])
            copy.start()
            copies.append(copy)
    buf[base_cols - 16 : base_cols] = jnp.zeros((16, buf.shape[1]), F32)
    buf[base_corner - 16 : base_corner] = jnp.zeros((16, buf.shape[1]), F32)
    buf[-16:] = jnp.zeros((16, buf.shape[1]), F32)
    for copy in copies:
        copy.wait()
    wide[...] = top[...].astype(F32)
    slim[...] = left[...].astype(F32)
    for which in range(2):
        for z in range(geo.depth):
            for r in range(SH):
                at = which * n_rows + geo.rim_row(z, r)
                buf[at : at + own] = wide[which, z, r, SW:]
                at = base_corner + which * n_corner + geo.corner(z, r)
                buf[at : at + SW] = wide[which, z, r, 0:SW]
            for r in range(geo.rows - SH):
                at = base_cols + which * n_cols + geo.rim_col(z, r)
                buf[at : at + SW] = slim[which, z, r, 0:SW]
    rows_ref[...] = buf[0:base_cols].astype(BF16)
    cols_ref[...] = buf[base_cols:base_corner].astype(BF16)
    corner_ref[...] = buf[base_corner : base_corner + pad16(2 * n_corner)].astype(BF16)


BANDS = 8
SPAN = 96


def band_of(index):
    band = (index * 683) >> 16
    return band, index - band * SPAN


def lookup_kernel(heads, idx_ref, table_ref, bias_ref, split):
    win = idx_ref.shape[0]
    rows = heads * BANDS
    rest = table_ref[...]
    for part in range(3):
        low = rest.astype(BF16).astype(F32)
        for band in range(BANDS):
            at = part * rows + band * heads
            split[at : at + heads, :] = low[:, band * SPAN : (band + 1) * SPAN]
        rest = rest - low
    table = split[...].astype(BF16)
    iota = lax.broadcasted_iota(jnp.int32, (SPAN, win), 0)

    def step(block, carry):
        start = pl.multiple_of(block * 8, 8)
        band, place = band_of(idx_ref[pl.ds(start, 8), :])
        for j in range(8):
            onehot = jnp.where(iota == place[j : j + 1, :], 1.0, 0.0).astype(BF16)
            found = dot(table, onehot)
            found = (found[:rows] + found[rows : 2 * rows]) + found[2 * rows :]
            mine = jnp.broadcast_to(band[j : j + 1, :], (heads, win))
            total = jnp.zeros((heads, win), F32)
            for b in range(BANDS):
                total = jnp.where(mine == b, found[b * heads : (b + 1) * heads], total)
            for h in range(heads):
                bias_ref[h, pl.ds(start + j, 1), :] = total[h : h + 1]
        return carry

    lax.fori_loop(0, win // 8, step, 0)


def table_kernel(heads, idx_ref, sum_ref, gain_ref, out_ref, acc, line):
    win = idx_ref.shape[0]
    rows = heads * BANDS
    iota = lax.broadcasted_iota(jnp.int32, (SPAN, win), 0)
    bands = lax.broadcasted_iota(jnp.int32, (BANDS, win), 0)
    acc[...] = jnp.zeros_like(acc)

    def step(block, carry):
        start = pl.multiple_of(block * 8, 8)
        band, place = band_of(idx_ref[pl.ds(start, 8), :])
        tops, rests = [], []
        for h in range(heads):
            slab = sum_ref[h, pl.ds(start, 8), :]
            top = slab.astype(BF16).astype(F32)
            tops.append(top)
            rests.append(slab - top)
        total = None
        for j in range(8):
            onehot = jnp.where(iota == place[j : j + 1, :], 1.0, 0.0).astype(BF16)
            keep = jnp.where(bands == band[j : j + 1, :], 1.0, 0.0)
            spread = [p[h][j : j + 1, :] * keep for p in (tops, rests) for h in range(heads)]
            term = dot_nt(jnp.concatenate(spread, axis=0).astype(BF16), onehot)
            total = term if total is None else total + term
        acc[...] += total[:rows] + total[rows:]
        return carry

    lax.fori_loop(0, win // 8, step, 0)
    for h in range(heads):
        for b in range(BANDS):
            line[h : h + 1, b * SPAN : (b + 1) * SPAN] = acc[h * BANDS + b : h * BANDS + b + 1, :]
    width = out_ref.shape[1]
    more = BANDS * SPAN - width
    gain = jnp.sum(gain_ref[...], axis=0, keepdims=True)
    out_ref[0:heads, :] = line[:, :width]
    out_ref[heads:, 0:more] = line[:, width:]
    out_ref[heads:, more:] = jnp.zeros((16 - heads, width - more), F32)
    out_ref[heads : heads + 1, more:] = gain[:, : width - more]
    out_ref[heads + 1 : heads + 2, more:] = gain[:, width - more :]


def main_kernel(
    geo, heads, info_ref, tok_ref, cot_ref, rows_ref, cols_ref, corner_ref, gain_ref, wqkv_ref,
    wout_ref, bias_ref,
    send_ref, keep_ref, bsum_ref, dproj, ftok, inv, cotb,
    loc, rim_rows, rim_cols, rim_corner, fcot, normed, proj, gatt, att_t, dq_t,
    bias2, normed_t, gout, grads,
):
    width = ftok.shape[1]
    win = geo.win
    head_size = width // heads
    scale = head_size ** (-0.5)

    for which, (ref, dst) in enumerate(((tok_ref, ftok), (cot_ref, fcot))):
        loc[...] = ref[...].astype(F32)
        if which == 0:
            rim_rows[...] = rows_ref[...].astype(F32)
            rim_cols[...] = cols_ref[...].astype(F32)
            rim_corner[...] = corner_ref[...].astype(F32)
        sources = {
            "local": (loc, 0),
            "rows": (rim_rows, which * geo.n_rows),
            "cols": (rim_cols, which * geo.n_cols),
            "corner": (rim_corner, which * geo.n_corner),
        }
        for z in range(geo.depth):
            for r in range(geo.rows):
                for name, first, column, length in forward_pieces(geo, z, r):
                    src, base = sources[name]
                    for at, count in window_cuts(column, length):
                        begin = base + first + at - column
                        cell = geo.cell(z, r, at)
                        dst[cell : cell + count] = src[begin : begin + count]

    gain = gain_ref[...]

    spot = lax.broadcasted_iota(jnp.int32, (win, win), 0)
    other = lax.broadcasted_iota(jnp.int32, (win, win), 1)
    half = WH * WW
    polar_a = jnp.where(spot >= half, spot - half, spot) >= (WH - SH) * WW
    polar_b = jnp.where(other >= half, other - half, other) >= (WH - SH) * WW
    flag_a = jnp.where(polar_a, 1.0, 0.0)
    flag_b = jnp.where(polar_b, 1.0, 0.0)
    mask = jnp.where(flag_a == flag_b, 0.0, -1e30)
    for h in range(heads):
        plain = bias_ref[h]
        bias2[0, h] = plain
        bias2[1, h] = plain + mask
        bsum_ref[h] = jnp.zeros((win, win), F32)
    gout[...] = jnp.zeros_like(gout)

    def norm_step(w, carry):
        at = pl.ds(pl.multiple_of(w * win, 16), win)
        x = ftok[at, :]
        centred = x - jnp.mean(x, axis=-1, keepdims=True)
        istd = lax.rsqrt(jnp.mean(centred * centred, axis=-1, keepdims=True) + 1e-05)
        unit = centred * istd
        ftok[at, :] = unit
        inv[at, :] = jnp.broadcast_to(istd, (win, 128))
        normed[at, :] = (unit * gain).astype(BF16)
        cotb[at, :] = fcot[at, :].astype(BF16)
        return carry

    lax.fori_loop(0, geo.nwin, norm_step, 0)

    def proj_step(w, carry):
        at = pl.ds(pl.multiple_of(w * (2 * win), 16), 2 * win)
        x = normed[at, :]
        for part in range(3):
            cols = slice(part * width, (part + 1) * width)
            proj[at, cols] = dot(x, wqkv_ref[:, cols]).astype(BF16)
        gatt[at, :] = dot_nt(cotb[at, :], wout_ref[...]).astype(BF16)
        return carry

    lax.fori_loop(0, geo.nwin // 2, proj_step, 0)

    lane = lax.broadcasted_iota(jnp.int32, (win, 128), 1)
    lower = lane < head_size
    polar_from = geo.nwin - geo.wins_lon

    def attend(w, carry):
        at = pl.ds(pl.multiple_of(w * win, 16), win)
        sel = jnp.where(w >= polar_from, info_ref[LAST], 0)
        k_t = proj[at, width : 2 * width].T
        v_t = proj[at, 2 * width :].T
        for pair in range(heads // 2):
            cols = slice(pair * 128, (pair + 1) * 128)
            q = proj[at, cols] * BF16(scale)
            k = proj[at, width + pair * 128 : width + (pair + 1) * 128]
            v = proj[at, 2 * width + pair * 128 : 2 * width + (pair + 1) * 128]
            g = gatt[at, cols]
            dv = None
            dk = None
            for side in range(2):
                h = 2 * pair + side
                keep = lower if side == 0 else jnp.logical_not(lower)
                qm = jnp.where(keep, q, BF16(0))
                gm = jnp.where(keep, g, BF16(0))
                scores = dot_nt(k, qm) + bias2[sel, h]
                top = jnp.max(scores, axis=0, keepdims=True)
                grown = jnp.exp(scores - top)
                probs = grown * (1.0 / jnp.sum(grown, axis=0, keepdims=True))
                probs_low = probs.astype(BF16)
                gprobs = dot_nt(v, gm)
                weighted = jnp.sum(probs * gprobs, axis=0, keepdims=True)
                gscores = probs * (gprobs - weighted)
                bsum_ref[h] += gscores
                scores_low = gscores.astype(BF16)
                feats = slice(h * head_size, (h + 1) * head_size)
                att_t[feats, :] = dot(v_t[feats], probs_low).astype(BF16)
                dq_t[feats, :] = (dot(k_t[feats], scores_low) * scale).astype(BF16)
                dv_term = dot(probs_low, gm)
                dk_term = dot(scores_low, qm)
                dv = dv_term if dv is None else dv + dv_term
                dk = dk_term if dk is None else dk + dk_term
            dproj[at, width + pair * 128 : width + (pair + 1) * 128] = dk.astype(BF16)
            dproj[at, 2 * width + pair * 128 : 2 * width + (pair + 1) * 128] = dv.astype(BF16)
        dproj[at, 0:width] = dq_t[...].T
        gout[...] += dot(att_t[...], cotb[at, :])
        return carry

    lax.fori_loop(0, geo.nwin, attend, 0)

    grads[1, width:, :] = gout[...].astype(BF16)
    for block in range(geo.cells // 128):
        rows = slice(block * 128, (block + 1) * 128)
        normed_t[:, rows] = normed[rows, :].T

    for part in range(3):
        half, first = part // 2, part % 2 * width
        for sub in range(2):
            cols = slice(part * width + sub * 256, part * width + (sub + 1) * 256)
            grads[half, first : first + width, sub * 256 : (sub + 1) * 256] = dot(
                normed_t[...], dproj[:, cols]
            ).astype(BF16)
    keep_ref[...] = grads[info_ref[CORE]]
    send_ref[...] = grads[1 - info_ref[CORE]]


def back_kernel(geo, dproj, unit_ref, inv, cotb, gain_ref, wqkv_ref, gtok_ref, ggain_ref):
    win, width = geo.win, unit_ref.shape[1]
    gain = gain_ref[...]

    def back_step(w, total):
        at = pl.ds(pl.multiple_of(w * win, 16), win)
        gn = dot_nt(dproj[at, :], wqkv_ref[...]).astype(BF16).astype(F32)
        unit = unit_ref[at, :]
        prod = gn * unit
        hat = gn * gain
        centre = jnp.mean(hat, axis=-1, keepdims=True)
        slope = jnp.mean(prod * gain, axis=-1, keepdims=True)
        istd = inv[at, 0:1]
        cot = cotb[at, :].astype(F32)
        gtok_ref[at, :] = (cot + istd * (hat - centre - unit * slope)).astype(BF16)
        return total + jnp.sum(prod.reshape(win // 8, 8, width), axis=0)

    ggain_ref[...] = lax.fori_loop(0, geo.nwin, back_step, jnp.zeros((8, width), F32))


def unpack_send_kernel(geo, gtok_ref, rows_ref, cols_ref, corner_ref, fg, buf):
    base_cols = pad16(geo.n_rows)
    base_corner = base_cols + pad16(geo.n_cols)
    fg[...] = gtok_ref[...].astype(F32)
    buf[...] = jnp.zeros_like(buf)
    bases = {"rows": 0, "cols": base_cols, "corner": base_corner}
    for z in range(geo.depth):
        for r in range(geo.rows):
            for name, first, column, length in forward_pieces(geo, z, r):
                if name == "local":
                    continue
                for at, count in window_cuts(column, length):
                    to = bases[name] + first + at - column
                    cell = geo.cell(z, r, at)
                    buf[to : to + count] = fg[cell : cell + count]
    rows_ref[...] = buf[0:base_cols].astype(BF16)
    cols_ref[...] = buf[base_cols:base_corner].astype(BF16)
    corner_ref[...] = buf[base_corner : base_corner + pad16(geo.n_corner)].astype(BF16)


def assemble_kernel(geo, gtok_ref, rows_ref, cols_ref, corner_ref, out_ref, fg, rr, rc, rk, grid):
    fg[...] = gtok_ref[...].astype(F32)
    rr[...] = rows_ref[...].astype(F32)
    rc[...] = cols_ref[...].astype(F32)
    rk[...] = corner_ref[...].astype(F32)
    own = geo.cols - SW
    for z in range(geo.depth):
        for r in range(geo.rows):
            for name, first, column, length in forward_pieces(geo, z, r):
                if name != "local":
                    continue
                for at, count in window_cuts(column, length):
                    to = first + at - column
                    cell = geo.cell(z, r, at)
                    grid[to : to + count] = fg[cell : cell + count]
        for r in range(SH):
            to = geo.local(z, r, SW)
            grid[to : to + own] = rr[geo.rim_row(z, r) : geo.rim_row(z, r) + own]
            to = geo.local(z, r, 0)
            grid[to : to + SW] = rk[geo.corner(z, r) : geo.corner(z, r) + SW]
        for r in range(geo.rows - SH):
            to = geo.local(z, r + SH, 0)
            grid[to : to + SW] = rc[geo.rim_col(z, r) : geo.rim_col(z, r) + SW]
    out_ref[...] = grid[...].astype(BF16)


def call(kernel, out_shapes, scratch, n_in, limit, smem_first=False, cost=None):
    specs = [pl.BlockSpec(memory_space=pltpu.VMEM)] * n_in
    if smem_first:
        specs[0] = pl.BlockSpec(memory_space=pltpu.SMEM)
    return pl.pallas_call(
        kernel,
        out_shape=out_shapes,
        in_specs=specs,
        out_specs=jax.tree.map(lambda s: pl.BlockSpec(memory_space=pltpu.VMEM), out_shapes),
        scratch_shapes=scratch,
        compiler_params=pltpu.CompilerParams(vmem_limit_bytes=limit),
        cost_estimate=cost,
    )


def shape(dims, dtype):
    return jax.ShapeDtypeStruct(dims, dtype)


def moved(value, lat_step, lon_step):
    lats, lons = lax.axis_size("lat"), lax.axis_size("lon")
    pairs = []
    for a in range(lats):
        for o in range(lons):
            target = ((a - lat_step) % lats) * lons + (o - lon_step) % lons
            pairs.append((a * lons + o, target))
    return lax.ppermute(value, ("lat", "lon"), pairs)


class Chips:
    def __init__(self):
        self.lats, self.lons = lax.axis_size("lat"), lax.axis_size("lon")
        self.nz, self.nx, self.ny = self.lats // 2, 4, self.lons // 4

    def split(self, device):
        lat, lon = device // self.lons, device % self.lons
        x = lon // (2 * self.ny) * 2 + lat % 2
        return lat // 2, x, lon // 2 % self.ny, lon % 2

    def join(self, z, x, y, core):
        return (z * 2 + x % 2) * self.lons + (x // 2 * self.ny + y) * 2 + core

    def send(self, value, change):
        pairs = []
        for device in range(self.lats * self.lons):
            z, x, y, core = change(*self.split(device))
            pairs.append((device, self.join(z, x, y, core)))
        return lax.ppermute(value, ("lat", "lon"), pairs)

    def core(self, value):
        return self.send(value, lambda z, x, y, c: (z, x, y, 1 - c))

    def x(self, value, step):
        return self.send(value, lambda z, x, y, c: (z, (x + step) % self.nx, y, c))

    def y(self, value, step):
        return self.send(value, lambda z, x, y, c: (z, x, (y + step) % self.ny, c))

    def z(self, value, bit):
        return self.send(value, lambda z, x, y, c: (z ^ bit, x, y, c))


def pair_sum_kernel(ny, nx, info_ref, keep_ref, recv_ref, *outs):
    rows = keep_ref.shape[0] // 2
    for base, count, place, refs in ((0, ny, Y, outs[:ny]), (rows, nx, X, outs[ny:])):
        piece = rows // count
        for k, ref in enumerate(refs):
            part = (info_ref[place] + k) & (count - 1)
            at = pl.ds(pl.multiple_of(base + part * piece, 16), piece)
            ref[...] = (keep_ref[at, :].astype(F32) + recv_ref[at, :].astype(F32)).astype(BF16)


def total_of(refs):
    total = refs[0][...].astype(F32)
    for ref in refs[1:]:
        total += ref[...].astype(F32)
    return total


def cross_sum_kernel(ny, nx, info_ref, *refs):
    ins_a, ins_b = refs[:ny], refs[ny : ny + nx]
    outs_a, outs_b = refs[ny + nx : ny + 2 * nx], refs[ny + 2 * nx : 2 * ny + 2 * nx]
    hold = refs[-1]
    for ins, outs, count, place in ((ins_a, outs_a, nx, X), (ins_b, outs_b, ny, Y)):
        hold[...] = total_of(ins)
        piece = hold.shape[0] // count
        for k, ref in enumerate(outs):
            part = (info_ref[place] + k) & (count - 1)
            at = pl.ds(pl.multiple_of(part * piece, 16), piece)
            ref[...] = hold[at, :].astype(BF16)


SMALL = 16


def put_small(ref, base, total):
    top = total.astype(BF16)
    ref[base : base + SMALL] = top
    ref[base + SMALL : base + 2 * SMALL] = (total - top.astype(F32)).astype(BF16)


def small_of(refs, base):
    total = None
    for ref in refs:
        for part in range(2):
            at = base + part * SMALL
            term = ref[at : at + SMALL].astype(F32)
            total = term if total is None else total + term
    return total


def join_sum_kernel(ny, nx, *refs):
    piece = refs[0].shape[0]
    small_ref, out_ref = refs[-2:]
    out_ref[0:piece] = total_of(refs[:nx]).astype(BF16)
    out_ref[piece : 2 * piece] = total_of(refs[nx : nx + ny]).astype(BF16)
    put_small(out_ref, 2 * piece, small_ref[...])


def z_sum_kernel(mine_ref, got_ref, *outs):
    rows = mine_ref.shape[0] - 2 * SMALL
    total = (mine_ref[0:rows].astype(F32) + got_ref[0:rows].astype(F32)).astype(BF16)
    last = small_of((mine_ref, got_ref), rows)
    if len(outs) == 1:
        outs[0][0:rows] = total
    else:
        outs[0][...] = total[: rows // 2]
        outs[1][0 : rows // 2] = total[rows // 2 :]
    put_small(outs[-1], outs[-1].shape[0] - 2 * SMALL, last)


def gather_kernel(ny, nx, info_ref, *refs):
    a_ref, b_ref = refs[-2:]
    ins_a, ins_b = refs[:nx], refs[nx : nx + ny]
    piece = ins_a[0].shape[0]
    for ins, out, count, place in ((ins_a, a_ref, nx, X), (ins_b, b_ref, ny, Y)):
        for k, ref in enumerate(ins):
            part = (info_ref[place] + (count - k)) & (count - 1)
            out[pl.ds(pl.multiple_of(part * piece, 16), piece), :] = ref[0:piece]
    put_small(b_ref, ny * piece, small_of(ins_b, piece))


def place_kernel(ny, nx, info_ref, *refs):
    ins, (gqkv_ref, gout_ref, line_ref, gain_ref) = refs[:-4], refs[-4:]
    width = gout_ref.shape[1]
    piece = ins[0].shape[0]
    core = info_ref[CORE]

    total = small_of(ins[ny : ny + nx], piece)
    more = line_ref.shape[1] - width
    line_ref[:, 0:width] = total[0:8]
    line_ref[:, width:] = total[8:, 0:more]
    gain_ref[:, 0 : width - more] = total[8:9, more:]
    gain_ref[:, width - more :] = total[9:10, more:]

    def place(owner, group):
        columns = {(0, 0): 0, (0, 1): width, (1, 0): 2 * width}
        for mine in range(2):
            half = owner if mine else 1 - owner
            base = 0 if mine else ny + nx
            for which, (start, count, axis) in enumerate(((0, ny, Y), (ny, nx, X))):
                for k in range(count):
                    part = (info_ref[axis] + (count - k)) & (count - 1)
                    at = pl.ds(pl.multiple_of(part * piece, 16), piece)
                    value = group[base + start + k][0:piece].astype(F32)
                    if (half, which) in columns:
                        first = columns[(half, which)]
                        gqkv_ref[at, first : first + width] = value
                    else:
                        gout_ref[at, :] = value

    @pl.when(core == 0)
    def _():
        place(0, ins)

    @pl.when(core == 1)
    def _():
        place(1, ins)


def per_device(tokens, norm_gain, qkv_weight, out_weight, bias_table, bias_index, cotangent):
    depth, rows_lat, cols_lon, width = tokens.shape
    entries, heads = bias_table.shape
    geo = Geometry(depth, rows_lat, cols_lon)
    win, cells = geo.win, geo.cells
    tok = tokens.reshape(cells, width)
    cot = cotangent.reshape(cells, width)

    n_rows, n_cols, n_corner = pad16(2 * geo.n_rows), pad16(2 * geo.n_cols), pad16(2 * geo.n_corner)
    rim = pl.pallas_call(
        lambda *refs: pack_kernel(geo, *refs),
        out_shape=[shape((n, width), BF16) for n in (n_rows, n_cols, n_corner)],
        in_specs=[pl.BlockSpec(memory_space=pl.ANY)] * 2,
        out_specs=[pl.BlockSpec(memory_space=pltpu.VMEM)] * 3,
        scratch_shapes=[
            pltpu.VMEM((2, depth, SH, cols_lon, width), BF16),
            pltpu.VMEM((2, depth, rows_lat - SH, 16, width), BF16),
            pltpu.VMEM((2, depth, SH, cols_lon, width), F32),
            pltpu.VMEM((2, depth, rows_lat - SH, 16, width), F32),
            pltpu.VMEM((n_rows + n_cols + n_corner, width), F32),
            pltpu.SemaphoreType.DMA((2, 2)),
        ],
        compiler_params=pltpu.CompilerParams(vmem_limit_bytes=60 * MIB),
    )(tokens, cotangent)
    rim = (moved(rim[0], 1, 0), moved(rim[1], 0, 1), moved(rim[2], 1, 1))

    index_t = bias_index.T
    table = jnp.pad(bias_table.T, ((0, 0), (0, BANDS * SPAN - entries)))
    bias = call(
        lambda *refs: lookup_kernel(heads, *refs),
        shape((heads, win, win), F32),
        [pltpu.VMEM((3 * heads * BANDS, SPAN), F32)],
        2,
        8 * MIB,
        cost=pl.CostEstimate(flops=4 * 10**9, bytes_accessed=10**6, transcendentals=0),
    )(index_t, table)

    chips = Chips()
    ny, nx = chips.ny, chips.nx
    lat, lon = lax.axis_index("lat"), lax.axis_index("lon")
    is_last = (lat == chips.lats - 1).astype(jnp.int32)
    info = jnp.stack([is_last, lon % 2, lon // (2 * ny) * 2 + lat % 2, lon // 2 % ny])
    half_rows = 2 * width
    big = 34 * MIB
    small_limit = 10 * MIB

    send, keep, bias_sum, grad_proj, unit, inv, cot_win = call(
        lambda *refs: main_kernel(geo, heads, *refs),
        [
            shape((half_rows, width), BF16),
            shape((half_rows, width), BF16),
            shape((heads, win, win), F32),
            shape((cells, 3 * width), BF16),
            shape((cells, width), F32),
            shape((cells, 128), F32),
            shape((cells, width), BF16),
        ],
        [
            pltpu.VMEM((cells, width), F32),
            pltpu.VMEM((n_rows, width), F32),
            pltpu.VMEM((n_cols, width), F32),
            pltpu.VMEM((n_corner, width), F32),
            pltpu.VMEM((cells, width), F32),
            pltpu.VMEM((cells, width), BF16),
            pltpu.VMEM((cells, 3 * width), BF16),
            pltpu.VMEM((cells, width), BF16),
            pltpu.VMEM((width, win), BF16),
            pltpu.VMEM((width, win), BF16),
            pltpu.VMEM((2, heads, win, win), F32),
            pltpu.VMEM((width, cells), BF16),
            pltpu.VMEM((width, width), F32),
            pltpu.VMEM((2, half_rows, width), BF16),
        ],
        10,
        big,
        smem_first=True,
    )(info, tok, cot, *rim, norm_gain.reshape(1, width), qkv_weight, out_weight, bias)

    got = chips.core(send)
    piece = half_rows // 2 // ny
    outs = call(
        lambda *refs: pair_sum_kernel(ny, nx, *refs),
        [shape((piece, width), BF16)] * (ny + nx),
        [],
        3,
        small_limit,
        smem_first=True,
    )(info, keep, got)

    outs, grad_proj = lax.optimization_barrier((outs, grad_proj))
    got_a = [outs[0]] + [chips.y(outs[k], k) for k in range(1, ny)]
    got_b = [outs[ny]] + [chips.x(outs[ny + k], k) for k in range(1, nx)]
    gtok, gain_part = call(
        lambda *refs: back_kernel(geo, *refs),
        [shape((cells, width), BF16), shape((8, width), F32)],
        [],
        6,
        small_limit,
        cost=pl.CostEstimate(flops=6 * 10**9, bytes_accessed=10**7, transcendentals=0),
    )(grad_proj, unit, inv, cot_win, norm_gain.reshape(1, width), qkv_weight)
    b_rows, b_cols, b_corner = pad16(geo.n_rows), pad16(geo.n_cols), pad16(geo.n_corner)
    back = call(
        lambda *refs: unpack_send_kernel(geo, *refs),
        [shape((n, width), BF16) for n in (b_rows, b_cols, b_corner)],
        [
            pltpu.VMEM((cells, width), F32),
            pltpu.VMEM((b_rows + b_cols + b_corner, width), F32),
        ],
        1,
        small_limit,
    )(gtok)
    outs = call(
        lambda *refs: cross_sum_kernel(ny, nx, *refs),
        [shape((piece // nx, width), BF16)] * nx + [shape((piece // ny, width), BF16)] * ny,
        [pltpu.VMEM((piece, width), F32)],
        1 + ny + nx,
        small_limit,
        smem_first=True,
    )(info, *got_a, *got_b)

    outs, bias_sum, back = lax.optimization_barrier((outs, bias_sum, back))
    got_a = [outs[0]] + [chips.x(outs[k], k) for k in range(1, nx)]
    got_b = [outs[nx]] + [chips.y(outs[nx + k], k) for k in range(1, ny)]
    small = call(
        lambda *refs: table_kernel(heads, *refs),
        shape((SMALL, width), F32),
        [pltpu.VMEM((heads * BANDS, SPAN), F32), pltpu.VMEM((heads, BANDS * SPAN), F32)],
        3,
        small_limit,
        cost=pl.CostEstimate(flops=3 * 10**9, bytes_accessed=10**6, transcendentals=0),
    )(index_t, bias_sum, gain_part)
    small = small + chips.core(small)
    part = piece // nx
    mine = call(
        lambda *refs: join_sum_kernel(ny, nx, *refs),
        shape((2 * part + 2 * SMALL, width), BF16),
        [],
        ny + nx + 1,
        small_limit,
    )(*got_a, *got_b, small)

    bit = 1
    while 2 * bit < chips.nz:
        mine = call(z_sum_kernel, shape(mine.shape, BF16), [], 2, small_limit)(
            mine, chips.z(mine, bit)
        )
        bit *= 2
    own_a, own_b = call(
        z_sum_kernel,
        [shape((part, width), BF16), shape((part + 2 * SMALL, width), BF16)],
        [],
        2,
        small_limit,
    )(mine, chips.z(mine, bit))
    own_a, own_b, back = lax.optimization_barrier((own_a, own_b, back))

    got_a = [own_a] + [chips.x(own_a, k) for k in range(1, nx)]
    got_b = [own_b] + [chips.y(own_b, k) for k in range(1, ny)]
    own_a, own_b = call(
        lambda *refs: gather_kernel(ny, nx, *refs),
        [shape((piece, width), BF16), shape((piece + 2 * SMALL, width), BF16)],
        [],
        1 + ny + nx,
        small_limit,
        smem_first=True,
    )(info, *got_a, *got_b)
    got = [own_a] + [chips.y(own_a, k) for k in range(1, ny)]
    got += [own_b] + [chips.x(own_b, k) for k in range(1, nx)]
    theirs = [chips.core(value) for value in got]
    own_a, back = lax.optimization_barrier((own_a, back))
    back = (moved(back[0], -1, 0), moved(back[1], 0, -1), moved(back[2], -1, -1))

    grad_tokens = call(
        lambda *refs: assemble_kernel(geo, *refs),
        shape((cells, width), BF16),
        [
            pltpu.VMEM((cells, width), F32),
            pltpu.VMEM((b_rows, width), F32),
            pltpu.VMEM((b_cols, width), F32),
            pltpu.VMEM((b_corner, width), F32),
            pltpu.VMEM((cells, width), F32),
        ],
        4,
        small_limit,
    )(gtok, *back)
    grad_qkv, grad_out, line, grad_gain = call(
        lambda *refs: place_kernel(ny, nx, *refs),
        [
            shape((width, 3 * width), F32),
            shape((width, width), F32),
            shape((heads, BANDS * SPAN), F32),
            shape((1, width), F32),
        ],
        [],
        1 + 2 * (ny + nx),
        small_limit,
        smem_first=True,
    )(info, *got, *theirs)
    grad_bias = line.T[:entries]
    return (grad_tokens.reshape(tokens.shape), grad_qkv, grad_out, grad_bias, grad_gain.reshape(width))


def solution(mesh):
    in_specs = (P(None, "lat", "lon", None), P(), P(), P(), P(), P(), P(None, "lat", "lon", None))
    out_specs = (P(None, "lat", "lon", None), P(), P(), P(), P())
    return jax.shard_map(
        per_device, mesh=mesh, in_specs=in_specs, out_specs=out_specs, check_vma=False
    )
```

```python
import jax
import jax.numpy as jnp
from jax import lax
from jax.experimental import pallas as pl
from jax.experimental.pallas import tpu as pltpu
from jax.sharding import PartitionSpec as P

WH = 6
WW = 12
SH = 3
SW = 6
F32 = jnp.float32
BF16 = jnp.bfloat16
MIB = 1024 * 1024

LAST, CORE, X, Y = range(4)

NT = (((1,), (1,)), ((), ()))


def dot(a, b):
    return jnp.dot(a, b, preferred_element_type=F32)


def dot_nt(a, b):
    return lax.dot_general(a, b, NT, preferred_element_type=F32)


class Geometry:
    def __init__(self, depth, rows, cols):
        self.depth, self.rows, self.cols = depth, rows, cols
        self.cells = depth * rows * cols
        self.win = depth * WH * WW
        self.nwin = self.cells // self.win
        self.wins_lon = cols // WW
        self.wins_lat = rows // WH
        self.n_rows = depth * SH * (cols - SW)
        self.n_cols = depth * (rows - SH) * SW
        self.n_corner = depth * SH * SW

    def local(self, z, r, c):
        return (z * self.rows + r) * self.cols + c

    def rim_row(self, z, r):
        return (z * SH + r) * (self.cols - SW)

    def rim_col(self, z, r):
        return (z * (self.rows - SH) + r) * SW

    def corner(self, z, r):
        return (z * SH + r) * SW

    def cell(self, z, r, c):
        window = (r // WH) * self.wins_lon + c // WW
        return window * self.win + (z * WH + r % WH) * WW + c % WW


def pad16(n):
    return (n + 15) // 16 * 16


def forward_pieces(geo, z, r):
    own = geo.cols - SW
    if r < geo.rows - SH:
        first = ("local", geo.local(z, r + SH, SW), 0, own)
        second = ("cols", geo.rim_col(z, r), own, SW)
    else:
        first = ("rows", geo.rim_row(z, r - geo.rows + SH), 0, own)
        second = ("corner", geo.corner(z, r - geo.rows + SH), own, SW)
    return (first, second)


def window_cuts(start, length):
    at = start
    while at < start + length:
        stop = min(start + length, (at // WW + 1) * WW)
        yield at, stop - at
        at = stop


def pack_kernel(geo, tok_ref, cot_ref, rows_ref, cols_ref, corner_ref, top, left, wide, slim, buf, sems):
    n_rows, n_cols, n_corner = geo.n_rows, geo.n_cols, geo.n_corner
    base_cols = pad16(2 * n_rows)
    base_corner = base_cols + pad16(2 * n_cols)
    own = geo.cols - SW
    copies = []
    for which, ref in enumerate((tok_ref, cot_ref)):
        for part, (src, dst) in enumerate(
            (
                (ref.at[:, 0:SH], top.at[which]),
                (ref.at[:, SH : geo.rows, 0:16], left.at[which]),
            )
        ):
            copy = pltpu.make_async_copy(src, dst, sems.at[which, part])
            copy.start()
            copies.append(copy)
    buf[base_cols - 16 : base_cols] = jnp.zeros((16, buf.shape[1]), F32)
    buf[base_corner - 16 : base_corner] = jnp.zeros((16, buf.shape[1]), F32)
    buf[-16:] = jnp.zeros((16, buf.shape[1]), F32)
    for copy in copies:
        copy.wait()
    wide[...] = top[...].astype(F32)
    slim[...] = left[...].astype(F32)
    for which in range(2):
        for z in range(geo.depth):
            for r in range(SH):
                at = which * n_rows + geo.rim_row(z, r)
                buf[at : at + own] = wide[which, z, r, SW:]
                at = base_corner + which * n_corner + geo.corner(z, r)
                buf[at : at + SW] = wide[which, z, r, 0:SW]
            for r in range(geo.rows - SH):
                at = base_cols + which * n_cols + geo.rim_col(z, r)
                buf[at : at + SW] = slim[which, z, r, 0:SW]
    rows_ref[...] = buf[0:base_cols].astype(BF16)
    cols_ref[...] = buf[base_cols:base_corner].astype(BF16)
    corner_ref[...] = buf[base_corner : base_corner + pad16(2 * n_corner)].astype(BF16)


BANDS = 8
SPAN = 96


def band_of(index):
    band = (index * 683) >> 16
    return band, index - band * SPAN


def lookup_kernel(heads, raw_ref, table_ref, bias_ref, idx_ref, split):
    win = idx_ref.shape[0]
    rows = heads * BANDS
    entries = table_ref.shape[1]
    idx_ref[...] = raw_ref[...].T
    split[...] = jnp.zeros_like(split)
    rest = table_ref[...]
    for part in range(3):
        low = rest.astype(BF16).astype(F32)
        for band in range(BANDS):
            at = part * rows + band * heads
            stop = min(entries, (band + 1) * SPAN)
            split[at : at + heads, 0 : stop - band * SPAN] = low[:, band * SPAN : stop]
        rest = rest - low
    table = split[...].astype(BF16)
    iota = lax.broadcasted_iota(jnp.int32, (SPAN, win), 0)

    def step(block, carry):
        start = pl.multiple_of(block * 8, 8)
        band, place = band_of(idx_ref[pl.ds(start, 8), :])
        for j in range(8):
            onehot = jnp.where(iota == place[j : j + 1, :], 1.0, 0.0).astype(BF16)
            found = dot(table, onehot)
            found = (found[:rows] + found[rows : 2 * rows]) + found[2 * rows :]
            mine = jnp.broadcast_to(band[j : j + 1, :], (heads, win))
            total = jnp.zeros((heads, win), F32)
            for b in range(BANDS):
                total = jnp.where(mine == b, found[b * heads : (b + 1) * heads], total)
            for h in range(heads):
                bias_ref[h, pl.ds(start + j, 1), :] = total[h : h + 1]
        return carry

    lax.fori_loop(0, win // 8, step, 0)


def table_kernel(heads, idx_ref, sum_ref, gsum_ref, gain_ref, out_ref, acc, line):
    win = idx_ref.shape[0]
    rows = heads * BANDS
    iota = lax.broadcasted_iota(jnp.int32, (SPAN, win), 0)
    bands = lax.broadcasted_iota(jnp.int32, (BANDS, win), 0)
    acc[...] = jnp.zeros_like(acc)

    def step(block, carry):
        start = pl.multiple_of(block * 8, 8)
        band, place = band_of(idx_ref[pl.ds(start, 8), :])
        tops, rests = [], []
        for h in range(heads):
            slab = sum_ref[h, pl.ds(start, 8), :]
            top = slab.astype(BF16).astype(F32)
            tops.append(top)
            rests.append(slab - top)
        total = None
        for j in range(8):
            onehot = jnp.where(iota == place[j : j + 1, :], 1.0, 0.0).astype(BF16)
            keep = jnp.where(bands == band[j : j + 1, :], 1.0, 0.0)
            spread = [p[h][j : j + 1, :] * keep for p in (tops, rests) for h in range(heads)]
            term = dot_nt(jnp.concatenate(spread, axis=0).astype(BF16), onehot)
            total = term if total is None else total + term
        acc[...] += total[:rows] + total[rows:]
        return carry

    lax.fori_loop(0, win // 8, step, 0)
    for h in range(heads):
        for b in range(BANDS):
            line[h : h + 1, b * SPAN : (b + 1) * SPAN] = acc[h * BANDS + b : h * BANDS + b + 1, :]
    width = out_ref.shape[1]
    more = BANDS * SPAN - width
    gain = jnp.sum(gsum_ref[...].T, axis=0, keepdims=True) / gain_ref[...]
    out_ref[0:heads, :] = line[:, :width]
    out_ref[heads:, 0:more] = line[:, width:]
    out_ref[heads:, more:] = jnp.zeros((16 - heads, width - more), F32)
    out_ref[heads : heads + 1, more:] = gain[:, : width - more]
    out_ref[heads + 1 : heads + 2, more:] = gain[:, width - more :]


def main_kernel(
    geo, heads, info_ref, tok_ref, cot_ref, rows_ref, cols_ref, corner_ref, gain_ref, wqkv_hbm,
    wout_hbm, bias_ref,
    send_ref, keep_ref, bsum_ref, dproj, ftok, inv, cotb, gsum_ref,
    loc, rim_rows, rim_cols, rim_corner, fcot, normed, proj, gatt, att_t, dq_t,
    bias2, normed_t, gout, grads, wqkv_ref, wout_ref, sems,
):
    copies = [
        pltpu.make_async_copy(wqkv_hbm, wqkv_ref, sems.at[0]),
        pltpu.make_async_copy(wout_hbm, wout_ref, sems.at[1]),
    ]
    for copy in copies:
        copy.start()
    width = ftok.shape[1]
    win = geo.win
    head_size = width // heads
    scale = head_size ** (-0.5)

    for which, (ref, dst) in enumerate(((tok_ref, ftok), (cot_ref, fcot))):
        loc[...] = ref[...].astype(F32)
        if which == 0:
            rim_rows[...] = rows_ref[...].astype(F32)
            rim_cols[...] = cols_ref[...].astype(F32)
            rim_corner[...] = corner_ref[...].astype(F32)
        sources = {
            "local": (loc, 0),
            "rows": (rim_rows, which * geo.n_rows),
            "cols": (rim_cols, which * geo.n_cols),
            "corner": (rim_corner, which * geo.n_corner),
        }
        for z in range(geo.depth):
            for r in range(geo.rows):
                for name, first, column, length in forward_pieces(geo, z, r):
                    src, base = sources[name]
                    for at, count in window_cuts(column, length):
                        begin = base + first + at - column
                        cell = geo.cell(z, r, at)
                        dst[cell : cell + count] = src[begin : begin + count]

    gain = gain_ref[...]

    spot = lax.broadcasted_iota(jnp.int32, (win, win), 0)
    other = lax.broadcasted_iota(jnp.int32, (win, win), 1)
    half = WH * WW
    polar_a = jnp.where(spot >= half, spot - half, spot) >= (WH - SH) * WW
    polar_b = jnp.where(other >= half, other - half, other) >= (WH - SH) * WW
    flag_a = jnp.where(polar_a, 1.0, 0.0)
    flag_b = jnp.where(polar_b, 1.0, 0.0)
    mask = jnp.where(flag_a == flag_b, 0.0, -1e30)
    for h in range(heads):
        plain = bias_ref[h]
        bias2[0, h] = plain
        bias2[1, h] = plain + mask
        bsum_ref[h] = jnp.zeros((win, win), F32)
    gout[...] = jnp.zeros_like(gout)

    def norm_step(w, carry):
        at = pl.ds(pl.multiple_of(w * win, 16), win)
        x = ftok[at, :]
        centred = x - jnp.mean(x, axis=-1, keepdims=True)
        istd = lax.rsqrt(jnp.mean(centred * centred, axis=-1, keepdims=True) + 1e-05)
        unit = centred * istd
        ftok[at, :] = unit
        inv[at, :] = jnp.broadcast_to(istd, (win, 128))
        normed[at, :] = (unit * gain).astype(BF16)
        cotb[at, :] = fcot[at, :].astype(BF16)
        return carry

    lax.fori_loop(0, geo.nwin, norm_step, 0)
    for copy in copies:
        copy.wait()

    def proj_step(w, carry):
        at = pl.ds(pl.multiple_of(w * (2 * win), 16), 2 * win)
        x = normed[at, :]
        for part in range(3):
            cols = slice(part * width, (part + 1) * width)
            proj[at, cols] = dot(x, wqkv_ref[:, cols]).astype(BF16)
        gatt[at, :] = dot_nt(cotb[at, :], wout_ref[...]).astype(BF16)
        return carry

    lax.fori_loop(0, geo.nwin // 2, proj_step, 0)

    lane = lax.broadcasted_iota(jnp.int32, (win, 128), 1)
    lower = lane < head_size
    polar_from = geo.nwin - geo.wins_lon

    def attend(w, carry):
        at = pl.ds(pl.multiple_of(w * win, 16), win)
        sel = jnp.where(w >= polar_from, info_ref[LAST], 0)
        k_t = proj[at, width : 2 * width].T
        v_t = proj[at, 2 * width :].T
        for pair in range(heads // 2):
            cols = slice(pair * 128, (pair + 1) * 128)
            q = proj[at, cols] * BF16(scale)
            k = proj[at, width + pair * 128 : width + (pair + 1) * 128]
            v = proj[at, 2 * width + pair * 128 : 2 * width + (pair + 1) * 128]
            g = gatt[at, cols]
            dv = None
            dk = None
            for side in range(2):
                h = 2 * pair + side
                keep = lower if side == 0 else jnp.logical_not(lower)
                qm = jnp.where(keep, q, BF16(0))
                gm = jnp.where(keep, g, BF16(0))
                scores = dot_nt(k, qm) + bias2[sel, h]
                top = jnp.max(scores, axis=0, keepdims=True)
                grown = jnp.exp(scores - top)
                probs = grown * (1.0 / jnp.sum(grown, axis=0, keepdims=True))
                probs_low = probs.astype(BF16)
                gprobs = dot_nt(v, gm)
                weighted = jnp.sum(probs * gprobs, axis=0, keepdims=True)
                gscores = probs * (gprobs - weighted)
                bsum_ref[h] += gscores
                scores_low = gscores.astype(BF16)
                feats = slice(h * head_size, (h + 1) * head_size)
                att_t[feats, :] = dot(v_t[feats], probs_low).astype(BF16)
                dq_t[feats, :] = (dot(k_t[feats], scores_low) * scale).astype(BF16)
                dv_term = dot(probs_low, gm)
                dk_term = dot(scores_low, qm)
                dv = dv_term if dv is None else dv + dv_term
                dk = dk_term if dk is None else dk + dk_term
            dproj[at, width + pair * 128 : width + (pair + 1) * 128] = dk.astype(BF16)
            dproj[at, 2 * width + pair * 128 : 2 * width + (pair + 1) * 128] = dv.astype(BF16)
        dproj[at, 0:width] = dq_t[...].T
        gout[...] += dot(att_t[...], cotb[at, :])
        return carry

    lax.fori_loop(0, geo.nwin, attend, 0)

    grads[1, width:, :] = gout[...].astype(BF16)
    for block in range(geo.cells // 128):
        rows = slice(block * 128, (block + 1) * 128)
        normed_t[:, rows] = normed[rows, :].T

    gsum = jnp.zeros((width, 128), F32)
    for part in range(3):
        half, first = part // 2, part % 2 * width
        for sub in range(2):
            cols = slice(part * width + sub * 256, part * width + (sub + 1) * 256)
            term = dot(normed_t[...], dproj[:, cols])
            grads[half, first : first + width, sub * 256 : (sub + 1) * 256] = term.astype(BF16)
            term = term * wqkv_ref[:, cols].astype(F32)
            gsum = gsum + (term[:, :128] + term[:, 128:])
    gsum_ref[...] = gsum
    keep_ref[...] = grads[info_ref[CORE]]
    send_ref[...] = grads[1 - info_ref[CORE]]


def back_kernel(geo, first, count, dproj, unit_ref, inv, cotb, gain_ref, wqkv_ref, gtok_ref):
    win = geo.win
    gain = gain_ref[...]

    def back_step(w, carry):
        at = pl.ds(pl.multiple_of((first + w) * win, 16), win)
        gn = dot_nt(dproj[at, :], wqkv_ref[...]).astype(BF16).astype(F32)
        unit = unit_ref[at, :]
        hat = gn * gain
        centre = jnp.mean(hat, axis=-1, keepdims=True)
        slope = jnp.mean(hat * unit, axis=-1, keepdims=True)
        istd = inv[at, 0:1]
        cot = cotb[at, :].astype(F32)
        to = pl.ds(pl.multiple_of(w * win, 16), win)
        gtok_ref[to, :] = (cot + istd * (hat - centre - unit * slope)).astype(BF16)
        return carry

    lax.fori_loop(0, count, back_step, 0)


def unpack_send_kernel(geo, low_ref, high_ref, rows_ref, cols_ref, corner_ref, fg, buf):
    base_cols = pad16(geo.n_rows)
    base_corner = base_cols + pad16(geo.n_cols)
    half = low_ref.shape[0]
    fg[0:half] = low_ref[...].astype(F32)
    fg[half:] = high_ref[...].astype(F32)
    buf[...] = jnp.zeros_like(buf)
    bases = {"rows": 0, "cols": base_cols, "corner": base_corner}
    for z in range(geo.depth):
        for r in range(geo.rows):
            for name, first, column, length in forward_pieces(geo, z, r):
                if name == "local":
                    continue
                for at, count in window_cuts(column, length):
                    to = bases[name] + first + at - column
                    cell = geo.cell(z, r, at)
                    buf[to : to + count] = fg[cell : cell + count]
    rows_ref[...] = buf[0:base_cols].astype(BF16)
    cols_ref[...] = buf[base_cols:base_corner].astype(BF16)
    corner_ref[...] = buf[base_corner : base_corner + pad16(geo.n_corner)].astype(BF16)


def assemble_kernel(geo, low_ref, high_ref, rows_ref, cols_ref, corner_ref, out_ref, fg, rr, rc, rk, grid):
    half = low_ref.shape[0]
    fg[0:half] = low_ref[...].astype(F32)
    fg[half:] = high_ref[...].astype(F32)
    rr[...] = rows_ref[...].astype(F32)
    rc[...] = cols_ref[...].astype(F32)
    rk[...] = corner_ref[...].astype(F32)
    own = geo.cols - SW
    for z in range(geo.depth):
        for r in range(geo.rows):
            for name, first, column, length in forward_pieces(geo, z, r):
                if name != "local":
                    continue
                for at, count in window_cuts(column, length):
                    to = first + at - column
                    cell = geo.cell(z, r, at)
                    grid[to : to + count] = fg[cell : cell + count]
        for r in range(SH):
            to = geo.local(z, r, SW)
            grid[to : to + own] = rr[geo.rim_row(z, r) : geo.rim_row(z, r) + own]
            to = geo.local(z, r, 0)
            grid[to : to + SW] = rk[geo.corner(z, r) : geo.corner(z, r) + SW]
        for r in range(geo.rows - SH):
            to = geo.local(z, r + SH, 0)
            grid[to : to + SW] = rc[geo.rim_col(z, r) : geo.rim_col(z, r) + SW]
    out_ref[...] = grid[...].astype(BF16)


def call(kernel, out_shapes, scratch, n_in, limit, smem_first=False, cost=None):
    specs = [pl.BlockSpec(memory_space=pltpu.VMEM)] * n_in
    if smem_first:
        specs[0] = pl.BlockSpec(memory_space=pltpu.SMEM)
    return pl.pallas_call(
        kernel,
        out_shape=out_shapes,
        in_specs=specs,
        out_specs=jax.tree.map(lambda s: pl.BlockSpec(memory_space=pltpu.VMEM), out_shapes),
        scratch_shapes=scratch,
        compiler_params=pltpu.CompilerParams(vmem_limit_bytes=limit),
        cost_estimate=cost,
    )


def shape(dims, dtype):
    return jax.ShapeDtypeStruct(dims, dtype)


def moved(value, lat_step, lon_step):
    lats, lons = lax.axis_size("lat"), lax.axis_size("lon")
    pairs = []
    for a in range(lats):
        for o in range(lons):
            target = ((a - lat_step) % lats) * lons + (o - lon_step) % lons
            pairs.append((a * lons + o, target))
    return lax.ppermute(value, ("lat", "lon"), pairs)


class Chips:
    def __init__(self):
        self.lats, self.lons = lax.axis_size("lat"), lax.axis_size("lon")
        self.nz, self.nx, self.ny = self.lats // 2, 4, self.lons // 4

    def split(self, device):
        lat, lon = device // self.lons, device % self.lons
        x = lon // (2 * self.ny) * 2 + lat % 2
        return lat // 2, x, lon // 2 % self.ny, lon % 2

    def join(self, z, x, y, core):
        return (z * 2 + x % 2) * self.lons + (x // 2 * self.ny + y) * 2 + core

    def send(self, value, change):
        pairs = []
        for device in range(self.lats * self.lons):
            z, x, y, core = change(*self.split(device))
            pairs.append((device, self.join(z, x, y, core)))
        return lax.ppermute(value, ("lat", "lon"), pairs)

    def core(self, value):
        return self.send(value, lambda z, x, y, c: (z, x, y, 1 - c))

    def x(self, value, step):
        return self.send(value, lambda z, x, y, c: (z, (x + step) % self.nx, y, c))

    def y(self, value, step):
        return self.send(value, lambda z, x, y, c: (z, x, (y + step) % self.ny, c))

    def z(self, value, bit):
        return self.send(value, lambda z, x, y, c: (z ^ (2 * bit - 1), x, y, c))


def pair_sum_kernel(ny, nx, info_ref, keep_ref, recv_ref, *outs):
    rows = keep_ref.shape[0] // 2
    for base, count, place, refs in ((0, ny, Y, outs[:ny]), (rows, nx, X, outs[ny:])):
        piece = rows // count
        for k, ref in enumerate(refs):
            part = (info_ref[place] + k) & (count - 1)
            at = pl.ds(pl.multiple_of(base + part * piece, 16), piece)
            ref[...] = (keep_ref[at, :].astype(F32) + recv_ref[at, :].astype(F32)).astype(BF16)


def total_of(refs):
    total = refs[0][...].astype(F32)
    for ref in refs[1:]:
        total += ref[...].astype(F32)
    return total


def cross_sum_kernel(ny, nx, info_ref, *refs):
    ins_a, ins_b = refs[:ny], refs[ny : ny + nx]
    outs_a, outs_b = refs[ny + nx : ny + 2 * nx], refs[ny + 2 * nx : 2 * ny + 2 * nx]
    hold = refs[-1]
    for ins, outs, count, place in ((ins_a, outs_a, nx, X), (ins_b, outs_b, ny, Y)):
        hold[...] = total_of(ins)
        piece = hold.shape[0] // count
        for k, ref in enumerate(outs):
            part = (info_ref[place] + k) & (count - 1)
            at = pl.ds(pl.multiple_of(part * piece, 16), piece)
            ref[...] = hold[at, :].astype(BF16)


SMALL = 16


def put_small(ref, base, total):
    top = total.astype(BF16)
    ref[base : base + SMALL] = top
    ref[base + SMALL : base + 2 * SMALL] = (total - top.astype(F32)).astype(BF16)


def small_of(refs, base):
    total = None
    for ref in refs:
        for part in range(2):
            at = base + part * SMALL
            term = ref[at : at + SMALL].astype(F32)
            total = term if total is None else total + term
    return total


def join_sum_kernel(ny, nx, *refs):
    piece = refs[0].shape[0]
    small_ref, out_ref = refs[-2:]
    out_ref[0:piece] = total_of(refs[:nx]).astype(BF16)
    out_ref[piece : 2 * piece] = total_of(refs[nx : nx + ny]).astype(BF16)
    put_small(out_ref, 2 * piece, small_ref[...])


def z_sum_kernel(mine_ref, got_ref, *outs):
    rows = mine_ref.shape[0] - 2 * SMALL
    total = (mine_ref[0:rows].astype(F32) + got_ref[0:rows].astype(F32)).astype(BF16)
    last = small_of((mine_ref, got_ref), rows)
    if len(outs) == 1:
        outs[0][0:rows] = total
    else:
        outs[0][...] = total[: rows // 2]
        outs[1][0 : rows // 2] = total[rows // 2 :]
    put_small(outs[-1], outs[-1].shape[0] - 2 * SMALL, last)


def gather_kernel(ny, nx, info_ref, *refs):
    a_ref, b_ref = refs[-2:]
    ins_a, ins_b = refs[:nx], refs[nx : nx + ny]
    piece = ins_a[0].shape[0]
    for ins, out, count, place in ((ins_a, a_ref, nx, X), (ins_b, b_ref, ny, Y)):
        for k, ref in enumerate(ins):
            part = (info_ref[place] + (count - k)) & (count - 1)
            out[pl.ds(pl.multiple_of(part * piece, 16), piece), :] = ref[0:piece]
    put_small(b_ref, ny * piece, small_of(ins_b, piece))


def merge_kernel(count, place, with_small, info_ref, *refs):
    ins, outs = refs[:count], refs[count:]
    out_ref = outs[0]
    width = out_ref.shape[1]
    piece = out_ref.shape[0] // count
    for k, ref in enumerate(ins):
        part = (info_ref[place] + (count - k)) & (count - 1)
        out_ref[pl.ds(pl.multiple_of(part * piece, 16), piece), :] = ref[0:piece]
    if with_small:
        line_ref, gain_ref = outs[1:]
        total = small_of(ins, piece)
        more = line_ref.shape[1] - width
        line_ref[:, 0:width] = total[0:8]
        line_ref[:, width:] = total[8:, 0:more]
        gain_ref[:, 0 : width - more] = total[8:9, more:]
        gain_ref[:, width - more :] = total[9:10, more:]


def place_kernel(mine, info_ref, a_ref, b_ref, *refs):
    gqkv_ref, gout_ref, hold, sems = refs[-4:]
    width = gout_ref.shape[1]
    core = info_ref[CORE]
    half = core if mine else 1 - core
    steps = 4
    rows = width // steps

    def write(targets):
        copies = []
        for which, ref in enumerate((a_ref, b_ref)):
            for step in range(steps):
                at = slice(step * rows, (step + 1) * rows)
                hold[which, at] = ref[at].astype(F32)
                copy = pltpu.make_async_copy(
                    hold.at[which, at], targets[which].at[at], sems.at[which, step]
                )
                copy.start()
                copies.append(copy)
        for copy in copies:
            copy.wait()

    @pl.when(half == 0)
    def _():
        write((gqkv_ref.at[:, 0:width], gqkv_ref.at[:, width : 2 * width]))

    @pl.when(half == 1)
    def _():
        write((gqkv_ref.at[:, 2 * width :], gout_ref))


def per_device(tokens, norm_gain, qkv_weight, out_weight, bias_table, bias_index, cotangent):
    depth, rows_lat, cols_lon, width = tokens.shape
    entries, heads = bias_table.shape
    geo = Geometry(depth, rows_lat, cols_lon)
    win, cells = geo.win, geo.cells
    tok = tokens.reshape(cells, width)
    cot = cotangent.reshape(cells, width)

    n_rows, n_cols, n_corner = pad16(2 * geo.n_rows), pad16(2 * geo.n_cols), pad16(2 * geo.n_corner)
    rim = pl.pallas_call(
        lambda *refs: pack_kernel(geo, *refs),
        out_shape=[shape((n, width), BF16) for n in (n_rows, n_cols, n_corner)],
        in_specs=[pl.BlockSpec(memory_space=pl.ANY)] * 2,
        out_specs=[pl.BlockSpec(memory_space=pltpu.VMEM)] * 3,
        scratch_shapes=[
            pltpu.VMEM((2, depth, SH, cols_lon, width), BF16),
            pltpu.VMEM((2, depth, rows_lat - SH, 16, width), BF16),
            pltpu.VMEM((2, depth, SH, cols_lon, width), F32),
            pltpu.VMEM((2, depth, rows_lat - SH, 16, width), F32),
            pltpu.VMEM((n_rows + n_cols + n_corner, width), F32),
            pltpu.SemaphoreType.DMA((2, 2)),
        ],
        compiler_params=pltpu.CompilerParams(vmem_limit_bytes=60 * MIB),
    )(tokens, cotangent)
    rim = (moved(rim[0], 1, 0), moved(rim[1], 0, 1), moved(rim[2], 1, 1))

    bias, index_t = call(
        lambda *refs: lookup_kernel(heads, *refs),
        [shape((heads, win, win), F32), shape((win, win), jnp.int32)],
        [pltpu.VMEM((3 * heads * BANDS, SPAN), F32)],
        2,
        8 * MIB,
        cost=pl.CostEstimate(flops=4 * 10**9, bytes_accessed=10**6, transcendentals=0),
    )(bias_index, bias_table.T)

    chips = Chips()
    ny, nx = chips.ny, chips.nx
    lat, lon = lax.axis_index("lat"), lax.axis_index("lon")
    is_last = (lat == chips.lats - 1).astype(jnp.int32)
    info = jnp.stack([is_last, lon % 2, lon // (2 * ny) * 2 + lat % 2, lon // 2 % ny])
    half_rows = 2 * width
    big = 36 * MIB
    small_limit = 10 * MIB

    vmem, smem = pl.BlockSpec(memory_space=pltpu.VMEM), pl.BlockSpec(memory_space=pltpu.SMEM)
    hbm = pl.BlockSpec(memory_space=pl.ANY)
    send, keep, bias_sum, grad_proj, unit, inv, cot_win, gain_sum = pl.pallas_call(
        lambda *refs: main_kernel(geo, heads, *refs),
        in_specs=[smem] + [vmem] * 6 + [hbm, hbm, vmem],
        out_specs=[vmem] * 8,
        compiler_params=pltpu.CompilerParams(vmem_limit_bytes=big),
        out_shape=[
            shape((half_rows, width), BF16),
            shape((half_rows, width), BF16),
            shape((heads, win, win), F32),
            shape((cells, 3 * width), BF16),
            shape((cells, width), F32),
            shape((cells, 128), F32),
            shape((cells, width), BF16),
            shape((width, 128), F32),
        ],
        scratch_shapes=[
            pltpu.VMEM((cells, width), F32),
            pltpu.VMEM((n_rows, width), F32),
            pltpu.VMEM((n_cols, width), F32),
            pltpu.VMEM((n_corner, width), F32),
            pltpu.VMEM((cells, width), F32),
            pltpu.VMEM((cells, width), BF16),
            pltpu.VMEM((cells, 3 * width), BF16),
            pltpu.VMEM((cells, width), BF16),
            pltpu.VMEM((width, win), BF16),
            pltpu.VMEM((width, win), BF16),
            pltpu.VMEM((2, heads, win, win), F32),
            pltpu.VMEM((width, cells), BF16),
            pltpu.VMEM((width, width), F32),
            pltpu.VMEM((2, half_rows, width), BF16),
            pltpu.VMEM((width, 3 * width), BF16),
            pltpu.VMEM((width, width), BF16),
            pltpu.SemaphoreType.DMA((2,)),
        ],
    )(info, tok, cot, *rim, norm_gain.reshape(1, width), qkv_weight, out_weight, bias)

    got = chips.core(send)
    piece = half_rows // 2 // ny
    outs = call(
        lambda *refs: pair_sum_kernel(ny, nx, *refs),
        [shape((piece, width), BF16)] * (ny + nx),
        [],
        3,
        small_limit,
        smem_first=True,
    )(info, keep, got)

    outs, bias_sum = lax.optimization_barrier((outs, bias_sum))
    got_a = [outs[0]] + [chips.y(outs[k], k) for k in range(1, ny)]
    got_b = [outs[ny]] + [chips.x(outs[ny + k], k) for k in range(1, nx)]
    gain_row = norm_gain.reshape(1, width)
    small = call(
        lambda *refs: table_kernel(heads, *refs),
        shape((SMALL, width), F32),
        [pltpu.VMEM((heads * BANDS, SPAN), F32), pltpu.VMEM((heads, BANDS * SPAN), F32)],
        4,
        small_limit,
        cost=pl.CostEstimate(flops=3 * 10**9, bytes_accessed=10**6, transcendentals=0),
    )(index_t, bias_sum, gain_sum, gain_row)
    outs = call(
        lambda *refs: cross_sum_kernel(ny, nx, *refs),
        [shape((piece // nx, width), BF16)] * nx + [shape((piece // ny, width), BF16)] * ny,
        [pltpu.VMEM((piece, width), F32)],
        1 + ny + nx,
        small_limit,
        smem_first=True,
    )(info, *got_a, *got_b)

    got_a = [outs[0]] + [chips.x(outs[k], k) for k in range(1, nx)]
    got_b = [outs[nx]] + [chips.y(outs[nx + k], k) for k in range(1, ny)]
    small = small + chips.core(small)
    part = piece // nx
    mine = call(
        lambda *refs: join_sum_kernel(ny, nx, *refs),
        shape((2 * part + 2 * SMALL, width), BF16),
        [],
        ny + nx + 1,
        small_limit,
    )(*got_a, *got_b, small)

    def layer_norm_back(first, count, proj):
        return call(
            lambda *refs: back_kernel(geo, first, count, *refs),
            shape((count * win, width), BF16),
            [],
            6,
            small_limit,
            cost=pl.CostEstimate(flops=3 * 10**9, bytes_accessed=10**7, transcendentals=0),
        )(proj, unit, inv, cot_win, gain_row, qkv_weight)

    half_wins = geo.nwin // 2
    mine, grad_proj = lax.optimization_barrier((mine, grad_proj))
    got = chips.z(mine, 1)
    low = layer_norm_back(0, half_wins, grad_proj)
    mine = call(z_sum_kernel, shape(mine.shape, BF16), [], 2, small_limit)(mine, got)
    mine, grad_proj = lax.optimization_barrier((mine, grad_proj))
    got = chips.z(mine, 2)
    high = layer_norm_back(half_wins, geo.nwin - half_wins, grad_proj)
    b_rows, b_cols, b_corner = pad16(geo.n_rows), pad16(geo.n_cols), pad16(geo.n_corner)
    back = call(
        lambda *refs: unpack_send_kernel(geo, *refs),
        [shape((n, width), BF16) for n in (b_rows, b_cols, b_corner)],
        [
            pltpu.VMEM((cells, width), F32),
            pltpu.VMEM((b_rows + b_cols + b_corner, width), F32),
        ],
        2,
        small_limit,
    )(low, high)
    mine = call(z_sum_kernel, shape(mine.shape, BF16), [], 2, small_limit)(mine, got)
    mine, back = lax.optimization_barrier((mine, back))
    got = chips.z(mine, 4)
    back = (moved(back[0], -1, 0), moved(back[1], 0, -1), moved(back[2], -1, -1))
    own_a, own_b = call(
        z_sum_kernel,
        [shape((part, width), BF16), shape((part + 2 * SMALL, width), BF16)],
        [],
        2,
        small_limit,
    )(mine, got)

    got_a = [own_a] + [chips.x(own_a, k) for k in range(1, nx)]
    got_b = [own_b] + [chips.y(own_b, k) for k in range(1, ny)]
    own_a, own_b = call(
        lambda *refs: gather_kernel(ny, nx, *refs),
        [shape((piece, width), BF16), shape((piece + 2 * SMALL, width), BF16)],
        [],
        1 + ny + nx,
        small_limit,
        smem_first=True,
    )(info, *got_a, *got_b)
    own_a, own_b, back, low = lax.optimization_barrier((own_a, own_b, back, low))
    got_a = [own_a] + [chips.y(own_a, k) for k in range(1, ny)]
    got_b = [own_b] + [chips.x(own_b, k) for k in range(1, nx)]
    grad_tokens = call(
        lambda *refs: assemble_kernel(geo, *refs),
        shape((cells, width), BF16),
        [
            pltpu.VMEM((cells, width), F32),
            pltpu.VMEM((b_rows, width), F32),
            pltpu.VMEM((b_cols, width), F32),
            pltpu.VMEM((b_corner, width), F32),
            pltpu.VMEM((cells, width), F32),
        ],
        5,
        small_limit,
    )(low, high, *back)
    mine_a = call(
        lambda *refs: merge_kernel(ny, Y, False, *refs),
        [shape((width, width), BF16)],
        [],
        1 + ny,
        small_limit,
        smem_first=True,
    )(info, *got_a)[0]
    their_a = chips.core(mine_a)
    mine_b, line, grad_gain = call(
        lambda *refs: merge_kernel(nx, X, True, *refs),
        [
            shape((width, width), BF16),
            shape((heads, BANDS * SPAN), F32),
            shape((1, width), F32),
        ],
        [],
        1 + nx,
        small_limit,
        smem_first=True,
    )(info, *got_b)
    their_b = chips.core(mine_b)

    def write(mine, a, b, written):
        return pl.pallas_call(
            lambda *refs: place_kernel(mine, *refs),
            out_shape=[shape((width, 3 * width), F32), shape((width, width), F32)],
            in_specs=[smem, vmem, vmem] + [hbm] * len(written),
            out_specs=[hbm, hbm],
            input_output_aliases={3 + i: i for i in range(len(written))},
            scratch_shapes=[
                pltpu.VMEM((2, width, width), F32),
                pltpu.SemaphoreType.DMA((2, 4)),
            ],
            compiler_params=pltpu.CompilerParams(vmem_limit_bytes=small_limit),
        )(info, a, b, *written)

    written = write(True, mine_a, mine_b, ())
    grad_qkv, grad_out = write(False, their_a, their_b, tuple(written))
    grad_bias = line.T[:entries]
    return (grad_tokens.reshape(tokens.shape), grad_qkv, grad_out, grad_bias, grad_gain.reshape(width))


def solution(mesh):
    in_specs = (P(None, "lat", "lon", None), P(), P(), P(), P(), P(), P(None, "lat", "lon", None))
    out_specs = (P(None, "lat", "lon", None), P(), P(), P(), P())
    return jax.shard_map(
        per_device, mesh=mesh, in_specs=in_specs, out_specs=out_specs, check_vma=False
    )
```

```python
import jax
import jax.numpy as jnp
from jax import lax
from jax.experimental import pallas as pl
from jax.experimental.pallas import tpu as pltpu
from jax.sharding import PartitionSpec as P

WH = 6
WW = 12
SH = 3
SW = 6
F32 = jnp.float32
BF16 = jnp.bfloat16
MIB = 1024 * 1024

LAST, CORE, X, Y = range(4)

NT = (((1,), (1,)), ((), ()))


def dot(a, b):
    return jnp.dot(a, b, preferred_element_type=F32)


def dot_nt(a, b):
    return lax.dot_general(a, b, NT, preferred_element_type=F32)


class Geometry:
    def __init__(self, depth, rows, cols):
        self.depth, self.rows, self.cols = depth, rows, cols
        self.cells = depth * rows * cols
        self.win = depth * WH * WW
        self.nwin = self.cells // self.win
        self.wins_lon = cols // WW
        self.wins_lat = rows // WH
        self.n_rows = depth * SH * (cols - SW)
        self.n_cols = depth * (rows - SH) * SW
        self.n_corner = depth * SH * SW

    def local(self, z, r, c):
        return (z * self.rows + r) * self.cols + c

    def rim_row(self, z, r):
        return (z * SH + r) * (self.cols - SW)

    def rim_col(self, z, r):
        return (z * (self.rows - SH) + r) * SW

    def corner(self, z, r):
        return (z * SH + r) * SW

    def cell(self, z, r, c):
        window = (r // WH) * self.wins_lon + c // WW
        return window * self.win + (z * WH + r % WH) * WW + c % WW


def pad16(n):
    return (n + 15) // 16 * 16


def forward_pieces(geo, z, r):
    own = geo.cols - SW
    if r < geo.rows - SH:
        first = ("local", geo.local(z, r + SH, SW), 0, own)
        second = ("cols", geo.rim_col(z, r), own, SW)
    else:
        first = ("rows", geo.rim_row(z, r - geo.rows + SH), 0, own)
        second = ("corner", geo.corner(z, r - geo.rows + SH), own, SW)
    return (first, second)


def window_cuts(start, length):
    at = start
    while at < start + length:
        stop = min(start + length, (at // WW + 1) * WW)
        yield at, stop - at
        at = stop


def pack_kernel(geo, tok_ref, cot_ref, rows_ref, cols_ref, corner_ref, top, left, wide, slim, buf, sems):
    n_rows, n_cols, n_corner = geo.n_rows, geo.n_cols, geo.n_corner
    base_cols = pad16(2 * n_rows)
    base_corner = base_cols + pad16(2 * n_cols)
    own = geo.cols - SW
    copies = []
    for which, ref in enumerate((tok_ref, cot_ref)):
        for part, (src, dst) in enumerate(
            (
                (ref.at[:, 0:SH], top.at[which]),
                (ref.at[0, SH : geo.rows, 0:16], left.at[which, 0]),
                (ref.at[1, SH : geo.rows, 0:16], left.at[which, 1]),
            )
        ):
            copy = pltpu.make_async_copy(src, dst, sems.at[which, part])
            copy.start()
            copies.append(copy)
    buf[base_cols - 16 : base_cols] = jnp.zeros((16, buf.shape[1]), F32)
    buf[base_corner - 16 : base_corner] = jnp.zeros((16, buf.shape[1]), F32)
    buf[-16:] = jnp.zeros((16, buf.shape[1]), F32)
    for copy in copies:
        copy.wait()
    wide[...] = top[...].astype(F32)
    slim[...] = left[...].astype(F32)
    for which in range(2):
        for z in range(geo.depth):
            for r in range(SH):
                at = which * n_rows + geo.rim_row(z, r)
                buf[at : at + own] = wide[which, z, r, SW:]
                at = base_corner + which * n_corner + geo.corner(z, r)
                buf[at : at + SW] = wide[which, z, r, 0:SW]
            for r in range(geo.rows - SH):
                at = base_cols + which * n_cols + geo.rim_col(z, r)
                buf[at : at + SW] = slim[which, z, r, 0:SW]
    rows_ref[...] = buf[0:base_cols].astype(BF16)
    cols_ref[...] = buf[base_cols:base_corner].astype(BF16)
    corner_ref[...] = buf[base_corner : base_corner + pad16(2 * n_corner)].astype(BF16)


BANDS = 8
SPAN = 96


def band_of(index):
    band = (index * 683) >> 16
    return band, index - band * SPAN


def lookup_kernel(heads, raw_ref, table_ref, bias_ref, idx_ref, split):
    win = idx_ref.shape[0]
    rows = heads * BANDS
    entries = table_ref.shape[1]
    idx_ref[...] = raw_ref[...].T
    split[...] = jnp.zeros_like(split)
    rest = table_ref[...]
    for part in range(3):
        low = rest.astype(BF16).astype(F32)
        for band in range(BANDS):
            at = part * rows + band * heads
            stop = min(entries, (band + 1) * SPAN)
            split[at : at + heads, 0 : stop - band * SPAN] = low[:, band * SPAN : stop]
        rest = rest - low
    table = split[...].astype(BF16)
    iota = lax.broadcasted_iota(jnp.int32, (SPAN, win), 0)

    def step(block, carry):
        start = pl.multiple_of(block * 8, 8)
        band, place = band_of(idx_ref[pl.ds(start, 8), :])
        for j in range(8):
            onehot = jnp.where(iota == place[j : j + 1, :], 1.0, 0.0).astype(BF16)
            found = dot(table, onehot)
            found = (found[:rows] + found[rows : 2 * rows]) + found[2 * rows :]
            mine = jnp.broadcast_to(band[j : j + 1, :], (heads, win))
            total = jnp.zeros((heads, win), F32)
            for b in range(BANDS):
                total = jnp.where(mine == b, found[b * heads : (b + 1) * heads], total)
            for h in range(heads):
                bias_ref[h, pl.ds(start + j, 1), :] = total[h : h + 1]
        return carry

    lax.fori_loop(0, win // 8, step, 0)


def table_sums(heads, first, count, idx_ref, sum_ref, acc):
    win = idx_ref.shape[0]
    rows = heads * BANDS
    iota = lax.broadcasted_iota(jnp.int32, (SPAN, win), 0)
    bands = lax.broadcasted_iota(jnp.int32, (BANDS, win), 0)

    def step(block, carry):
        start = pl.multiple_of(first + block * 8, 8)
        band, place = band_of(idx_ref[pl.ds(start, 8), :])
        tops, rests = [], []
        for h in range(heads):
            slab = sum_ref[h, pl.ds(start, 8), :]
            top = slab.astype(BF16).astype(F32)
            tops.append(top)
            rests.append(slab - top)
        total = None
        for j in range(8):
            onehot = jnp.where(iota == place[j : j + 1, :], 1.0, 0.0).astype(BF16)
            keep = jnp.where(bands == band[j : j + 1, :], 1.0, 0.0)
            spread = [p[h][j : j + 1, :] * keep for p in (tops, rests) for h in range(heads)]
            term = dot_nt(jnp.concatenate(spread, axis=0).astype(BF16), onehot)
            total = term if total is None else total + term
        acc[...] += total[:rows] + total[rows:]
        return carry

    lax.fori_loop(0, count // 8, step, 0)


def first_table_kernel(heads, count, idx_ref, sum_ref, out_ref):
    out_ref[...] = jnp.zeros_like(out_ref)
    table_sums(heads, 0, count, idx_ref, sum_ref, out_ref)


def table_kernel(heads, first, idx_ref, sum_ref, part_ref, gsum_ref, gain_ref, out_ref, acc, line):
    acc[...] = part_ref[...]
    table_sums(heads, first, idx_ref.shape[0] - first, idx_ref, sum_ref, acc)
    for h in range(heads):
        for b in range(BANDS):
            line[h : h + 1, b * SPAN : (b + 1) * SPAN] = acc[h * BANDS + b : h * BANDS + b + 1, :]
    width = out_ref.shape[1]
    more = BANDS * SPAN - width
    gain = jnp.sum(gsum_ref[...].T, axis=0, keepdims=True) / gain_ref[...]
    out_ref[0:heads, :] = line[:, :width]
    out_ref[heads:, 0:more] = line[:, width:]
    out_ref[heads:, more:] = jnp.zeros((16 - heads, width - more), F32)
    out_ref[heads : heads + 1, more:] = gain[:, : width - more]
    out_ref[heads + 1 : heads + 2, more:] = gain[:, width - more :]


def main_kernel(
    geo, heads, info_ref, tok_ref, cot_ref, rows_ref, cols_ref, corner_ref, gain_ref, wqkv_hbm,
    wout_hbm, bias_ref,
    send_ref, keep_ref, bsum_ref, dproj, ftok, inv, cotb, gsum_ref,
    loc, rim_rows, rim_cols, rim_corner, fcot, normed, proj, gatt, att_t, dq_t,
    bias2, normed_t, gout, grads, wqkv_ref, wout_ref, sems,
):
    copies = [
        pltpu.make_async_copy(wqkv_hbm, wqkv_ref, sems.at[0]),
        pltpu.make_async_copy(wout_hbm, wout_ref, sems.at[1]),
    ]
    for copy in copies:
        copy.start()
    width = ftok.shape[1]
    win = geo.win
    head_size = width // heads
    scale = head_size ** (-0.5)

    for which, (ref, dst) in enumerate(((tok_ref, ftok), (cot_ref, fcot))):
        loc[...] = ref[...].astype(F32)
        if which == 0:
            rim_rows[...] = rows_ref[...].astype(F32)
            rim_cols[...] = cols_ref[...].astype(F32)
            rim_corner[...] = corner_ref[...].astype(F32)
        sources = {
            "local": (loc, 0),
            "rows": (rim_rows, which * geo.n_rows),
            "cols": (rim_cols, which * geo.n_cols),
            "corner": (rim_corner, which * geo.n_corner),
        }
        for z in range(geo.depth):
            for r in range(geo.rows):
                for name, first, column, length in forward_pieces(geo, z, r):
                    src, base = sources[name]
                    for at, count in window_cuts(column, length):
                        begin = base + first + at - column
                        cell = geo.cell(z, r, at)
                        dst[cell : cell + count] = src[begin : begin + count]

    gain = gain_ref[...]

    spot = lax.broadcasted_iota(jnp.int32, (win, win), 0)
    other = lax.broadcasted_iota(jnp.int32, (win, win), 1)
    half = WH * WW
    polar_a = jnp.where(spot >= half, spot - half, spot) >= (WH - SH) * WW
    polar_b = jnp.where(other >= half, other - half, other) >= (WH - SH) * WW
    flag_a = jnp.where(polar_a, 1.0, 0.0)
    flag_b = jnp.where(polar_b, 1.0, 0.0)
    mask = jnp.where(flag_a == flag_b, 0.0, -1e30)
    for h in range(heads):
        plain = bias_ref[h]
        bias2[0, h] = plain
        bias2[1, h] = plain + mask
        bsum_ref[h] = jnp.zeros((win, win), F32)
    gout[...] = jnp.zeros_like(gout)

    def norm_step(w, carry):
        at = pl.ds(pl.multiple_of(w * win, 16), win)
        x = ftok[at, :]
        centred = x - jnp.mean(x, axis=-1, keepdims=True)
        istd = lax.rsqrt(jnp.mean(centred * centred, axis=-1, keepdims=True) + 1e-05)
        unit = centred * istd
        ftok[at, :] = unit
        inv[at, :] = jnp.broadcast_to(istd, (win, 128))
        normed[at, :] = (unit * gain).astype(BF16)
        cotb[at, :] = fcot[at, :].astype(BF16)
        return carry

    lax.fori_loop(0, geo.nwin, norm_step, 0)
    for copy in copies:
        copy.wait()

    def proj_step(w, carry):
        at = pl.ds(pl.multiple_of(w * (2 * win), 16), 2 * win)
        x = normed[at, :]
        for part in range(3):
            cols = slice(part * width, (part + 1) * width)
            proj[at, cols] = dot(x, wqkv_ref[:, cols]).astype(BF16)
        gatt[at, :] = dot_nt(cotb[at, :], wout_ref[...]).astype(BF16)
        return carry

    lax.fori_loop(0, geo.nwin // 2, proj_step, 0)

    lane = lax.broadcasted_iota(jnp.int32, (win, 128), 1)
    lower = lane < head_size
    polar_from = geo.nwin - geo.wins_lon

    def attend(w, carry):
        at = pl.ds(pl.multiple_of(w * win, 16), win)
        sel = jnp.where(w >= polar_from, info_ref[LAST], 0)
        k_t = proj[at, width : 2 * width].T
        v_t = proj[at, 2 * width :].T
        for pair in range(heads // 2):
            cols = slice(pair * 128, (pair + 1) * 128)
            q = proj[at, cols] * BF16(scale)
            k = proj[at, width + pair * 128 : width + (pair + 1) * 128]
            v = proj[at, 2 * width + pair * 128 : 2 * width + (pair + 1) * 128]
            g = gatt[at, cols]
            dv = None
            dk = None
            for side in range(2):
                h = 2 * pair + side
                keep = lower if side == 0 else jnp.logical_not(lower)
                qm = jnp.where(keep, q, BF16(0))
                gm = jnp.where(keep, g, BF16(0))
                scores = dot_nt(k, qm) + bias2[sel, h]
                top = jnp.max(scores, axis=0, keepdims=True)
                grown = jnp.exp(scores - top)
                probs = grown * (1.0 / jnp.sum(grown, axis=0, keepdims=True))
                probs_low = probs.astype(BF16)
                gprobs = dot_nt(v, gm)
                weighted = jnp.sum(probs * gprobs, axis=0, keepdims=True)
                gscores = probs * (gprobs - weighted)
                bsum_ref[h] += gscores
                scores_low = gscores.astype(BF16)
                feats = slice(h * head_size, (h + 1) * head_size)
                att_t[feats, :] = dot(v_t[feats], probs_low).astype(BF16)
                dq_t[feats, :] = (dot(k_t[feats], scores_low) * scale).astype(BF16)
                dv_term = dot(probs_low, gm)
                dk_term = dot(scores_low, qm)
                dv = dv_term if dv is None else dv + dv_term
                dk = dk_term if dk is None else dk + dk_term
            dproj[at, width + pair * 128 : width + (pair + 1) * 128] = dk.astype(BF16)
            dproj[at, 2 * width + pair * 128 : 2 * width + (pair + 1) * 128] = dv.astype(BF16)
        dproj[at, 0:width] = dq_t[...].T
        gout[...] += dot(att_t[...], cotb[at, :])
        return carry

    lax.fori_loop(0, geo.nwin, attend, 0)

    grads[1, width:, :] = gout[...].astype(BF16)
    for block in range(geo.cells // 128):
        rows = slice(block * 128, (block + 1) * 128)
        normed_t[:, rows] = normed[rows, :].T

    gsum = jnp.zeros((width, 128), F32)
    for part in range(3):
        half, first = part // 2, part % 2 * width
        for sub in range(2):
            cols = slice(part * width + sub * 256, part * width + (sub + 1) * 256)
            term = dot(normed_t[...], dproj[:, cols])
            grads[half, first : first + width, sub * 256 : (sub + 1) * 256] = term.astype(BF16)
            term = term * wqkv_ref[:, cols].astype(F32)
            gsum = gsum + (term[:, :128] + term[:, 128:])
    gsum_ref[...] = gsum
    keep_ref[...] = grads[info_ref[CORE]]
    send_ref[...] = grads[1 - info_ref[CORE]]


def back_kernel(geo, first, count, dproj, unit_ref, inv, cotb, gain_ref, wqkv_ref, gtok_ref):
    win = geo.win
    gain = gain_ref[...]

    def back_step(w, carry):
        at = pl.ds(pl.multiple_of((first + w) * win, 16), win)
        gn = dot_nt(dproj[at, :], wqkv_ref[...]).astype(BF16).astype(F32)
        unit = unit_ref[at, :]
        hat = gn * gain
        centre = jnp.mean(hat, axis=-1, keepdims=True)
        slope = jnp.mean(hat * unit, axis=-1, keepdims=True)
        istd = inv[at, 0:1]
        cot = cotb[at, :].astype(F32)
        to = pl.ds(pl.multiple_of(w * win, 16), win)
        gtok_ref[to, :] = (cot + istd * (hat - centre - unit * slope)).astype(BF16)
        return carry

    lax.fori_loop(0, count, back_step, 0)


def unpack_send_kernel(geo, low_ref, high_ref, rows_ref, cols_ref, corner_ref, fg, buf):
    base_cols = pad16(geo.n_rows)
    base_corner = base_cols + pad16(geo.n_cols)
    half = low_ref.shape[0]
    fg[0:half] = low_ref[...].astype(F32)
    fg[half:] = high_ref[...].astype(F32)
    buf[...] = jnp.zeros_like(buf)
    bases = {"rows": 0, "cols": base_cols, "corner": base_corner}
    for z in range(geo.depth):
        for r in range(geo.rows):
            for name, first, column, length in forward_pieces(geo, z, r):
                if name == "local":
                    continue
                for at, count in window_cuts(column, length):
                    to = bases[name] + first + at - column
                    cell = geo.cell(z, r, at)
                    buf[to : to + count] = fg[cell : cell + count]
    rows_ref[...] = buf[0:base_cols].astype(BF16)
    cols_ref[...] = buf[base_cols:base_corner].astype(BF16)
    corner_ref[...] = buf[base_corner : base_corner + pad16(geo.n_corner)].astype(BF16)


def assemble_kernel(geo, low_ref, high_ref, rows_ref, cols_ref, corner_ref, out_ref, fg, rr, rc, rk, grid):
    half = low_ref.shape[0]
    fg[0:half] = low_ref[...].astype(F32)
    fg[half:] = high_ref[...].astype(F32)
    rr[...] = rows_ref[...].astype(F32)
    rc[...] = cols_ref[...].astype(F32)
    rk[...] = corner_ref[...].astype(F32)
    own = geo.cols - SW
    for z in range(geo.depth):
        for r in range(geo.rows):
            for name, first, column, length in forward_pieces(geo, z, r):
                if name != "local":
                    continue
                for at, count in window_cuts(column, length):
                    to = first + at - column
                    cell = geo.cell(z, r, at)
                    grid[to : to + count] = fg[cell : cell + count]
        for r in range(SH):
            to = geo.local(z, r, SW)
            grid[to : to + own] = rr[geo.rim_row(z, r) : geo.rim_row(z, r) + own]
            to = geo.local(z, r, 0)
            grid[to : to + SW] = rk[geo.corner(z, r) : geo.corner(z, r) + SW]
        for r in range(geo.rows - SH):
            to = geo.local(z, r + SH, 0)
            grid[to : to + SW] = rc[geo.rim_col(z, r) : geo.rim_col(z, r) + SW]
    out_ref[...] = grid[...].astype(BF16)


def call(kernel, out_shapes, scratch, n_in, limit, smem_first=False, cost=None):
    specs = [pl.BlockSpec(memory_space=pltpu.VMEM)] * n_in
    if smem_first:
        specs[0] = pl.BlockSpec(memory_space=pltpu.SMEM)
    return pl.pallas_call(
        kernel,
        out_shape=out_shapes,
        in_specs=specs,
        out_specs=jax.tree.map(lambda s: pl.BlockSpec(memory_space=pltpu.VMEM), out_shapes),
        scratch_shapes=scratch,
        compiler_params=pltpu.CompilerParams(vmem_limit_bytes=limit),
        cost_estimate=cost,
    )


def shape(dims, dtype):
    return jax.ShapeDtypeStruct(dims, dtype)


def moved(value, lat_step, lon_step):
    lats, lons = lax.axis_size("lat"), lax.axis_size("lon")
    pairs = []
    for a in range(lats):
        for o in range(lons):
            target = ((a - lat_step) % lats) * lons + (o - lon_step) % lons
            pairs.append((a * lons + o, target))
    return lax.ppermute(value, ("lat", "lon"), pairs)


class Chips:
    def __init__(self):
        self.lats, self.lons = lax.axis_size("lat"), lax.axis_size("lon")
        self.nz, self.nx, self.ny = self.lats // 2, 4, self.lons // 4

    def split(self, device):
        lat, lon = device // self.lons, device % self.lons
        x = lon // (2 * self.ny) * 2 + lat % 2
        return lat // 2, x, lon // 2 % self.ny, lon % 2

    def join(self, z, x, y, core):
        return (z * 2 + x % 2) * self.lons + (x // 2 * self.ny + y) * 2 + core

    def send(self, value, change):
        pairs = []
        for device in range(self.lats * self.lons):
            z, x, y, core = change(*self.split(device))
            pairs.append((device, self.join(z, x, y, core)))
        return lax.ppermute(value, ("lat", "lon"), pairs)

    def core(self, value):
        return self.send(value, lambda z, x, y, c: (z, x, y, 1 - c))

    def x(self, value, step):
        return self.send(value, lambda z, x, y, c: (z, (x + step) % self.nx, y, c))

    def y(self, value, step):
        return self.send(value, lambda z, x, y, c: (z, x, (y + step) % self.ny, c))

    def z(self, value, bit):
        return self.send(value, lambda z, x, y, c: (z ^ (2 * bit - 1), x, y, c))


def pair_sum_kernel(ny, nx, info_ref, keep_ref, recv_ref, *outs):
    rows = keep_ref.shape[0] // 2
    for base, count, place, refs in ((0, ny, Y, outs[:ny]), (rows, nx, X, outs[ny:])):
        piece = rows // count
        for k, ref in enumerate(refs):
            part = (info_ref[place] + k) & (count - 1)
            at = pl.ds(pl.multiple_of(base + part * piece, 16), piece)
            ref[...] = (keep_ref[at, :].astype(F32) + recv_ref[at, :].astype(F32)).astype(BF16)


def total_of(refs):
    total = refs[0][...].astype(F32)
    for ref in refs[1:]:
        total += ref[...].astype(F32)
    return total


def cross_sum_kernel(ny, nx, info_ref, *refs):
    ins_a, ins_b = refs[:ny], refs[ny : ny + nx]
    outs_a, outs_b = refs[ny + nx : ny + 2 * nx], refs[ny + 2 * nx : 2 * ny + 2 * nx]
    hold = refs[-1]
    for ins, outs, count, place in ((ins_a, outs_a, nx, X), (ins_b, outs_b, ny, Y)):
        hold[...] = total_of(ins)
        piece = hold.shape[0] // count
        for k, ref in enumerate(outs):
            part = (info_ref[place] + k) & (count - 1)
            at = pl.ds(pl.multiple_of(part * piece, 16), piece)
            ref[...] = hold[at, :].astype(BF16)


SMALL = 16


def put_small(ref, base, total):
    top = total.astype(BF16)
    ref[base : base + SMALL] = top
    ref[base + SMALL : base + 2 * SMALL] = (total - top.astype(F32)).astype(BF16)


def small_of(refs, base):
    total = None
    for ref in refs:
        for part in range(2):
            at = base + part * SMALL
            term = ref[at : at + SMALL].astype(F32)
            total = term if total is None else total + term
    return total


def join_sum_kernel(ny, nx, *refs):
    piece = refs[0].shape[0]
    small_ref, out_ref = refs[-2:]
    out_ref[0:piece] = total_of(refs[:nx]).astype(BF16)
    out_ref[piece : 2 * piece] = total_of(refs[nx : nx + ny]).astype(BF16)
    put_small(out_ref, 2 * piece, small_ref[...])


def z_sum_kernel(mine_ref, got_ref, *outs):
    rows = mine_ref.shape[0] - 2 * SMALL
    total = (mine_ref[0:rows].astype(F32) + got_ref[0:rows].astype(F32)).astype(BF16)
    last = small_of((mine_ref, got_ref), rows)
    if len(outs) == 1:
        outs[0][0:rows] = total
    else:
        outs[0][...] = total[: rows // 2]
        outs[1][0 : rows // 2] = total[rows // 2 :]
    put_small(outs[-1], outs[-1].shape[0] - 2 * SMALL, last)


def gather_kernel(ny, nx, info_ref, *refs):
    a_ref, b_ref = refs[-2:]
    ins_a, ins_b = refs[:nx], refs[nx : nx + ny]
    piece = ins_a[0].shape[0]
    for ins, out, count, place in ((ins_a, a_ref, nx, X), (ins_b, b_ref, ny, Y)):
        for k, ref in enumerate(ins):
            part = (info_ref[place] + (count - k)) & (count - 1)
            out[pl.ds(pl.multiple_of(part * piece, 16), piece), :] = ref[0:piece]
    put_small(b_ref, ny * piece, small_of(ins_b, piece))


def merge_kernel(count, place, with_small, info_ref, *refs):
    ins, out_ref = refs[:count], refs[count]
    width = out_ref.shape[1]
    piece = width // count
    for k, ref in enumerate(ins):
        part = (info_ref[place] + (count - k)) & (count - 1)
        out_ref[pl.ds(pl.multiple_of(part * piece, 16), piece), :] = ref[0:piece]
    if with_small:
        put_small(out_ref, width, small_of(ins, piece))


def place_kernel(which, mine, info_ref, value_ref, *refs):
    gqkv_ref, gout_ref, hold, sems = refs[-4:]
    width = gout_ref.shape[1]
    core = info_ref[CORE]
    half = core if mine else 1 - core
    steps = 4
    rows = width // steps

    def write(target):
        copies = []
        for step in range(steps):
            at = slice(step * rows, (step + 1) * rows)
            hold[at] = value_ref[at].astype(F32)
            copy = pltpu.make_async_copy(hold.at[at], target.at[at], sems.at[step])
            copy.start()
            copies.append(copy)
        for copy in copies:
            copy.wait()

    @pl.when(half == 0)
    def _():
        write(gqkv_ref.at[:, which * width : (which + 1) * width])

    @pl.when(half == 1)
    def _():
        write(gqkv_ref.at[:, 2 * width :] if which == 0 else gout_ref)


def last_small_kernel(mine_ref, got_ref, line_ref, gain_ref):
    width = mine_ref.shape[1]
    total = small_of((mine_ref, got_ref), width)
    more = line_ref.shape[1] - width
    line_ref[:, 0:width] = total[0:8]
    line_ref[:, width:] = total[8:, 0:more]
    gain_ref[:, 0 : width - more] = total[8:9, more:]
    gain_ref[:, width - more :] = total[9:10, more:]


def per_device(tokens, norm_gain, qkv_weight, out_weight, bias_table, bias_index, cotangent):
    depth, rows_lat, cols_lon, width = tokens.shape
    entries, heads = bias_table.shape
    geo = Geometry(depth, rows_lat, cols_lon)
    win, cells = geo.win, geo.cells
    tok = tokens.reshape(cells, width)
    cot = cotangent.reshape(cells, width)

    n_rows, n_cols, n_corner = pad16(2 * geo.n_rows), pad16(2 * geo.n_cols), pad16(2 * geo.n_corner)
    rim = pl.pallas_call(
        lambda *refs: pack_kernel(geo, *refs),
        out_shape=[shape((n, width), BF16) for n in (n_rows, n_cols, n_corner)],
        in_specs=[pl.BlockSpec(memory_space=pltpu.HBM)] * 2,
        out_specs=[pl.BlockSpec(memory_space=pltpu.VMEM)] * 3,
        scratch_shapes=[
            pltpu.VMEM((2, depth, SH, cols_lon, width), BF16),
            pltpu.VMEM((2, depth, rows_lat - SH, 16, width), BF16),
            pltpu.VMEM((2, depth, SH, cols_lon, width), F32),
            pltpu.VMEM((2, depth, rows_lat - SH, 16, width), F32),
            pltpu.VMEM((n_rows + n_cols + n_corner, width), F32),
            pltpu.SemaphoreType.DMA((2, 3)),
        ],
        compiler_params=pltpu.CompilerParams(vmem_limit_bytes=60 * MIB),
    )(tokens, cotangent)
    rim = (moved(rim[0], 1, 0), moved(rim[1], 0, 1), moved(rim[2], 1, 1))

    bias, index_t = call(
        lambda *refs: lookup_kernel(heads, *refs),
        [shape((heads, win, win), F32), shape((win, win), jnp.int32)],
        [pltpu.VMEM((3 * heads * BANDS, SPAN), F32)],
        2,
        8 * MIB,
        cost=pl.CostEstimate(flops=4 * 10**9, bytes_accessed=10**6, transcendentals=0),
    )(bias_index, bias_table.T)

    chips = Chips()
    ny, nx = chips.ny, chips.nx
    lat, lon = lax.axis_index("lat"), lax.axis_index("lon")
    is_last = (lat == chips.lats - 1).astype(jnp.int32)
    info = jnp.stack([is_last, lon % 2, lon // (2 * ny) * 2 + lat % 2, lon // 2 % ny])
    half_rows = 2 * width
    big = 36 * MIB
    small_limit = 10 * MIB

    vmem, smem = pl.BlockSpec(memory_space=pltpu.VMEM), pl.BlockSpec(memory_space=pltpu.SMEM)
    hbm = pl.BlockSpec(memory_space=pltpu.HBM)
    send, keep, bias_sum, grad_proj, unit, inv, cot_win, gain_sum = pl.pallas_call(
        lambda *refs: main_kernel(geo, heads, *refs),
        in_specs=[smem] + [vmem] * 6 + [hbm, hbm, vmem],
        out_specs=[vmem] * 8,
        compiler_params=pltpu.CompilerParams(vmem_limit_bytes=big),
        out_shape=[
            shape((half_rows, width), BF16),
            shape((half_rows, width), BF16),
            shape((heads, win, win), F32),
            shape((cells, 3 * width), BF16),
            shape((cells, width), F32),
            shape((cells, 128), F32),
            shape((cells, width), BF16),
            shape((width, 128), F32),
        ],
        scratch_shapes=[
            pltpu.VMEM((cells, width), F32),
            pltpu.VMEM((n_rows, width), F32),
            pltpu.VMEM((n_cols, width), F32),
            pltpu.VMEM((n_corner, width), F32),
            pltpu.VMEM((cells, width), F32),
            pltpu.VMEM((cells, width), BF16),
            pltpu.VMEM((cells, 3 * width), BF16),
            pltpu.VMEM((cells, width), BF16),
            pltpu.VMEM((width, win), BF16),
            pltpu.VMEM((width, win), BF16),
            pltpu.VMEM((2, heads, win, win), F32),
            pltpu.VMEM((width, cells), BF16),
            pltpu.VMEM((width, width), F32),
            pltpu.VMEM((2, half_rows, width), BF16),
            pltpu.VMEM((width, 3 * width), BF16),
            pltpu.VMEM((width, width), BF16),
            pltpu.SemaphoreType.DMA((2,)),
        ],
    )(info, tok, cot, *rim, norm_gain.reshape(1, width), qkv_weight, out_weight, bias)

    got = chips.core(send)
    first = win // 16 * 8
    folded = call(
        lambda *refs: first_table_kernel(heads, first, *refs),
        shape((heads * BANDS, SPAN), F32),
        [],
        2,
        small_limit,
        cost=pl.CostEstimate(flops=2 * 10**9, bytes_accessed=10**6, transcendentals=0),
    )(index_t, bias_sum)
    piece = half_rows // 2 // ny
    outs = call(
        lambda *refs: pair_sum_kernel(ny, nx, *refs),
        [shape((piece, width), BF16)] * (ny + nx),
        [],
        3,
        small_limit,
        smem_first=True,
    )(info, *lax.optimization_barrier((keep, got, folded))[:2])

    got_a = [outs[0]] + [chips.y(outs[k], k) for k in range(1, ny)]
    got_b = [outs[ny]] + [chips.x(outs[ny + k], k) for k in range(1, nx)]
    gain_row = norm_gain.reshape(1, width)
    outs = call(
        lambda *refs: cross_sum_kernel(ny, nx, *refs),
        [shape((piece // nx, width), BF16)] * nx + [shape((piece // ny, width), BF16)] * ny,
        [pltpu.VMEM((piece, width), F32)],
        1 + ny + nx,
        small_limit,
        smem_first=True,
    )(info, *got_a, *got_b)

    outs, bias_sum = lax.optimization_barrier((outs, bias_sum))
    got_a = [outs[0]] + [chips.x(outs[k], k) for k in range(1, nx)]
    got_b = [outs[nx]] + [chips.y(outs[nx + k], k) for k in range(1, ny)]
    small = call(
        lambda *refs: table_kernel(heads, first, *refs),
        shape((SMALL, width), F32),
        [pltpu.VMEM((heads * BANDS, SPAN), F32), pltpu.VMEM((heads, BANDS * SPAN), F32)],
        5,
        small_limit,
        cost=pl.CostEstimate(flops=2 * 10**9, bytes_accessed=10**6, transcendentals=0),
    )(index_t, bias_sum, folded, gain_sum, gain_row)
    part = piece // nx
    mine = call(
        lambda *refs: join_sum_kernel(ny, nx, *refs),
        shape((2 * part + 2 * SMALL, width), BF16),
        [],
        ny + nx + 1,
        small_limit,
    )(*got_a, *got_b, small)

    def layer_norm_back(first, count, proj):
        return call(
            lambda *refs: back_kernel(geo, first, count, *refs),
            shape((count * win, width), BF16),
            [],
            6,
            small_limit,
            cost=pl.CostEstimate(flops=3 * 10**9, bytes_accessed=10**7, transcendentals=0),
        )(proj, unit, inv, cot_win, gain_row, qkv_weight)

    half_wins = geo.nwin // 2
    mine, grad_proj, qkv_weight = lax.optimization_barrier((mine, grad_proj, qkv_weight))
    got = chips.z(mine, 1)
    low = layer_norm_back(0, half_wins, grad_proj)
    mine = call(z_sum_kernel, shape(mine.shape, BF16), [], 2, small_limit)(mine, got)
    mine, grad_proj = lax.optimization_barrier((mine, grad_proj))
    got = chips.z(mine, 2)
    high = layer_norm_back(half_wins, geo.nwin - half_wins, grad_proj)
    mine = call(z_sum_kernel, shape(mine.shape, BF16), [], 2, small_limit)(mine, got)
    mine, low, high = lax.optimization_barrier((mine, low, high))
    got = chips.z(mine, 4)
    b_rows, b_cols, b_corner = pad16(geo.n_rows), pad16(geo.n_cols), pad16(geo.n_corner)
    back = call(
        lambda *refs: unpack_send_kernel(geo, *refs),
        [shape((n, width), BF16) for n in (b_rows, b_cols, b_corner)],
        [
            pltpu.VMEM((cells, width), F32),
            pltpu.VMEM((b_rows + b_cols + b_corner, width), F32),
        ],
        2,
        small_limit,
    )(low, high)
    back = (moved(back[0], -1, 0), moved(back[1], 0, -1), moved(back[2], -1, -1))
    got, back = lax.optimization_barrier((got, back))
    own_a, own_b = call(
        z_sum_kernel,
        [shape((part, width), BF16), shape((part + 2 * SMALL, width), BF16)],
        [],
        2,
        small_limit,
    )(mine, got)

    got_a = [own_a] + [chips.x(own_a, k) for k in range(1, nx)]
    got_b = [own_b] + [chips.y(own_b, k) for k in range(1, ny)]
    own_a, own_b = call(
        lambda *refs: gather_kernel(ny, nx, *refs),
        [shape((piece, width), BF16), shape((piece + 2 * SMALL, width), BF16)],
        [],
        1 + ny + nx,
        small_limit,
        smem_first=True,
    )(info, *got_a, *got_b)
    own_a, own_b, back, low = lax.optimization_barrier((own_a, own_b, back, low))
    got_a = [own_a] + [chips.y(own_a, k) for k in range(1, ny)]
    got_b = [own_b] + [chips.x(own_b, k) for k in range(1, nx)]
    grad_tokens = call(
        lambda *refs: assemble_kernel(geo, *refs),
        shape((cells, width), BF16),
        [
            pltpu.VMEM((cells, width), F32),
            pltpu.VMEM((b_rows, width), F32),
            pltpu.VMEM((b_cols, width), F32),
            pltpu.VMEM((b_corner, width), F32),
            pltpu.VMEM((cells, width), F32),
        ],
        5,
        small_limit,
    )(low, high, *back)
    own_a, grad_tokens = lax.optimization_barrier((own_a, grad_tokens))
    got_a[0] = own_a
    mine_a = call(
        lambda *refs: merge_kernel(ny, Y, False, *refs),
        shape((width, width), BF16),
        [],
        1 + ny,
        small_limit,
        smem_first=True,
    )(info, *got_a)
    their_a = chips.core(mine_a)

    def write(which, mine, value, written):
        return pl.pallas_call(
            lambda *refs: place_kernel(which, mine, *refs),
            out_shape=[shape((width, 3 * width), F32), shape((width, width), F32)],
            in_specs=[smem, vmem] + [hbm] * len(written),
            out_specs=[hbm, hbm],
            input_output_aliases={2 + i: i for i in range(len(written))},
            scratch_shapes=[pltpu.VMEM((width, width), F32), pltpu.SemaphoreType.DMA((4,))],
            compiler_params=pltpu.CompilerParams(vmem_limit_bytes=small_limit),
        )(info, value, *written)

    written = write(0, True, mine_a, ())
    mine_b = call(
        lambda *refs: merge_kernel(nx, X, True, *refs),
        shape((width + 2 * SMALL, width), BF16),
        [],
        1 + nx,
        small_limit,
        smem_first=True,
    )(info, *got_b)
    their_b = chips.core(mine_b)
    written = write(1, True, mine_b, tuple(written))
    written = write(0, False, their_a, tuple(written))
    line, grad_gain = call(
        last_small_kernel,
        [shape((heads, BANDS * SPAN), F32), shape((1, width), F32)],
        [],
        2,
        small_limit,
    )(mine_b, their_b)
    grad_qkv, grad_out = write(1, False, their_b, tuple(written))
    grad_bias = line.T[:entries]
    return (grad_tokens.reshape(tokens.shape), grad_qkv, grad_out, grad_bias, grad_gain.reshape(width))


def solution(mesh):
    in_specs = (P(None, "lat", "lon", None), P(), P(), P(), P(), P(), P(None, "lat", "lon", None))
    out_specs = (P(None, "lat", "lon", None), P(), P(), P(), P())
    return jax.shard_map(
        per_device, mesh=mesh, in_specs=in_specs, out_specs=out_specs, check_vma=False
    )
```

```python
import jax
import jax.numpy as jnp
from jax import lax
from jax.experimental import pallas as pl
from jax.experimental.pallas import tpu as pltpu
from jax.sharding import PartitionSpec as P

WH = 6
WW = 12
SH = 3
SW = 6
F32 = jnp.float32
BF16 = jnp.bfloat16
MIB = 1024 * 1024

LAST, CORE, X, Y = range(4)

NT = (((1,), (1,)), ((), ()))


def dot(a, b):
    return jnp.dot(a, b, preferred_element_type=F32)


def dot_nt(a, b):
    return lax.dot_general(a, b, NT, preferred_element_type=F32)


class Geometry:
    def __init__(self, depth, rows, cols):
        self.depth, self.rows, self.cols = depth, rows, cols
        self.cells = depth * rows * cols
        self.win = depth * WH * WW
        self.nwin = self.cells // self.win
        self.wins_lon = cols // WW
        self.wins_lat = rows // WH
        self.n_rows = depth * SH * (cols - SW)
        self.n_cols = depth * (rows - SH) * SW
        self.n_corner = depth * SH * SW

    def local(self, z, r, c):
        return (z * self.rows + r) * self.cols + c

    def rim_row(self, z, r):
        return (z * SH + r) * (self.cols - SW)

    def rim_col(self, z, r):
        return (z * (self.rows - SH) + r) * SW

    def corner(self, z, r):
        return (z * SH + r) * SW

    def cell(self, z, r, c):
        window = (r // WH) * self.wins_lon + c // WW
        return window * self.win + (z * WH + r % WH) * WW + c % WW


def pad16(n):
    return (n + 15) // 16 * 16


def forward_pieces(geo, z, r):
    own = geo.cols - SW
    if r < geo.rows - SH:
        first = ("local", geo.local(z, r + SH, SW), 0, own)
        second = ("cols", geo.rim_col(z, r), own, SW)
    else:
        first = ("rows", geo.rim_row(z, r - geo.rows + SH), 0, own)
        second = ("corner", geo.corner(z, r - geo.rows + SH), own, SW)
    return (first, second)


def window_cuts(start, length):
    at = start
    while at < start + length:
        stop = min(start + length, (at // WW + 1) * WW)
        yield at, stop - at
        at = stop


def pack_kernel(geo, tok_ref, cot_ref, rows_ref, cols_ref, corner_ref, top, left, wide, slim, buf, sems):
    n_rows, n_cols, n_corner = geo.n_rows, geo.n_cols, geo.n_corner
    base_cols = pad16(2 * n_rows)
    base_corner = base_cols + pad16(2 * n_cols)
    own = geo.cols - SW
    copies = []
    for which, ref in enumerate((tok_ref, cot_ref)):
        for part, (src, dst) in enumerate(
            (
                (ref.at[:, 0:SH], top.at[which]),
                (ref.at[0, SH : geo.rows, 0:16], left.at[which, 0]),
                (ref.at[1, SH : geo.rows, 0:16], left.at[which, 1]),
            )
        ):
            copy = pltpu.make_async_copy(src, dst, sems.at[which, part])
            copy.start()
            copies.append(copy)
    buf[base_cols - 16 : base_cols] = jnp.zeros((16, buf.shape[1]), F32)
    buf[base_corner - 16 : base_corner] = jnp.zeros((16, buf.shape[1]), F32)
    buf[-16:] = jnp.zeros((16, buf.shape[1]), F32)
    for copy in copies:
        copy.wait()
    wide[...] = top[...].astype(F32)
    slim[...] = left[...].astype(F32)
    for which in range(2):
        for z in range(geo.depth):
            for r in range(SH):
                at = which * n_rows + geo.rim_row(z, r)
                buf[at : at + own] = wide[which, z, r, SW:]
                at = base_corner + which * n_corner + geo.corner(z, r)
                buf[at : at + SW] = wide[which, z, r, 0:SW]
            for r in range(geo.rows - SH):
                at = base_cols + which * n_cols + geo.rim_col(z, r)
                buf[at : at + SW] = slim[which, z, r, 0:SW]
    rows_ref[...] = buf[0:base_cols].astype(BF16)
    cols_ref[...] = buf[base_cols:base_corner].astype(BF16)
    corner_ref[...] = buf[base_corner : base_corner + pad16(2 * n_corner)].astype(BF16)


BANDS = 8
SPAN = 96


def band_of(index):
    band = (index * 683) >> 16
    return band, index - band * SPAN


def lookup_kernel(heads, raw_ref, table_ref, bias_ref, idx_ref, split):
    win = idx_ref.shape[0]
    rows = heads * BANDS
    entries = table_ref.shape[1]
    idx_ref[...] = raw_ref[...].T
    split[...] = jnp.zeros_like(split)
    rest = table_ref[...]
    for part in range(3):
        low = rest.astype(BF16).astype(F32)
        for band in range(BANDS):
            at = part * rows + band * heads
            stop = min(entries, (band + 1) * SPAN)
            split[at : at + heads, 0 : stop - band * SPAN] = low[:, band * SPAN : stop]
        rest = rest - low
    table = split[...].astype(BF16)
    iota = lax.broadcasted_iota(jnp.int32, (SPAN, win), 0)

    def step(block, carry):
        start = pl.multiple_of(block * 8, 8)
        band, place = band_of(idx_ref[pl.ds(start, 8), :])
        for j in range(8):
            onehot = jnp.where(iota == place[j : j + 1, :], 1.0, 0.0).astype(BF16)
            found = dot(table, onehot)
            found = (found[:rows] + found[rows : 2 * rows]) + found[2 * rows :]
            mine = jnp.broadcast_to(band[j : j + 1, :], (heads, win))
            total = jnp.zeros((heads, win), F32)
            for b in range(BANDS):
                total = jnp.where(mine == b, found[b * heads : (b + 1) * heads], total)
            for h in range(heads):
                bias_ref[h, pl.ds(start + j, 1), :] = total[h : h + 1]
        return carry

    lax.fori_loop(0, win // 8, step, 0)


def table_sums(heads, first, count, idx_ref, sum_ref, acc):
    win = idx_ref.shape[0]
    rows = heads * BANDS
    iota = lax.broadcasted_iota(jnp.int32, (SPAN, win), 0)
    bands = lax.broadcasted_iota(jnp.int32, (BANDS, win), 0)

    def step(block, carry):
        start = pl.multiple_of(first + block * 8, 8)
        band, place = band_of(idx_ref[pl.ds(start, 8), :])
        tops, rests = [], []
        for h in range(heads):
            slab = sum_ref[h, pl.ds(start, 8), :]
            top = slab.astype(BF16).astype(F32)
            tops.append(top)
            rests.append(slab - top)
        total = None
        for j in range(8):
            onehot = jnp.where(iota == place[j : j + 1, :], 1.0, 0.0).astype(BF16)
            keep = jnp.where(bands == band[j : j + 1, :], 1.0, 0.0)
            spread = [p[h][j : j + 1, :] * keep for p in (tops, rests) for h in range(heads)]
            term = dot_nt(jnp.concatenate(spread, axis=0).astype(BF16), onehot)
            total = term if total is None else total + term
        acc[...] += total[:rows] + total[rows:]
        return carry

    lax.fori_loop(0, count // 8, step, 0)


def table_kernel(heads, idx_ref, sum_ref, gsum_ref, gain_ref, out_ref, acc, line):
    acc[...] = jnp.zeros_like(acc)
    table_sums(heads, 0, idx_ref.shape[0], idx_ref, sum_ref, acc)
    for h in range(heads):
        for b in range(BANDS):
            line[h : h + 1, b * SPAN : (b + 1) * SPAN] = acc[h * BANDS + b : h * BANDS + b + 1, :]
    width = out_ref.shape[1]
    more = BANDS * SPAN - width
    gain = jnp.sum(gsum_ref[...].T, axis=0, keepdims=True) / gain_ref[...]
    out_ref[0:heads, :] = line[:, :width]
    out_ref[heads:, 0:more] = line[:, width:]
    out_ref[heads:, more:] = jnp.zeros((16 - heads, width - more), F32)
    out_ref[heads : heads + 1, more:] = gain[:, : width - more]
    out_ref[heads + 1 : heads + 2, more:] = gain[:, width - more :]


def main_kernel(
    geo, heads, info_ref, tok_ref, cot_ref, rows_ref, cols_ref, corner_ref, gain_ref, wqkv_hbm,
    wout_hbm, bias_ref,
    send_ref, keep_ref, bsum_ref, dproj, ftok, inv, cotb, gsum_ref,
    loc, rim_rows, rim_cols, rim_corner, fcot, normed, proj, gatt, att_t, dq_t,
    bias2, normed_t, gout, grads, wqkv_ref, wout_ref, sems,
):
    copies = [
        pltpu.make_async_copy(wqkv_hbm, wqkv_ref, sems.at[0]),
        pltpu.make_async_copy(wout_hbm, wout_ref, sems.at[1]),
    ]
    for copy in copies:
        copy.start()
    width = ftok.shape[1]
    win = geo.win
    head_size = width // heads
    scale = head_size ** (-0.5)

    for which, (ref, dst) in enumerate(((tok_ref, ftok), (cot_ref, fcot))):
        loc[...] = ref[...].astype(F32)
        if which == 0:
            rim_rows[...] = rows_ref[...].astype(F32)
            rim_cols[...] = cols_ref[...].astype(F32)
            rim_corner[...] = corner_ref[...].astype(F32)
        sources = {
            "local": (loc, 0),
            "rows": (rim_rows, which * geo.n_rows),
            "cols": (rim_cols, which * geo.n_cols),
            "corner": (rim_corner, which * geo.n_corner),
        }
        for z in range(geo.depth):
            for r in range(geo.rows):
                for name, first, column, length in forward_pieces(geo, z, r):
                    src, base = sources[name]
                    for at, count in window_cuts(column, length):
                        begin = base + first + at - column
                        cell = geo.cell(z, r, at)
                        dst[cell : cell + count] = src[begin : begin + count]

    gain = gain_ref[...]

    spot = lax.broadcasted_iota(jnp.int32, (win, win), 0)
    other = lax.broadcasted_iota(jnp.int32, (win, win), 1)
    half = WH * WW
    polar_a = jnp.where(spot >= half, spot - half, spot) >= (WH - SH) * WW
    polar_b = jnp.where(other >= half, other - half, other) >= (WH - SH) * WW
    flag_a = jnp.where(polar_a, 1.0, 0.0)
    flag_b = jnp.where(polar_b, 1.0, 0.0)
    mask = jnp.where(flag_a == flag_b, 0.0, -1e30)
    for h in range(heads):
        plain = bias_ref[h]
        bias2[0, h] = plain
        bias2[1, h] = plain + mask
        bsum_ref[h] = jnp.zeros((win, win), F32)
    gout[...] = jnp.zeros_like(gout)

    def norm_step(w, carry):
        at = pl.ds(pl.multiple_of(w * win, 16), win)
        x = ftok[at, :]
        centred = x - jnp.mean(x, axis=-1, keepdims=True)
        istd = lax.rsqrt(jnp.mean(centred * centred, axis=-1, keepdims=True) + 1e-05)
        unit = centred * istd
        ftok[at, :] = unit
        inv[at, :] = jnp.broadcast_to(istd, (win, 128))
        normed[at, :] = (unit * gain).astype(BF16)
        cotb[at, :] = fcot[at, :].astype(BF16)
        return carry

    lax.fori_loop(0, geo.nwin, norm_step, 0)
    for copy in copies:
        copy.wait()

    def proj_step(w, carry):
        at = pl.ds(pl.multiple_of(w * (2 * win), 16), 2 * win)
        x = normed[at, :]
        for part in range(3):
            cols = slice(part * width, (part + 1) * width)
            proj[at, cols] = dot(x, wqkv_ref[:, cols]).astype(BF16)
        gatt[at, :] = dot_nt(cotb[at, :], wout_ref[...]).astype(BF16)
        return carry

    lax.fori_loop(0, geo.nwin // 2, proj_step, 0)

    lane = lax.broadcasted_iota(jnp.int32, (win, 128), 1)
    lower = lane < head_size
    polar_from = geo.nwin - geo.wins_lon

    def attend(w, carry):
        at = pl.ds(pl.multiple_of(w * win, 16), win)
        sel = jnp.where(w >= polar_from, info_ref[LAST], 0)
        k_t = proj[at, width : 2 * width].T
        v_t = proj[at, 2 * width :].T
        for pair in range(heads // 2):
            cols = slice(pair * 128, (pair + 1) * 128)
            q = proj[at, cols] * BF16(scale)
            k = proj[at, width + pair * 128 : width + (pair + 1) * 128]
            v = proj[at, 2 * width + pair * 128 : 2 * width + (pair + 1) * 128]
            g = gatt[at, cols]
            dv = None
            dk = None
            for side in range(2):
                h = 2 * pair + side
                keep = lower if side == 0 else jnp.logical_not(lower)
                qm = jnp.where(keep, q, BF16(0))
                gm = jnp.where(keep, g, BF16(0))
                scores = dot_nt(k, qm) + bias2[sel, h]
                top = jnp.max(scores, axis=0, keepdims=True)
                grown = jnp.exp(scores - top)
                probs = grown * (1.0 / jnp.sum(grown, axis=0, keepdims=True))
                probs_low = probs.astype(BF16)
                gprobs = dot_nt(v, gm)
                weighted = jnp.sum(probs * gprobs, axis=0, keepdims=True)
                gscores = probs * (gprobs - weighted)
                bsum_ref[h] += gscores
                scores_low = gscores.astype(BF16)
                feats = slice(h * head_size, (h + 1) * head_size)
                att_t[feats, :] = dot(v_t[feats], probs_low).astype(BF16)
                dq_t[feats, :] = (dot(k_t[feats], scores_low) * scale).astype(BF16)
                dv_term = dot(probs_low, gm)
                dk_term = dot(scores_low, qm)
                dv = dv_term if dv is None else dv + dv_term
                dk = dk_term if dk is None else dk + dk_term
            dproj[at, width + pair * 128 : width + (pair + 1) * 128] = dk.astype(BF16)
            dproj[at, 2 * width + pair * 128 : 2 * width + (pair + 1) * 128] = dv.astype(BF16)
        dproj[at, 0:width] = dq_t[...].T
        gout[...] += dot(att_t[...], cotb[at, :])
        return carry

    lax.fori_loop(0, geo.nwin, attend, 0)

    grads[1, width:, :] = gout[...].astype(BF16)
    for block in range(geo.cells // 128):
        rows = slice(block * 128, (block + 1) * 128)
        normed_t[:, rows] = normed[rows, :].T

    gsum = jnp.zeros((width, 128), F32)
    for part in range(3):
        half, first = part // 2, part % 2 * width
        for sub in range(2):
            cols = slice(part * width + sub * 256, part * width + (sub + 1) * 256)
            term = dot(normed_t[...], dproj[:, cols])
            grads[half, first : first + width, sub * 256 : (sub + 1) * 256] = term.astype(BF16)
            term = term * wqkv_ref[:, cols].astype(F32)
            gsum = gsum + (term[:, :128] + term[:, 128:])
    gsum_ref[...] = gsum
    keep_ref[...] = grads[info_ref[CORE]]
    send_ref[...] = grads[1 - info_ref[CORE]]


def back_kernel(geo, dproj, unit_ref, inv, cotb, gain_ref, wqkv_ref, gtok_ref):
    win = geo.win
    gain = gain_ref[...]

    def back_step(w, carry):
        at = pl.ds(pl.multiple_of(w * win, 16), win)
        gn = dot_nt(dproj[at, :], wqkv_ref[...]).astype(BF16).astype(F32)
        unit = unit_ref[at, :]
        hat = gn * gain
        centre = jnp.mean(hat, axis=-1, keepdims=True)
        slope = jnp.mean(hat * unit, axis=-1, keepdims=True)
        istd = inv[at, 0:1]
        cot = cotb[at, :].astype(F32)
        gtok_ref[at, :] = (cot + istd * (hat - centre - unit * slope)).astype(BF16)
        return carry

    lax.fori_loop(0, geo.nwin, back_step, 0)


def unpack_send_kernel(geo, gtok_ref, rows_ref, cols_ref, corner_ref, fg, buf):
    base_cols = pad16(geo.n_rows)
    base_corner = base_cols + pad16(geo.n_cols)
    fg[...] = gtok_ref[...].astype(F32)
    buf[...] = jnp.zeros_like(buf)
    bases = {"rows": 0, "cols": base_cols, "corner": base_corner}
    for z in range(geo.depth):
        for r in range(geo.rows):
            for name, first, column, length in forward_pieces(geo, z, r):
                if name == "local":
                    continue
                for at, count in window_cuts(column, length):
                    to = bases[name] + first + at - column
                    cell = geo.cell(z, r, at)
                    buf[to : to + count] = fg[cell : cell + count]
    rows_ref[...] = buf[0:base_cols].astype(BF16)
    cols_ref[...] = buf[base_cols:base_corner].astype(BF16)
    corner_ref[...] = buf[base_corner : base_corner + pad16(geo.n_corner)].astype(BF16)


def assemble_kernel(geo, gtok_ref, rows_ref, cols_ref, corner_ref, out_ref, fg, rr, rc, rk, grid):
    fg[...] = gtok_ref[...].astype(F32)
    rr[...] = rows_ref[...].astype(F32)
    rc[...] = cols_ref[...].astype(F32)
    rk[...] = corner_ref[...].astype(F32)
    own = geo.cols - SW
    for z in range(geo.depth):
        for r in range(geo.rows):
            for name, first, column, length in forward_pieces(geo, z, r):
                if name != "local":
                    continue
                for at, count in window_cuts(column, length):
                    to = first + at - column
                    cell = geo.cell(z, r, at)
                    grid[to : to + count] = fg[cell : cell + count]
        for r in range(SH):
            to = geo.local(z, r, SW)
            grid[to : to + own] = rr[geo.rim_row(z, r) : geo.rim_row(z, r) + own]
            to = geo.local(z, r, 0)
            grid[to : to + SW] = rk[geo.corner(z, r) : geo.corner(z, r) + SW]
        for r in range(geo.rows - SH):
            to = geo.local(z, r + SH, 0)
            grid[to : to + SW] = rc[geo.rim_col(z, r) : geo.rim_col(z, r) + SW]
    out_ref[...] = grid[...].astype(BF16)


def call(kernel, out_shapes, scratch, n_in, limit, smem_first=False, cost=None):
    specs = [pl.BlockSpec(memory_space=pltpu.VMEM)] * n_in
    if smem_first:
        specs[0] = pl.BlockSpec(memory_space=pltpu.SMEM)
    return pl.pallas_call(
        kernel,
        out_shape=out_shapes,
        in_specs=specs,
        out_specs=jax.tree.map(lambda s: pl.BlockSpec(memory_space=pltpu.VMEM), out_shapes),
        scratch_shapes=scratch,
        compiler_params=pltpu.CompilerParams(vmem_limit_bytes=limit),
        cost_estimate=cost,
    )


def shape(dims, dtype):
    return jax.ShapeDtypeStruct(dims, dtype)


def moved(value, lat_step, lon_step):
    lats, lons = lax.axis_size("lat"), lax.axis_size("lon")
    pairs = []
    for a in range(lats):
        for o in range(lons):
            target = ((a - lat_step) % lats) * lons + (o - lon_step) % lons
            pairs.append((a * lons + o, target))
    return lax.ppermute(value, ("lat", "lon"), pairs)


class Chips:
    def __init__(self):
        self.lats, self.lons = lax.axis_size("lat"), lax.axis_size("lon")
        self.nz, self.nx, self.ny = self.lats // 2, 4, self.lons // 4

    def split(self, device):
        lat, lon = device // self.lons, device % self.lons
        x = lon // (2 * self.ny) * 2 + lat % 2
        return lat // 2, x, lon // 2 % self.ny, lon % 2

    def join(self, z, x, y, core):
        return (z * 2 + x % 2) * self.lons + (x // 2 * self.ny + y) * 2 + core

    def send(self, value, change):
        pairs = []
        for device in range(self.lats * self.lons):
            z, x, y, core = change(*self.split(device))
            pairs.append((device, self.join(z, x, y, core)))
        return lax.ppermute(value, ("lat", "lon"), pairs)

    def core(self, value):
        return self.send(value, lambda z, x, y, c: (z, x, y, 1 - c))

    def x(self, value, step):
        return self.send(value, lambda z, x, y, c: (z, (x + step) % self.nx, y, c))

    def y(self, value, step):
        return self.send(value, lambda z, x, y, c: (z, x, (y + step) % self.ny, c))

    def z(self, value, bit):
        return self.send(value, lambda z, x, y, c: (z ^ (2 * bit - 1), x, y, c))


def part_rows(info_ref, place, step, count, rows):
    part = (info_ref[place] + step) & (count - 1)
    return pl.ds(pl.multiple_of(part * rows, 16), rows)


def pair_sum_kernel(info_ref, keep_ref, recv_ref, *outs):
    for k, ref in enumerate(outs):
        at = part_rows(info_ref, Y, k, len(outs), ref.shape[0])
        ref[...] = (keep_ref[at, :].astype(F32) + recv_ref[at, :].astype(F32)).astype(BF16)


def total_of(refs):
    total = refs[0][...].astype(F32)
    for ref in refs[1:]:
        total += ref[...].astype(F32)
    return total


def cross_sum_kernel(ny, nx, info_ref, *refs):
    outs, hold = refs[ny : ny + nx], refs[-1]
    hold[...] = total_of(refs[:ny])
    for k, ref in enumerate(outs):
        at = part_rows(info_ref, X, k, nx, ref.shape[0])
        ref[...] = hold[at, :].astype(BF16)


SMALL = 16


def put_small(ref, base, total):
    top = total.astype(BF16)
    ref[base : base + SMALL] = top
    ref[base + SMALL : base + 2 * SMALL] = (total - top.astype(F32)).astype(BF16)


def small_of(refs, base):
    total = None
    for ref in refs:
        for part in range(2):
            at = base + part * SMALL
            term = ref[at : at + SMALL].astype(F32)
            total = term if total is None else total + term
    return total


def join_sum_kernel(*refs):
    piece = refs[0].shape[0]
    small_ref, out_ref = refs[-2:]
    out_ref[0:piece] = total_of(refs[:-2]).astype(BF16)
    put_small(out_ref, piece, small_ref[...])


def z_sum_kernel(mine_ref, got_ref, out_ref):
    rows = mine_ref.shape[0] - 2 * SMALL
    out_ref[0:rows] = (mine_ref[0:rows].astype(F32) + got_ref[0:rows].astype(F32)).astype(BF16)
    put_small(out_ref, rows, small_of((mine_ref, got_ref), rows))


def gather_kernel(place, info_ref, *refs):
    ins, out_ref = refs[:-1], refs[-1]
    piece = ins[0].shape[0] - 2 * SMALL
    for k, ref in enumerate(ins):
        at = part_rows(info_ref, place, len(ins) - k, len(ins), piece)
        out_ref[at, :] = ref[0:piece]
    put_small(out_ref, len(ins) * piece, small_of(ins, piece))


def place_rows(half, value_ref, gqkv_ref, gout_ref, hold, sems):
    width = gout_ref.shape[1]
    steps = 4
    rows = width // steps

    def write(targets):
        copies = []
        for which, target in enumerate(targets):
            for step in range(steps):
                at = slice(step * rows, (step + 1) * rows)
                src = slice(which * width + step * rows, which * width + (step + 1) * rows)
                hold[src] = value_ref[src].astype(F32)
                copy = pltpu.make_async_copy(
                    hold.at[src], target.at[at], sems.at[which, step]
                )
                copy.start()
                copies.append(copy)
        for copy in copies:
            copy.wait()

    @pl.when(half == 0)
    def _():
        write((gqkv_ref.at[:, 0:width], gqkv_ref.at[:, width : 2 * width]))

    @pl.when(half == 1)
    def _():
        write((gqkv_ref.at[:, 2 * width :], gout_ref))


def place_own_kernel(info_ref, mine_ref, gqkv_ref, gout_ref, hold, sems):
    place_rows(info_ref[CORE], mine_ref, gqkv_ref, gout_ref, hold, sems)


def place_other_kernel(
    info_ref, mine_ref, got_ref, gqkv_in, gout_in, gqkv_ref, gout_ref, line_ref, gain_ref, hold, sems
):
    width = gout_ref.shape[1]
    total = small_of((mine_ref, got_ref), 2 * width)
    more = line_ref.shape[1] - width
    line_ref[:, 0:width] = total[0:8]
    line_ref[:, width:] = total[8:, 0:more]
    gain_ref[:, 0 : width - more] = total[8:9, more:]
    gain_ref[:, width - more :] = total[9:10, more:]
    place_rows(1 - info_ref[CORE], got_ref, gqkv_ref, gout_ref, hold, sems)


def per_device(tokens, norm_gain, qkv_weight, out_weight, bias_table, bias_index, cotangent):
    depth, rows_lat, cols_lon, width = tokens.shape
    entries, heads = bias_table.shape
    geo = Geometry(depth, rows_lat, cols_lon)
    win, cells = geo.win, geo.cells
    tok = tokens.reshape(cells, width)
    cot = cotangent.reshape(cells, width)

    n_rows, n_cols, n_corner = pad16(2 * geo.n_rows), pad16(2 * geo.n_cols), pad16(2 * geo.n_corner)
    rim = pl.pallas_call(
        lambda *refs: pack_kernel(geo, *refs),
        out_shape=[shape((n, width), BF16) for n in (n_rows, n_cols, n_corner)],
        in_specs=[pl.BlockSpec(memory_space=pltpu.HBM)] * 2,
        out_specs=[pl.BlockSpec(memory_space=pltpu.VMEM)] * 3,
        scratch_shapes=[
            pltpu.VMEM((2, depth, SH, cols_lon, width), BF16),
            pltpu.VMEM((2, depth, rows_lat - SH, 16, width), BF16),
            pltpu.VMEM((2, depth, SH, cols_lon, width), F32),
            pltpu.VMEM((2, depth, rows_lat - SH, 16, width), F32),
            pltpu.VMEM((n_rows + n_cols + n_corner, width), F32),
            pltpu.SemaphoreType.DMA((2, 3)),
        ],
        compiler_params=pltpu.CompilerParams(vmem_limit_bytes=60 * MIB),
    )(tokens, cotangent)
    rim = (moved(rim[0], 1, 0), moved(rim[1], 0, 1), moved(rim[2], 1, 1))

    bias, index_t = call(
        lambda *refs: lookup_kernel(heads, *refs),
        [shape((heads, win, win), F32), shape((win, win), jnp.int32)],
        [pltpu.VMEM((3 * heads * BANDS, SPAN), F32)],
        2,
        8 * MIB,
        cost=pl.CostEstimate(flops=4 * 10**9, bytes_accessed=10**6, transcendentals=0),
    )(bias_index, bias_table.T)

    chips = Chips()
    ny, nx = chips.ny, chips.nx
    lat, lon = lax.axis_index("lat"), lax.axis_index("lon")
    is_last = (lat == chips.lats - 1).astype(jnp.int32)
    info = jnp.stack([is_last, lon % 2, lon // (2 * ny) * 2 + lat % 2, lon // 2 % ny])
    half_rows = 2 * width
    big = 36 * MIB
    small_limit = 10 * MIB

    vmem, smem = pl.BlockSpec(memory_space=pltpu.VMEM), pl.BlockSpec(memory_space=pltpu.SMEM)
    hbm = pl.BlockSpec(memory_space=pltpu.HBM)
    send, keep, bias_sum, grad_proj, unit, inv, cot_win, gain_sum = pl.pallas_call(
        lambda *refs: main_kernel(geo, heads, *refs),
        in_specs=[smem] + [vmem] * 6 + [hbm, hbm, vmem],
        out_specs=[vmem] * 8,
        compiler_params=pltpu.CompilerParams(vmem_limit_bytes=big),
        out_shape=[
            shape((half_rows, width), BF16),
            shape((half_rows, width), BF16),
            shape((heads, win, win), F32),
            shape((cells, 3 * width), BF16),
            shape((cells, width), F32),
            shape((cells, 128), F32),
            shape((cells, width), BF16),
            shape((width, 128), F32),
        ],
        scratch_shapes=[
            pltpu.VMEM((cells, width), F32),
            pltpu.VMEM((n_rows, width), F32),
            pltpu.VMEM((n_cols, width), F32),
            pltpu.VMEM((n_corner, width), F32),
            pltpu.VMEM((cells, width), F32),
            pltpu.VMEM((cells, width), BF16),
            pltpu.VMEM((cells, 3 * width), BF16),
            pltpu.VMEM((cells, width), BF16),
            pltpu.VMEM((width, win), BF16),
            pltpu.VMEM((width, win), BF16),
            pltpu.VMEM((2, heads, win, win), F32),
            pltpu.VMEM((width, cells), BF16),
            pltpu.VMEM((width, width), F32),
            pltpu.VMEM((2, half_rows, width), BF16),
            pltpu.VMEM((width, 3 * width), BF16),
            pltpu.VMEM((width, width), BF16),
            pltpu.SemaphoreType.DMA((2,)),
        ],
    )(info, tok, cot, *rim, norm_gain.reshape(1, width), qkv_weight, out_weight, bias)

    got = chips.core(send)
    piece = half_rows // ny
    outs = call(
        pair_sum_kernel,
        [shape((piece, width), BF16)] * ny,
        [],
        3,
        small_limit,
        smem_first=True,
    )(info, keep, got)

    outs, grad_proj, qkv_weight, bias_sum = lax.optimization_barrier(
        (outs, grad_proj, qkv_weight, bias_sum)
    )
    got = [outs[0]] + [chips.y(outs[k], k) for k in range(1, ny)]
    gain_row = norm_gain.reshape(1, width)
    gtok = call(
        lambda *refs: back_kernel(geo, *refs),
        shape((cells, width), BF16),
        [],
        6,
        small_limit,
        cost=pl.CostEstimate(flops=6 * 10**9, bytes_accessed=10**7, transcendentals=0),
    )(grad_proj, unit, inv, cot_win, gain_row, qkv_weight)
    small = call(
        lambda *refs: table_kernel(heads, *refs),
        shape((SMALL, width), F32),
        [pltpu.VMEM((heads * BANDS, SPAN), F32), pltpu.VMEM((heads, BANDS * SPAN), F32)],
        4,
        small_limit,
        cost=pl.CostEstimate(flops=3 * 10**9, bytes_accessed=10**6, transcendentals=0),
    )(index_t, bias_sum, gain_sum, gain_row)
    got, gtok, small = lax.optimization_barrier((got, gtok, small))
    part = piece // nx
    outs = call(
        lambda *refs: cross_sum_kernel(ny, nx, *refs),
        [shape((part, width), BF16)] * nx,
        [pltpu.VMEM((piece, width), F32)],
        1 + ny,
        small_limit,
        smem_first=True,
    )(info, *got)

    got = [outs[0]] + [chips.x(outs[k], k) for k in range(1, nx)]
    mine = call(
        join_sum_kernel,
        shape((part + 2 * SMALL, width), BF16),
        [],
        nx + 1,
        small_limit,
    )(*got, small)
    bit = 1
    while bit < chips.nz:
        mine = call(z_sum_kernel, shape(mine.shape, BF16), [], 2, small_limit)(
            mine, chips.z(mine, bit)
        )
        bit *= 2

    def gathered(place, count, parts):
        rows = (parts[0].shape[0] - 2 * SMALL) * count + 2 * SMALL
        return call(
            lambda *refs: gather_kernel(place, *refs),
            shape((rows, width), BF16),
            [],
            1 + count,
            small_limit,
            smem_first=True,
        )(info, *parts)

    mine = gathered(X, nx, [mine] + [chips.x(mine, k) for k in range(1, nx)])
    parts = [mine] + [chips.y(mine, k) for k in range(1, ny)]

    parts[-1], gtok = lax.optimization_barrier((parts[-1], gtok))
    b_rows, b_cols, b_corner = pad16(geo.n_rows), pad16(geo.n_cols), pad16(geo.n_corner)
    back = call(
        lambda *refs: unpack_send_kernel(geo, *refs),
        [shape((n, width), BF16) for n in (b_rows, b_cols, b_corner)],
        [
            pltpu.VMEM((cells, width), F32),
            pltpu.VMEM((b_rows + b_cols + b_corner, width), F32),
        ],
        1,
        small_limit,
    )(gtok)
    back = (moved(back[0], -1, 0), moved(back[1], 0, -1), moved(back[2], -1, -1))
    parts, back = lax.optimization_barrier((parts, back))
    grad_tokens = call(
        lambda *refs: assemble_kernel(geo, *refs),
        shape((cells, width), BF16),
        [
            pltpu.VMEM((cells, width), F32),
            pltpu.VMEM((b_rows, width), F32),
            pltpu.VMEM((b_cols, width), F32),
            pltpu.VMEM((b_corner, width), F32),
            pltpu.VMEM((cells, width), F32),
        ],
        4,
        small_limit,
    )(gtok, *back)
    mine = gathered(Y, ny, parts)
    other = chips.core(mine)

    outputs = [shape((width, 3 * width), F32), shape((width, width), F32)]
    scratch = [pltpu.VMEM((half_rows, width), F32), pltpu.SemaphoreType.DMA((2, 4))]
    params = pltpu.CompilerParams(vmem_limit_bytes=small_limit)
    written = pl.pallas_call(
        place_own_kernel,
        out_shape=outputs,
        in_specs=[smem, vmem],
        out_specs=[hbm, hbm],
        scratch_shapes=scratch,
        compiler_params=params,
    )(info, mine)
    grad_qkv, grad_out, line, grad_gain = pl.pallas_call(
        place_other_kernel,
        out_shape=outputs + [shape((heads, BANDS * SPAN), F32), shape((1, width), F32)],
        in_specs=[smem, vmem, vmem, hbm, hbm],
        out_specs=[hbm, hbm, vmem, vmem],
        input_output_aliases={3: 0, 4: 1},
        scratch_shapes=scratch,
        compiler_params=params,
    )(info, mine, other, *written)
    grad_bias = line.T[:entries]
    return (grad_tokens.reshape(tokens.shape), grad_qkv, grad_out, grad_bias, grad_gain.reshape(width))


def solution(mesh):
    in_specs = (P(None, "lat", "lon", None), P(), P(), P(), P(), P(), P(None, "lat", "lon", None))
    out_specs = (P(None, "lat", "lon", None), P(), P(), P(), P())
    return jax.shard_map(
        per_device, mesh=mesh, in_specs=in_specs, out_specs=out_specs, check_vma=False
    )
```

```python
import jax
import jax.numpy as jnp
from jax import lax
from jax.experimental import pallas as pl
from jax.experimental.pallas import tpu as pltpu
from jax.sharding import PartitionSpec as P

WH = 6
WW = 12
SH = 3
SW = 6
F32 = jnp.float32
BF16 = jnp.bfloat16
MIB = 1024 * 1024

LAST, CORE, X, Y = range(4)

NT = (((1,), (1,)), ((), ()))


def dot(a, b):
    return jnp.dot(a, b, preferred_element_type=F32)


def dot_nt(a, b):
    return lax.dot_general(a, b, NT, preferred_element_type=F32)


class Geometry:
    def __init__(self, depth, rows, cols):
        self.depth, self.rows, self.cols = depth, rows, cols
        self.cells = depth * rows * cols
        self.win = depth * WH * WW
        self.nwin = self.cells // self.win
        self.wins_lon = cols // WW
        self.wins_lat = rows // WH
        self.n_rows = depth * SH * (cols - SW)
        self.n_cols = depth * (rows - SH) * SW
        self.n_corner = depth * SH * SW

    def local(self, z, r, c):
        return (z * self.rows + r) * self.cols + c

    def rim_row(self, z, r):
        return (z * SH + r) * (self.cols - SW)

    def rim_col(self, z, r):
        return (z * (self.rows - SH) + r) * SW

    def corner(self, z, r):
        return (z * SH + r) * SW

    def cell(self, z, r, c):
        window = (r // WH) * self.wins_lon + c // WW
        return window * self.win + (z * WH + r % WH) * WW + c % WW


def pad16(n):
    return (n + 15) // 16 * 16


def forward_pieces(geo, z, r):
    own = geo.cols - SW
    if r < geo.rows - SH:
        first = ("local", geo.local(z, r + SH, SW), 0, own)
        second = ("cols", geo.rim_col(z, r), own, SW)
    else:
        first = ("rows", geo.rim_row(z, r - geo.rows + SH), 0, own)
        second = ("corner", geo.corner(z, r - geo.rows + SH), own, SW)
    return (first, second)


def window_cuts(start, length):
    at = start
    while at < start + length:
        stop = min(start + length, (at // WW + 1) * WW)
        yield at, stop - at
        at = stop


def pack_kernel(geo, tok_ref, cot_ref, rows_ref, cols_ref, corner_ref, top, left, wide, slim, buf, sems):
    n_rows, n_cols, n_corner = geo.n_rows, geo.n_cols, geo.n_corner
    base_cols = pad16(2 * n_rows)
    base_corner = base_cols + pad16(2 * n_cols)
    own = geo.cols - SW
    copies = []
    for which, ref in enumerate((tok_ref, cot_ref)):
        for part, (src, dst) in enumerate(
            (
                (ref.at[:, 0:SH], top.at[which]),
                (ref.at[0, SH : geo.rows, 0:16], left.at[which, 0]),
                (ref.at[1, SH : geo.rows, 0:16], left.at[which, 1]),
            )
        ):
            copy = pltpu.make_async_copy(src, dst, sems.at[which, part])
            copy.start()
            copies.append(copy)
    buf[base_cols - 16 : base_cols] = jnp.zeros((16, buf.shape[1]), F32)
    buf[base_corner - 16 : base_corner] = jnp.zeros((16, buf.shape[1]), F32)
    buf[-16:] = jnp.zeros((16, buf.shape[1]), F32)
    for copy in copies:
        copy.wait()
    wide[...] = top[...].astype(F32)
    slim[...] = left[...].astype(F32)
    for which in range(2):
        for z in range(geo.depth):
            for r in range(SH):
                at = which * n_rows + geo.rim_row(z, r)
                buf[at : at + own] = wide[which, z, r, SW:]
                at = base_corner + which * n_corner + geo.corner(z, r)
                buf[at : at + SW] = wide[which, z, r, 0:SW]
            for r in range(geo.rows - SH):
                at = base_cols + which * n_cols + geo.rim_col(z, r)
                buf[at : at + SW] = slim[which, z, r, 0:SW]
    rows_ref[...] = buf[0:base_cols].astype(BF16)
    cols_ref[...] = buf[base_cols:base_corner].astype(BF16)
    corner_ref[...] = buf[base_corner : base_corner + pad16(2 * n_corner)].astype(BF16)


BANDS = 8
SPAN = 96


def band_of(index):
    band = (index * 683) >> 16
    return band, index - band * SPAN


def lookup_kernel(heads, raw_ref, table_ref, bias_ref, idx_ref, split):
    win = idx_ref.shape[0]
    rows = heads * BANDS
    entries = table_ref.shape[1]
    idx_ref[...] = raw_ref[...].T
    split[...] = jnp.zeros_like(split)
    rest = table_ref[...]
    for part in range(3):
        low = rest.astype(BF16).astype(F32)
        for band in range(BANDS):
            at = part * rows + band * heads
            stop = min(entries, (band + 1) * SPAN)
            split[at : at + heads, 0 : stop - band * SPAN] = low[:, band * SPAN : stop]
        rest = rest - low
    table = split[...].astype(BF16)
    iota = lax.broadcasted_iota(jnp.int32, (SPAN, win), 0)

    def step(block, carry):
        start = pl.multiple_of(block * 8, 8)
        band, place = band_of(idx_ref[pl.ds(start, 8), :])
        for j in range(8):
            onehot = jnp.where(iota == place[j : j + 1, :], 1.0, 0.0).astype(BF16)
            found = dot(table, onehot)
            found = (found[:rows] + found[rows : 2 * rows]) + found[2 * rows :]
            mine = jnp.broadcast_to(band[j : j + 1, :], (heads, win))
            total = jnp.zeros((heads, win), F32)
            for b in range(BANDS):
                total = jnp.where(mine == b, found[b * heads : (b + 1) * heads], total)
            for h in range(heads):
                bias_ref[h, pl.ds(start + j, 1), :] = total[h : h + 1]
        return carry

    lax.fori_loop(0, win // 8, step, 0)


def table_sums(heads, first, count, idx_ref, sum_ref, acc):
    win = idx_ref.shape[0]
    rows = heads * BANDS
    iota = lax.broadcasted_iota(jnp.int32, (SPAN, win), 0)
    bands = lax.broadcasted_iota(jnp.int32, (BANDS, win), 0)

    def step(block, carry):
        start = pl.multiple_of(first + block * 8, 8)
        band, place = band_of(idx_ref[pl.ds(start, 8), :])
        tops, rests = [], []
        for h in range(heads):
            slab = sum_ref[h, pl.ds(start, 8), :]
            top = slab.astype(BF16).astype(F32)
            tops.append(top)
            rests.append(slab - top)
        total = None
        for j in range(8):
            onehot = jnp.where(iota == place[j : j + 1, :], 1.0, 0.0).astype(BF16)
            keep = jnp.where(bands == band[j : j + 1, :], 1.0, 0.0)
            spread = [p[h][j : j + 1, :] * keep for p in (tops, rests) for h in range(heads)]
            term = dot_nt(jnp.concatenate(spread, axis=0).astype(BF16), onehot)
            total = term if total is None else total + term
        acc[...] += total[:rows] + total[rows:]
        return carry

    lax.fori_loop(0, count // 8, step, 0)


def table_kernel(heads, idx_ref, sum_ref, gsum_ref, gain_ref, out_ref, acc, line):
    acc[...] = jnp.zeros_like(acc)
    table_sums(heads, 0, idx_ref.shape[0], idx_ref, sum_ref, acc)
    for h in range(heads):
        for b in range(BANDS):
            line[h : h + 1, b * SPAN : (b + 1) * SPAN] = acc[h * BANDS + b : h * BANDS + b + 1, :]
    width = out_ref.shape[1]
    more = BANDS * SPAN - width
    gain = jnp.sum(gsum_ref[...].T, axis=0, keepdims=True) / gain_ref[...]
    out_ref[0:heads, :] = line[:, :width]
    out_ref[heads:, 0:more] = line[:, width:]
    out_ref[heads:, more:] = jnp.zeros((16 - heads, width - more), F32)
    out_ref[heads : heads + 1, more:] = gain[:, : width - more]
    out_ref[heads + 1 : heads + 2, more:] = gain[:, width - more :]


def main_kernel(
    geo, heads, info_ref, tok_ref, cot_ref, rows_ref, cols_ref, corner_ref, gain_ref, wqkv_hbm,
    wout_hbm, bias_ref,
    send_ref, keep_ref, bsum_ref, dproj, ftok, inv, cotb, gsum_ref,
    loc, rim_rows, rim_cols, rim_corner, fcot, normed, proj, gatt, att_t, dq_t,
    bias2, normed_t, gout, grads, wqkv_ref, wout_ref, sems,
):
    copies = [
        pltpu.make_async_copy(wqkv_hbm, wqkv_ref, sems.at[0]),
        pltpu.make_async_copy(wout_hbm, wout_ref, sems.at[1]),
    ]
    for copy in copies:
        copy.start()
    width = ftok.shape[1]
    win = geo.win
    head_size = width // heads
    scale = head_size ** (-0.5)

    for which, (ref, dst) in enumerate(((tok_ref, ftok), (cot_ref, fcot))):
        loc[...] = ref[...].astype(F32)
        if which == 0:
            rim_rows[...] = rows_ref[...].astype(F32)
            rim_cols[...] = cols_ref[...].astype(F32)
            rim_corner[...] = corner_ref[...].astype(F32)
        sources = {
            "local": (loc, 0),
            "rows": (rim_rows, which * geo.n_rows),
            "cols": (rim_cols, which * geo.n_cols),
            "corner": (rim_corner, which * geo.n_corner),
        }
        for z in range(geo.depth):
            for r in range(geo.rows):
                for name, first, column, length in forward_pieces(geo, z, r):
                    src, base = sources[name]
                    for at, count in window_cuts(column, length):
                        begin = base + first + at - column
                        cell = geo.cell(z, r, at)
                        dst[cell : cell + count] = src[begin : begin + count]

    gain = gain_ref[...]

    spot = lax.broadcasted_iota(jnp.int32, (win, win), 0)
    other = lax.broadcasted_iota(jnp.int32, (win, win), 1)
    half = WH * WW
    polar_a = jnp.where(spot >= half, spot - half, spot) >= (WH - SH) * WW
    polar_b = jnp.where(other >= half, other - half, other) >= (WH - SH) * WW
    flag_a = jnp.where(polar_a, 1.0, 0.0)
    flag_b = jnp.where(polar_b, 1.0, 0.0)
    mask = jnp.where(flag_a == flag_b, 0.0, -1e30)
    for h in range(heads):
        plain = bias_ref[h]
        bias2[0, h] = plain
        bias2[1, h] = plain + mask
        bsum_ref[h] = jnp.zeros((win, win), F32)
    gout[...] = jnp.zeros_like(gout)

    def norm_step(w, carry):
        at = pl.ds(pl.multiple_of(w * win, 16), win)
        x = ftok[at, :]
        centred = x - jnp.mean(x, axis=-1, keepdims=True)
        istd = lax.rsqrt(jnp.mean(centred * centred, axis=-1, keepdims=True) + 1e-05)
        unit = centred * istd
        ftok[at, :] = unit
        inv[at, :] = jnp.broadcast_to(istd, (win, 128))
        normed[at, :] = (unit * gain).astype(BF16)
        cotb[at, :] = fcot[at, :].astype(BF16)
        return carry

    lax.fori_loop(0, geo.nwin, norm_step, 0)
    for copy in copies:
        copy.wait()

    def proj_step(w, carry):
        at = pl.ds(pl.multiple_of(w * (2 * win), 16), 2 * win)
        x = normed[at, :]
        for part in range(3):
            cols = slice(part * width, (part + 1) * width)
            proj[at, cols] = dot(x, wqkv_ref[:, cols]).astype(BF16)
        gatt[at, :] = dot_nt(cotb[at, :], wout_ref[...]).astype(BF16)
        return carry

    lax.fori_loop(0, geo.nwin // 2, proj_step, 0)

    lane = lax.broadcasted_iota(jnp.int32, (win, 128), 1)
    lower = lane < head_size
    polar_from = geo.nwin - geo.wins_lon

    def attend(w, carry):
        at = pl.ds(pl.multiple_of(w * win, 16), win)
        sel = jnp.where(w >= polar_from, info_ref[LAST], 0)
        k_t = proj[at, width : 2 * width].T
        v_t = proj[at, 2 * width :].T
        for pair in range(heads // 2):
            cols = slice(pair * 128, (pair + 1) * 128)
            q = proj[at, cols] * BF16(scale)
            k = proj[at, width + pair * 128 : width + (pair + 1) * 128]
            v = proj[at, 2 * width + pair * 128 : 2 * width + (pair + 1) * 128]
            g = gatt[at, cols]
            dv = None
            dk = None
            for side in range(2):
                h = 2 * pair + side
                keep = lower if side == 0 else jnp.logical_not(lower)
                qm = jnp.where(keep, q, BF16(0))
                gm = jnp.where(keep, g, BF16(0))
                scores = dot_nt(k, qm) + bias2[sel, h]
                top = jnp.max(scores, axis=0, keepdims=True)
                grown = jnp.exp(scores - top)
                probs = grown * (1.0 / jnp.sum(grown, axis=0, keepdims=True))
                probs_low = probs.astype(BF16)
                gprobs = dot_nt(v, gm)
                weighted = jnp.sum(probs * gprobs, axis=0, keepdims=True)
                gscores = probs * (gprobs - weighted)
                bsum_ref[h] += gscores
                scores_low = gscores.astype(BF16)
                feats = slice(h * head_size, (h + 1) * head_size)
                att_t[feats, :] = dot(v_t[feats], probs_low).astype(BF16)
                dq_t[feats, :] = (dot(k_t[feats], scores_low) * scale).astype(BF16)
                dv_term = dot(probs_low, gm)
                dk_term = dot(scores_low, qm)
                dv = dv_term if dv is None else dv + dv_term
                dk = dk_term if dk is None else dk + dk_term
            dproj[at, width + pair * 128 : width + (pair + 1) * 128] = dk.astype(BF16)
            dproj[at, 2 * width + pair * 128 : 2 * width + (pair + 1) * 128] = dv.astype(BF16)
        dproj[at, 0:width] = dq_t[...].T
        gout[...] += dot(att_t[...], cotb[at, :])
        return carry

    lax.fori_loop(0, geo.nwin, attend, 0)

    grads[1, width:, :] = gout[...].astype(BF16)
    for block in range(geo.cells // 128):
        rows = slice(block * 128, (block + 1) * 128)
        normed_t[:, rows] = normed[rows, :].T

    gsum = jnp.zeros((width, 128), F32)
    for part in range(3):
        half, first = part // 2, part % 2 * width
        for sub in range(2):
            cols = slice(part * width + sub * 256, part * width + (sub + 1) * 256)
            term = dot(normed_t[...], dproj[:, cols])
            grads[half, first : first + width, sub * 256 : (sub + 1) * 256] = term.astype(BF16)
            term = term * wqkv_ref[:, cols].astype(F32)
            gsum = gsum + (term[:, :128] + term[:, 128:])
    gsum_ref[...] = gsum
    keep_ref[...] = grads[info_ref[CORE]]
    send_ref[...] = grads[1 - info_ref[CORE]]


def back_kernel(geo, first, count, dproj, unit_ref, inv, cotb, gain_ref, wqkv_ref, gtok_ref):
    win = geo.win
    gain = gain_ref[...]

    def back_step(w, carry):
        at = pl.ds(pl.multiple_of((first + w) * win, 16), win)
        gn = dot_nt(dproj[at, :], wqkv_ref[...]).astype(BF16).astype(F32)
        unit = unit_ref[at, :]
        hat = gn * gain
        centre = jnp.mean(hat, axis=-1, keepdims=True)
        slope = jnp.mean(hat * unit, axis=-1, keepdims=True)
        istd = inv[at, 0:1]
        cot = cotb[at, :].astype(F32)
        to = pl.ds(pl.multiple_of(w * win, 16), win)
        gtok_ref[to, :] = (cot + istd * (hat - centre - unit * slope)).astype(BF16)
        return carry

    lax.fori_loop(0, count, back_step, 0)


def unpack_send_kernel(geo, low_ref, high_ref, rows_ref, cols_ref, corner_ref, fg, buf):
    base_cols = pad16(geo.n_rows)
    base_corner = base_cols + pad16(geo.n_cols)
    half = low_ref.shape[0]
    fg[0:half] = low_ref[...].astype(F32)
    fg[half:] = high_ref[...].astype(F32)
    buf[...] = jnp.zeros_like(buf)
    bases = {"rows": 0, "cols": base_cols, "corner": base_corner}
    for z in range(geo.depth):
        for r in range(geo.rows):
            for name, first, column, length in forward_pieces(geo, z, r):
                if name == "local":
                    continue
                for at, count in window_cuts(column, length):
                    to = bases[name] + first + at - column
                    cell = geo.cell(z, r, at)
                    buf[to : to + count] = fg[cell : cell + count]
    rows_ref[...] = buf[0:base_cols].astype(BF16)
    cols_ref[...] = buf[base_cols:base_corner].astype(BF16)
    corner_ref[...] = buf[base_corner : base_corner + pad16(geo.n_corner)].astype(BF16)


def assemble_kernel(geo, low_ref, high_ref, rows_ref, cols_ref, corner_ref, out_ref, fg, rr, rc, rk, grid):
    half = low_ref.shape[0]
    fg[0:half] = low_ref[...].astype(F32)
    fg[half:] = high_ref[...].astype(F32)
    rr[...] = rows_ref[...].astype(F32)
    rc[...] = cols_ref[...].astype(F32)
    rk[...] = corner_ref[...].astype(F32)
    own = geo.cols - SW
    for z in range(geo.depth):
        for r in range(geo.rows):
            for name, first, column, length in forward_pieces(geo, z, r):
                if name != "local":
                    continue
                for at, count in window_cuts(column, length):
                    to = first + at - column
                    cell = geo.cell(z, r, at)
                    grid[to : to + count] = fg[cell : cell + count]
        for r in range(SH):
            to = geo.local(z, r, SW)
            grid[to : to + own] = rr[geo.rim_row(z, r) : geo.rim_row(z, r) + own]
            to = geo.local(z, r, 0)
            grid[to : to + SW] = rk[geo.corner(z, r) : geo.corner(z, r) + SW]
        for r in range(geo.rows - SH):
            to = geo.local(z, r + SH, 0)
            grid[to : to + SW] = rc[geo.rim_col(z, r) : geo.rim_col(z, r) + SW]
    out_ref[...] = grid[...].astype(BF16)


def call(kernel, out_shapes, scratch, n_in, limit, smem_first=False, cost=None):
    specs = [pl.BlockSpec(memory_space=pltpu.VMEM)] * n_in
    if smem_first:
        specs[0] = pl.BlockSpec(memory_space=pltpu.SMEM)
    return pl.pallas_call(
        kernel,
        out_shape=out_shapes,
        in_specs=specs,
        out_specs=jax.tree.map(lambda s: pl.BlockSpec(memory_space=pltpu.VMEM), out_shapes),
        scratch_shapes=scratch,
        compiler_params=pltpu.CompilerParams(vmem_limit_bytes=limit),
        cost_estimate=cost,
    )


def shape(dims, dtype):
    return jax.ShapeDtypeStruct(dims, dtype)


def moved(value, lat_step, lon_step):
    lats, lons = lax.axis_size("lat"), lax.axis_size("lon")
    pairs = []
    for a in range(lats):
        for o in range(lons):
            target = ((a - lat_step) % lats) * lons + (o - lon_step) % lons
            pairs.append((a * lons + o, target))
    return lax.ppermute(value, ("lat", "lon"), pairs)


class Chips:
    def __init__(self):
        self.lats, self.lons = lax.axis_size("lat"), lax.axis_size("lon")
        self.nz, self.nx, self.ny = self.lats // 2, 4, self.lons // 4

    def split(self, device):
        lat, lon = device // self.lons, device % self.lons
        x = lon // (2 * self.ny) * 2 + lat % 2
        return lat // 2, x, lon // 2 % self.ny, lon % 2

    def join(self, z, x, y, core):
        return (z * 2 + x % 2) * self.lons + (x // 2 * self.ny + y) * 2 + core

    def send(self, value, change):
        pairs = []
        for device in range(self.lats * self.lons):
            z, x, y, core = change(*self.split(device))
            pairs.append((device, self.join(z, x, y, core)))
        return lax.ppermute(value, ("lat", "lon"), pairs)

    def core(self, value):
        return self.send(value, lambda z, x, y, c: (z, x, y, 1 - c))

    def x(self, value, step):
        return self.send(value, lambda z, x, y, c: (z, (x + step) % self.nx, y, c))

    def y(self, value, step):
        return self.send(value, lambda z, x, y, c: (z, x, (y + step) % self.ny, c))

    def z(self, value, bit):
        return self.send(value, lambda z, x, y, c: (z ^ (2 * bit - 1), x, y, c))


def part_rows(info_ref, place, step, count, rows):
    part = (info_ref[place] + step) & (count - 1)
    return pl.ds(pl.multiple_of(part * rows, 16), rows)


def pair_sum_kernel(info_ref, keep_ref, recv_ref, *outs):
    for k, ref in enumerate(outs):
        at = part_rows(info_ref, Y, k, len(outs), ref.shape[0])
        ref[...] = (keep_ref[at, :].astype(F32) + recv_ref[at, :].astype(F32)).astype(BF16)


def total_of(refs):
    total = refs[0][...].astype(F32)
    for ref in refs[1:]:
        total += ref[...].astype(F32)
    return total


def cross_sum_kernel(ny, nx, info_ref, *refs):
    outs, hold = refs[ny : ny + nx], refs[-1]
    hold[...] = total_of(refs[:ny])
    for k, ref in enumerate(outs):
        at = part_rows(info_ref, X, k, nx, ref.shape[0])
        ref[...] = hold[at, :].astype(BF16)


SMALL = 16


def put_small(ref, base, total):
    top = total.astype(BF16)
    ref[base : base + SMALL] = top
    ref[base + SMALL : base + 2 * SMALL] = (total - top.astype(F32)).astype(BF16)


def small_of(refs, base):
    total = None
    for ref in refs:
        for part in range(2):
            at = base + part * SMALL
            term = ref[at : at + SMALL].astype(F32)
            total = term if total is None else total + term
    return total


def join_sum_kernel(*refs):
    piece = refs[0].shape[0]
    small_ref, out_ref = refs[-2:]
    out_ref[0:piece] = total_of(refs[:-2]).astype(BF16)
    put_small(out_ref, piece, small_ref[...])


def z_sum_kernel(mine_ref, got_ref, out_ref):
    rows = mine_ref.shape[0] - 2 * SMALL
    out_ref[0:rows] = (mine_ref[0:rows].astype(F32) + got_ref[0:rows].astype(F32)).astype(BF16)
    put_small(out_ref, rows, small_of((mine_ref, got_ref), rows))


def gather_kernel(place, info_ref, *refs):
    ins, out_ref = refs[:-1], refs[-1]
    piece = ins[0].shape[0] - 2 * SMALL
    for k, ref in enumerate(ins):
        at = part_rows(info_ref, place, len(ins) - k, len(ins), piece)
        out_ref[at, :] = ref[0:piece]
    put_small(out_ref, len(ins) * piece, small_of(ins, piece))


def place_rows(half, value_ref, gqkv_ref, gout_ref, hold, sems):
    width = gout_ref.shape[1]
    steps = 4
    rows = width // steps

    def write(targets):
        copies = []
        for which, target in enumerate(targets):
            for step in range(steps):
                at = slice(step * rows, (step + 1) * rows)
                src = slice(which * width + step * rows, which * width + (step + 1) * rows)
                hold[src] = value_ref[src].astype(F32)
                copy = pltpu.make_async_copy(
                    hold.at[src], target.at[at], sems.at[which, step]
                )
                copy.start()
                copies.append(copy)
        for copy in copies:
            copy.wait()

    @pl.when(half == 0)
    def _():
        write((gqkv_ref.at[:, 0:width], gqkv_ref.at[:, width : 2 * width]))

    @pl.when(half == 1)
    def _():
        write((gqkv_ref.at[:, 2 * width :], gout_ref))


def place_own_kernel(info_ref, mine_ref, gqkv_ref, gout_ref, hold, sems):
    place_rows(info_ref[CORE], mine_ref, gqkv_ref, gout_ref, hold, sems)


def place_other_kernel(
    info_ref, mine_ref, got_ref, gqkv_in, gout_in, gqkv_ref, gout_ref, line_ref, gain_ref, hold, sems
):
    width = gout_ref.shape[1]
    total = small_of((mine_ref, got_ref), 2 * width)
    more = line_ref.shape[1] - width
    line_ref[:, 0:width] = total[0:8]
    line_ref[:, width:] = total[8:, 0:more]
    gain_ref[:, 0 : width - more] = total[8:9, more:]
    gain_ref[:, width - more :] = total[9:10, more:]
    place_rows(1 - info_ref[CORE], got_ref, gqkv_ref, gout_ref, hold, sems)


def per_device(tokens, norm_gain, qkv_weight, out_weight, bias_table, bias_index, cotangent):
    depth, rows_lat, cols_lon, width = tokens.shape
    entries, heads = bias_table.shape
    geo = Geometry(depth, rows_lat, cols_lon)
    win, cells = geo.win, geo.cells
    tok = tokens.reshape(cells, width)
    cot = cotangent.reshape(cells, width)

    n_rows, n_cols, n_corner = pad16(2 * geo.n_rows), pad16(2 * geo.n_cols), pad16(2 * geo.n_corner)
    rim = pl.pallas_call(
        lambda *refs: pack_kernel(geo, *refs),
        out_shape=[shape((n, width), BF16) for n in (n_rows, n_cols, n_corner)],
        in_specs=[pl.BlockSpec(memory_space=pltpu.HBM)] * 2,
        out_specs=[pl.BlockSpec(memory_space=pltpu.VMEM)] * 3,
        scratch_shapes=[
            pltpu.VMEM((2, depth, SH, cols_lon, width), BF16),
            pltpu.VMEM((2, depth, rows_lat - SH, 16, width), BF16),
            pltpu.VMEM((2, depth, SH, cols_lon, width), F32),
            pltpu.VMEM((2, depth, rows_lat - SH, 16, width), F32),
            pltpu.VMEM((n_rows + n_cols + n_corner, width), F32),
            pltpu.SemaphoreType.DMA((2, 3)),
        ],
        compiler_params=pltpu.CompilerParams(vmem_limit_bytes=60 * MIB),
    )(tokens, cotangent)
    rim = (moved(rim[0], 1, 0), moved(rim[1], 0, 1), moved(rim[2], 1, 1))

    bias, index_t = call(
        lambda *refs: lookup_kernel(heads, *refs),
        [shape((heads, win, win), F32), shape((win, win), jnp.int32)],
        [pltpu.VMEM((3 * heads * BANDS, SPAN), F32)],
        2,
        8 * MIB,
        cost=pl.CostEstimate(flops=4 * 10**9, bytes_accessed=10**6, transcendentals=0),
    )(bias_index, bias_table.T)

    chips = Chips()
    ny, nx = chips.ny, chips.nx
    lat, lon = lax.axis_index("lat"), lax.axis_index("lon")
    is_last = (lat == chips.lats - 1).astype(jnp.int32)
    info = jnp.stack([is_last, lon % 2, lon // (2 * ny) * 2 + lat % 2, lon // 2 % ny])
    half_rows = 2 * width
    big = 36 * MIB
    small_limit = 10 * MIB

    vmem, smem = pl.BlockSpec(memory_space=pltpu.VMEM), pl.BlockSpec(memory_space=pltpu.SMEM)
    hbm = pl.BlockSpec(memory_space=pltpu.HBM)
    send, keep, bias_sum, grad_proj, unit, inv, cot_win, gain_sum = pl.pallas_call(
        lambda *refs: main_kernel(geo, heads, *refs),
        in_specs=[smem] + [vmem] * 6 + [hbm, hbm, vmem],
        out_specs=[vmem] * 8,
        compiler_params=pltpu.CompilerParams(vmem_limit_bytes=big),
        out_shape=[
            shape((half_rows, width), BF16),
            shape((half_rows, width), BF16),
            shape((heads, win, win), F32),
            shape((cells, 3 * width), BF16),
            shape((cells, width), F32),
            shape((cells, 128), F32),
            shape((cells, width), BF16),
            shape((width, 128), F32),
        ],
        scratch_shapes=[
            pltpu.VMEM((cells, width), F32),
            pltpu.VMEM((n_rows, width), F32),
            pltpu.VMEM((n_cols, width), F32),
            pltpu.VMEM((n_corner, width), F32),
            pltpu.VMEM((cells, width), F32),
            pltpu.VMEM((cells, width), BF16),
            pltpu.VMEM((cells, 3 * width), BF16),
            pltpu.VMEM((cells, width), BF16),
            pltpu.VMEM((width, win), BF16),
            pltpu.VMEM((width, win), BF16),
            pltpu.VMEM((2, heads, win, win), F32),
            pltpu.VMEM((width, cells), BF16),
            pltpu.VMEM((width, width), F32),
            pltpu.VMEM((2, half_rows, width), BF16),
            pltpu.VMEM((width, 3 * width), BF16),
            pltpu.VMEM((width, width), BF16),
            pltpu.SemaphoreType.DMA((2,)),
        ],
    )(info, tok, cot, *rim, norm_gain.reshape(1, width), qkv_weight, out_weight, bias)

    got = chips.core(send)
    piece = half_rows // ny
    outs = call(
        pair_sum_kernel,
        [shape((piece, width), BF16)] * ny,
        [],
        3,
        small_limit,
        smem_first=True,
    )(info, keep, got)

    outs, bias_sum = lax.optimization_barrier((outs, bias_sum))
    got = [outs[0]] + [chips.y(outs[k], k) for k in range(1, ny)]
    gain_row = norm_gain.reshape(1, width)
    small = call(
        lambda *refs: table_kernel(heads, *refs),
        shape((SMALL, width), F32),
        [pltpu.VMEM((heads * BANDS, SPAN), F32), pltpu.VMEM((heads, BANDS * SPAN), F32)],
        4,
        small_limit,
        cost=pl.CostEstimate(flops=3 * 10**9, bytes_accessed=10**6, transcendentals=0),
    )(index_t, bias_sum, gain_sum, gain_row)
    got, small = lax.optimization_barrier((got, small))
    part = piece // nx
    outs = call(
        lambda *refs: cross_sum_kernel(ny, nx, *refs),
        [shape((part, width), BF16)] * nx,
        [pltpu.VMEM((piece, width), F32)],
        1 + ny,
        small_limit,
        smem_first=True,
    )(info, *got)

    got = [outs[0]] + [chips.x(outs[k], k) for k in range(1, nx)]
    mine = call(
        join_sum_kernel,
        shape((part + 2 * SMALL, width), BF16),
        [],
        nx + 1,
        small_limit,
    )(*got, small)
    def layer_norm_back(first, count, proj):
        return call(
            lambda *refs: back_kernel(geo, first, count, *refs),
            shape((count * win, width), BF16),
            [],
            6,
            small_limit,
            cost=pl.CostEstimate(flops=3 * 10**9, bytes_accessed=10**7, transcendentals=0),
        )(proj, unit, inv, cot_win, gain_row, qkv_weight)

    half_wins = geo.nwin // 2
    halves = []
    bit = 1
    while bit < chips.nz:
        mine, grad_proj = lax.optimization_barrier((mine, grad_proj))
        got = chips.z(mine, bit)
        if len(halves) < 2:
            halves.append(layer_norm_back(len(halves) * half_wins, half_wins, grad_proj))
            got, halves[-1] = lax.optimization_barrier((got, halves[-1]))
        mine = call(z_sum_kernel, shape(mine.shape, BF16), [], 2, small_limit)(mine, got)
        bit *= 2

    def gathered(place, count, parts):
        rows = (parts[0].shape[0] - 2 * SMALL) * count + 2 * SMALL
        return call(
            lambda *refs: gather_kernel(place, *refs),
            shape((rows, width), BF16),
            [],
            1 + count,
            small_limit,
            smem_first=True,
        )(info, *parts)

    mine, halves = lax.optimization_barrier((mine, halves))
    b_rows, b_cols, b_corner = pad16(geo.n_rows), pad16(geo.n_cols), pad16(geo.n_corner)
    back = call(
        lambda *refs: unpack_send_kernel(geo, *refs),
        [shape((n, width), BF16) for n in (b_rows, b_cols, b_corner)],
        [
            pltpu.VMEM((cells, width), F32),
            pltpu.VMEM((b_rows + b_cols + b_corner, width), F32),
        ],
        2,
        small_limit,
    )(*halves)
    back = (moved(back[0], -1, 0), moved(back[1], 0, -1), moved(back[2], -1, -1))
    parts = [mine] + [chips.x(mine, k) for k in range(1, nx)]
    parts, back = lax.optimization_barrier((parts, back))
    mine = gathered(X, nx, parts)
    parts = [mine] + [chips.y(mine, k) for k in range(1, ny)]

    grad_tokens = call(
        lambda *refs: assemble_kernel(geo, *refs),
        shape((cells, width), BF16),
        [
            pltpu.VMEM((cells, width), F32),
            pltpu.VMEM((b_rows, width), F32),
            pltpu.VMEM((b_cols, width), F32),
            pltpu.VMEM((b_corner, width), F32),
            pltpu.VMEM((cells, width), F32),
        ],
        5,
        small_limit,
    )(*halves, *back)
    parts, grad_tokens = lax.optimization_barrier((parts, grad_tokens))
    mine = gathered(Y, ny, parts)
    other = chips.core(mine)

    outputs = [shape((width, 3 * width), F32), shape((width, width), F32)]
    scratch = [pltpu.VMEM((half_rows, width), F32), pltpu.SemaphoreType.DMA((2, 4))]
    params = pltpu.CompilerParams(vmem_limit_bytes=small_limit)
    written = pl.pallas_call(
        place_own_kernel,
        out_shape=outputs,
        in_specs=[smem, vmem],
        out_specs=[hbm, hbm],
        scratch_shapes=scratch,
        compiler_params=params,
    )(info, mine)
    grad_qkv, grad_out, line, grad_gain = pl.pallas_call(
        place_other_kernel,
        out_shape=outputs + [shape((heads, BANDS * SPAN), F32), shape((1, width), F32)],
        in_specs=[smem, vmem, vmem, hbm, hbm],
        out_specs=[hbm, hbm, vmem, vmem],
        input_output_aliases={3: 0, 4: 1},
        scratch_shapes=scratch,
        compiler_params=params,
    )(info, mine, other, *written)
    grad_bias = line.T[:entries]
    return (grad_tokens.reshape(tokens.shape), grad_qkv, grad_out, grad_bias, grad_gain.reshape(width))


def solution(mesh):
    in_specs = (P(None, "lat", "lon", None), P(), P(), P(), P(), P(), P(None, "lat", "lon", None))
    out_specs = (P(None, "lat", "lon", None), P(), P(), P(), P())
    return jax.shard_map(
        per_device, mesh=mesh, in_specs=in_specs, out_specs=out_specs, check_vma=False
    )
```

```python
import jax
import jax.numpy as jnp
from jax import lax
from jax.experimental import pallas as pl
from jax.experimental.pallas import tpu as pltpu
from jax.sharding import PartitionSpec as P

WH = 6
WW = 12
SH = 3
SW = 6
F32 = jnp.float32
BF16 = jnp.bfloat16
MIB = 1024 * 1024

LAST, CORE, X, Y = range(4)

NT = (((1,), (1,)), ((), ()))


def dot(a, b):
    return jnp.dot(a, b, preferred_element_type=F32)


def dot_nt(a, b):
    return lax.dot_general(a, b, NT, preferred_element_type=F32)


class Geometry:
    def __init__(self, depth, rows, cols):
        self.depth, self.rows, self.cols = depth, rows, cols
        self.cells = depth * rows * cols
        self.win = depth * WH * WW
        self.nwin = self.cells // self.win
        self.wins_lon = cols // WW
        self.wins_lat = rows // WH
        self.n_rows = depth * SH * (cols - SW)
        self.n_cols = depth * (rows - SH) * SW
        self.n_corner = depth * SH * SW

    def local(self, z, r, c):
        return (z * self.rows + r) * self.cols + c

    def rim_row(self, z, r):
        return (z * SH + r) * (self.cols - SW)

    def rim_col(self, z, r):
        return (z * (self.rows - SH) + r) * SW

    def corner(self, z, r):
        return (z * SH + r) * SW

    def cell(self, z, r, c):
        window = (r // WH) * self.wins_lon + c // WW
        return window * self.win + (z * WH + r % WH) * WW + c % WW


def pad16(n):
    return (n + 15) // 16 * 16


def forward_pieces(geo, z, r):
    own = geo.cols - SW
    if r < geo.rows - SH:
        first = ("local", geo.local(z, r + SH, SW), 0, own)
        second = ("cols", geo.rim_col(z, r), own, SW)
    else:
        first = ("rows", geo.rim_row(z, r - geo.rows + SH), 0, own)
        second = ("corner", geo.corner(z, r - geo.rows + SH), own, SW)
    return (first, second)


def window_cuts(start, length):
    at = start
    while at < start + length:
        stop = min(start + length, (at // WW + 1) * WW)
        yield at, stop - at
        at = stop


def pack_kernel(geo, tok_ref, cot_ref, rows_ref, cols_ref, corner_ref, top, left, wide, slim, buf, sems):
    n_rows, n_cols, n_corner = geo.n_rows, geo.n_cols, geo.n_corner
    base_cols = pad16(2 * n_rows)
    base_corner = base_cols + pad16(2 * n_cols)
    own = geo.cols - SW
    copies = []
    for which, ref in enumerate((tok_ref, cot_ref)):
        for part, (src, dst) in enumerate(
            (
                (ref.at[:, 0:SH], top.at[which]),
                (ref.at[0, SH : geo.rows, 0:16], left.at[which, 0]),
                (ref.at[1, SH : geo.rows, 0:16], left.at[which, 1]),
            )
        ):
            copy = pltpu.make_async_copy(src, dst, sems.at[which, part])
            copy.start()
            copies.append(copy)
    buf[base_cols - 16 : base_cols] = jnp.zeros((16, buf.shape[1]), F32)
    buf[base_corner - 16 : base_corner] = jnp.zeros((16, buf.shape[1]), F32)
    buf[-16:] = jnp.zeros((16, buf.shape[1]), F32)
    for copy in copies:
        copy.wait()
    wide[...] = top[...].astype(F32)
    slim[...] = left[...].astype(F32)
    for which in range(2):
        for z in range(geo.depth):
            for r in range(SH):
                at = which * n_rows + geo.rim_row(z, r)
                buf[at : at + own] = wide[which, z, r, SW:]
                at = base_corner + which * n_corner + geo.corner(z, r)
                buf[at : at + SW] = wide[which, z, r, 0:SW]
            for r in range(geo.rows - SH):
                at = base_cols + which * n_cols + geo.rim_col(z, r)
                buf[at : at + SW] = slim[which, z, r, 0:SW]
    rows_ref[...] = buf[0:base_cols].astype(BF16)
    cols_ref[...] = buf[base_cols:base_corner].astype(BF16)
    corner_ref[...] = buf[base_corner : base_corner + pad16(2 * n_corner)].astype(BF16)


BANDS = 8
SPAN = 96


def band_of(index):
    band = (index * 683) >> 16
    return band, index - band * SPAN


def lookup_kernel(heads, raw_ref, table_ref, bias_ref, idx_ref, split):
    win = idx_ref.shape[0]
    rows = heads * BANDS
    entries = table_ref.shape[1]
    idx_ref[...] = raw_ref[...].T
    split[...] = jnp.zeros_like(split)
    rest = table_ref[...]
    for part in range(3):
        low = rest.astype(BF16).astype(F32)
        for band in range(BANDS):
            at = part * rows + band * heads
            stop = min(entries, (band + 1) * SPAN)
            split[at : at + heads, 0 : stop - band * SPAN] = low[:, band * SPAN : stop]
        rest = rest - low
    table = split[...].astype(BF16)
    iota = lax.broadcasted_iota(jnp.int32, (SPAN, win), 0)

    def step(block, carry):
        start = pl.multiple_of(block * 8, 8)
        band, place = band_of(idx_ref[pl.ds(start, 8), :])
        for j in range(8):
            onehot = jnp.where(iota == place[j : j + 1, :], 1.0, 0.0).astype(BF16)
            found = dot(table, onehot)
            found = (found[:rows] + found[rows : 2 * rows]) + found[2 * rows :]
            mine = jnp.broadcast_to(band[j : j + 1, :], (heads, win))
            total = jnp.zeros((heads, win), F32)
            for b in range(BANDS):
                total = jnp.where(mine == b, found[b * heads : (b + 1) * heads], total)
            for h in range(heads):
                bias_ref[h, pl.ds(start + j, 1), :] = total[h : h + 1]
        return carry

    lax.fori_loop(0, win // 8, step, 0)


def table_sums(heads, first, count, idx_ref, sum_ref, acc):
    win = idx_ref.shape[0]
    rows = heads * BANDS
    iota = lax.broadcasted_iota(jnp.int32, (SPAN, win), 0)
    bands = lax.broadcasted_iota(jnp.int32, (BANDS, win), 0)

    def step(block, carry):
        start = pl.multiple_of(first + block * 8, 8)
        band, place = band_of(idx_ref[pl.ds(start, 8), :])
        tops, rests = [], []
        for h in range(heads):
            slab = sum_ref[h, pl.ds(start, 8), :]
            top = slab.astype(BF16).astype(F32)
            tops.append(top)
            rests.append(slab - top)
        total = None
        for j in range(8):
            onehot = jnp.where(iota == place[j : j + 1, :], 1.0, 0.0).astype(BF16)
            keep = jnp.where(bands == band[j : j + 1, :], 1.0, 0.0)
            spread = [p[h][j : j + 1, :] * keep for p in (tops, rests) for h in range(heads)]
            term = dot_nt(jnp.concatenate(spread, axis=0).astype(BF16), onehot)
            total = term if total is None else total + term
        acc[...] += total[:rows] + total[rows:]
        return carry

    lax.fori_loop(0, count // 8, step, 0)


def table_kernel(heads, idx_ref, sum_ref, gsum_ref, gain_ref, out_ref, acc, line):
    acc[...] = jnp.zeros_like(acc)
    table_sums(heads, 0, idx_ref.shape[0], idx_ref, sum_ref, acc)
    for h in range(heads):
        for b in range(BANDS):
            line[h : h + 1, b * SPAN : (b + 1) * SPAN] = acc[h * BANDS + b : h * BANDS + b + 1, :]
    width = out_ref.shape[1]
    more = BANDS * SPAN - width
    gain = jnp.sum(gsum_ref[...].T, axis=0, keepdims=True) / gain_ref[...]
    out_ref[0:heads, :] = line[:, :width]
    out_ref[heads:, 0:more] = line[:, width:]
    out_ref[heads:, more:] = jnp.zeros((16 - heads, width - more), F32)
    out_ref[heads : heads + 1, more:] = gain[:, : width - more]
    out_ref[heads + 1 : heads + 2, more:] = gain[:, width - more :]


def main_kernel(
    geo, heads, info_ref, tok_ref, cot_ref, rows_ref, cols_ref, corner_ref, gain_ref, wqkv_hbm,
    wout_hbm, bias_ref,
    send_ref, keep_ref, bsum_ref, dproj, ftok, inv, cotb, gsum_ref,
    loc, rim_rows, rim_cols, rim_corner, fcot, normed, proj, gatt, att_t, dq_t,
    bias2, normed_t, gout, grads, wqkv_ref, wout_ref, sems,
):
    copies = [
        pltpu.make_async_copy(wqkv_hbm, wqkv_ref, sems.at[0]),
        pltpu.make_async_copy(wout_hbm, wout_ref, sems.at[1]),
    ]
    for copy in copies:
        copy.start()
    width = ftok.shape[1]
    win = geo.win
    head_size = width // heads
    scale = head_size ** (-0.5)

    for which, (ref, dst) in enumerate(((tok_ref, ftok), (cot_ref, fcot))):
        loc[...] = ref[...].astype(F32)
        if which == 0:
            rim_rows[...] = rows_ref[...].astype(F32)
            rim_cols[...] = cols_ref[...].astype(F32)
            rim_corner[...] = corner_ref[...].astype(F32)
        sources = {
            "local": (loc, 0),
            "rows": (rim_rows, which * geo.n_rows),
            "cols": (rim_cols, which * geo.n_cols),
            "corner": (rim_corner, which * geo.n_corner),
        }
        for z in range(geo.depth):
            for r in range(geo.rows):
                for name, first, column, length in forward_pieces(geo, z, r):
                    src, base = sources[name]
                    for at, count in window_cuts(column, length):
                        begin = base + first + at - column
                        cell = geo.cell(z, r, at)
                        dst[cell : cell + count] = src[begin : begin + count]

    gain = gain_ref[...]

    spot = lax.broadcasted_iota(jnp.int32, (win, win), 0)
    other = lax.broadcasted_iota(jnp.int32, (win, win), 1)
    half = WH * WW
    polar_a = jnp.where(spot >= half, spot - half, spot) >= (WH - SH) * WW
    polar_b = jnp.where(other >= half, other - half, other) >= (WH - SH) * WW
    flag_a = jnp.where(polar_a, 1.0, 0.0)
    flag_b = jnp.where(polar_b, 1.0, 0.0)
    mask = jnp.where(flag_a == flag_b, 0.0, -1e30)
    for h in range(heads):
        plain = bias_ref[h]
        bias2[0, h] = plain
        bias2[1, h] = plain + mask
        bsum_ref[h] = jnp.zeros((win, win), F32)
    gout[...] = jnp.zeros_like(gout)

    def norm_step(w, carry):
        at = pl.ds(pl.multiple_of(w * win, 16), win)
        x = ftok[at, :]
        centred = x - jnp.mean(x, axis=-1, keepdims=True)
        istd = lax.rsqrt(jnp.mean(centred * centred, axis=-1, keepdims=True) + 1e-05)
        unit = centred * istd
        ftok[at, :] = unit
        inv[at, :] = jnp.broadcast_to(istd, (win, 128))
        normed[at, :] = (unit * gain).astype(BF16)
        cotb[at, :] = fcot[at, :].astype(BF16)
        return carry

    lax.fori_loop(0, geo.nwin, norm_step, 0)
    for copy in copies:
        copy.wait()

    def proj_step(w, carry):
        at = pl.ds(pl.multiple_of(w * (2 * win), 16), 2 * win)
        x = normed[at, :]
        for part in range(3):
            cols = slice(part * width, (part + 1) * width)
            proj[at, cols] = dot(x, wqkv_ref[:, cols]).astype(BF16)
        gatt[at, :] = dot_nt(cotb[at, :], wout_ref[...]).astype(BF16)
        return carry

    lax.fori_loop(0, geo.nwin // 2, proj_step, 0)

    lane = lax.broadcasted_iota(jnp.int32, (win, 128), 1)
    lower = lane < head_size
    polar_from = geo.nwin - geo.wins_lon

    def attend(w, carry):
        at = pl.ds(pl.multiple_of(w * win, 16), win)
        sel = jnp.where(w >= polar_from, info_ref[LAST], 0)
        k_t = proj[at, width : 2 * width].T
        v_t = proj[at, 2 * width :].T
        for pair in range(heads // 2):
            cols = slice(pair * 128, (pair + 1) * 128)
            q = proj[at, cols] * BF16(scale)
            k = proj[at, width + pair * 128 : width + (pair + 1) * 128]
            v = proj[at, 2 * width + pair * 128 : 2 * width + (pair + 1) * 128]
            g = gatt[at, cols]
            dv = None
            dk = None
            for side in range(2):
                h = 2 * pair + side
                keep = lower if side == 0 else jnp.logical_not(lower)
                qm = jnp.where(keep, q, BF16(0))
                gm = jnp.where(keep, g, BF16(0))
                scores = dot_nt(k, qm) + bias2[sel, h]
                top = jnp.max(scores, axis=0, keepdims=True)
                grown = jnp.exp(scores - top)
                probs = grown * (1.0 / jnp.sum(grown, axis=0, keepdims=True))
                probs_low = probs.astype(BF16)
                gprobs = dot_nt(v, gm)
                weighted = jnp.sum(probs * gprobs, axis=0, keepdims=True)
                gscores = probs * (gprobs - weighted)
                bsum_ref[h] += gscores
                scores_low = gscores.astype(BF16)
                feats = slice(h * head_size, (h + 1) * head_size)
                att_t[feats, :] = dot(v_t[feats], probs_low).astype(BF16)
                dq_t[feats, :] = (dot(k_t[feats], scores_low) * scale).astype(BF16)
                dv_term = dot(probs_low, gm)
                dk_term = dot(scores_low, qm)
                dv = dv_term if dv is None else dv + dv_term
                dk = dk_term if dk is None else dk + dk_term
            dproj[at, width + pair * 128 : width + (pair + 1) * 128] = dk.astype(BF16)
            dproj[at, 2 * width + pair * 128 : 2 * width + (pair + 1) * 128] = dv.astype(BF16)
        dproj[at, 0:width] = dq_t[...].T
        gout[...] += dot(att_t[...], cotb[at, :])
        return carry

    lax.fori_loop(0, geo.nwin, attend, 0)

    grads[1, width:, :] = gout[...].astype(BF16)
    for block in range(geo.cells // 128):
        rows = slice(block * 128, (block + 1) * 128)
        normed_t[:, rows] = normed[rows, :].T

    gsum = jnp.zeros((width, 128), F32)
    for part in range(3):
        half, first = part // 2, part % 2 * width
        for sub in range(2):
            cols = slice(part * width + sub * 256, part * width + (sub + 1) * 256)
            term = dot(normed_t[...], dproj[:, cols])
            grads[half, first : first + width, sub * 256 : (sub + 1) * 256] = term.astype(BF16)
            term = term * wqkv_ref[:, cols].astype(F32)
            gsum = gsum + (term[:, :128] + term[:, 128:])
    gsum_ref[...] = gsum
    keep_ref[...] = grads[info_ref[CORE]]
    send_ref[...] = grads[1 - info_ref[CORE]]


def back_kernel(geo, first, count, dproj, unit_ref, inv, cotb, gain_ref, wqkv_ref, gtok_ref):
    win = geo.win
    gain = gain_ref[...]

    def back_step(w, carry):
        at = pl.ds(pl.multiple_of((first + w) * win, 16), win)
        gn = dot_nt(dproj[at, :], wqkv_ref[...]).astype(BF16).astype(F32)
        unit = unit_ref[at, :]
        hat = gn * gain
        centre = jnp.mean(hat, axis=-1, keepdims=True)
        slope = jnp.mean(hat * unit, axis=-1, keepdims=True)
        istd = inv[at, 0:1]
        cot = cotb[at, :].astype(F32)
        to = pl.ds(pl.multiple_of(w * win, 16), win)
        gtok_ref[to, :] = (cot + istd * (hat - centre - unit * slope)).astype(BF16)
        return carry

    lax.fori_loop(0, count, back_step, 0)


def unpack_send_kernel(geo, low_ref, high_ref, rows_ref, cols_ref, corner_ref, fg, buf):
    base_cols = pad16(geo.n_rows)
    base_corner = base_cols + pad16(geo.n_cols)
    half = low_ref.shape[0]
    fg[0:half] = low_ref[...].astype(F32)
    fg[half:] = high_ref[...].astype(F32)
    buf[...] = jnp.zeros_like(buf)
    bases = {"rows": 0, "cols": base_cols, "corner": base_corner}
    for z in range(geo.depth):
        for r in range(geo.rows):
            for name, first, column, length in forward_pieces(geo, z, r):
                if name == "local":
                    continue
                for at, count in window_cuts(column, length):
                    to = bases[name] + first + at - column
                    cell = geo.cell(z, r, at)
                    buf[to : to + count] = fg[cell : cell + count]
    rows_ref[...] = buf[0:base_cols].astype(BF16)
    cols_ref[...] = buf[base_cols:base_corner].astype(BF16)
    corner_ref[...] = buf[base_corner : base_corner + pad16(geo.n_corner)].astype(BF16)


def assemble_kernel(geo, low_ref, high_ref, rows_ref, cols_ref, corner_ref, out_ref, fg, rr, rc, rk, grid):
    half = low_ref.shape[0]
    fg[0:half] = low_ref[...].astype(F32)
    fg[half:] = high_ref[...].astype(F32)
    rr[...] = rows_ref[...].astype(F32)
    rc[...] = cols_ref[...].astype(F32)
    rk[...] = corner_ref[...].astype(F32)
    own = geo.cols - SW
    for z in range(geo.depth):
        for r in range(geo.rows):
            for name, first, column, length in forward_pieces(geo, z, r):
                if name != "local":
                    continue
                for at, count in window_cuts(column, length):
                    to = first + at - column
                    cell = geo.cell(z, r, at)
                    grid[to : to + count] = fg[cell : cell + count]
        for r in range(SH):
            to = geo.local(z, r, SW)
            grid[to : to + own] = rr[geo.rim_row(z, r) : geo.rim_row(z, r) + own]
            to = geo.local(z, r, 0)
            grid[to : to + SW] = rk[geo.corner(z, r) : geo.corner(z, r) + SW]
        for r in range(geo.rows - SH):
            to = geo.local(z, r + SH, 0)
            grid[to : to + SW] = rc[geo.rim_col(z, r) : geo.rim_col(z, r) + SW]
    out_ref[...] = grid[...].astype(BF16)


def call(kernel, out_shapes, scratch, n_in, limit, smem_first=False, cost=None):
    specs = [pl.BlockSpec(memory_space=pltpu.VMEM)] * n_in
    if smem_first:
        specs[0] = pl.BlockSpec(memory_space=pltpu.SMEM)
    return pl.pallas_call(
        kernel,
        out_shape=out_shapes,
        in_specs=specs,
        out_specs=jax.tree.map(lambda s: pl.BlockSpec(memory_space=pltpu.VMEM), out_shapes),
        scratch_shapes=scratch,
        compiler_params=pltpu.CompilerParams(vmem_limit_bytes=limit),
        cost_estimate=cost,
    )


def shape(dims, dtype):
    return jax.ShapeDtypeStruct(dims, dtype)


def moved(value, lat_step, lon_step):
    lats, lons = lax.axis_size("lat"), lax.axis_size("lon")
    pairs = []
    for a in range(lats):
        for o in range(lons):
            target = ((a - lat_step) % lats) * lons + (o - lon_step) % lons
            pairs.append((a * lons + o, target))
    return lax.ppermute(value, ("lat", "lon"), pairs)


class Chips:
    def __init__(self):
        self.lats, self.lons = lax.axis_size("lat"), lax.axis_size("lon")
        self.nz, self.nx, self.ny = self.lats // 2, 4, self.lons // 4

    def split(self, device):
        lat, lon = device // self.lons, device % self.lons
        x = lon // (2 * self.ny) * 2 + lat % 2
        return lat // 2, x, lon // 2 % self.ny, lon % 2

    def join(self, z, x, y, core):
        return (z * 2 + x % 2) * self.lons + (x // 2 * self.ny + y) * 2 + core

    def send(self, value, change):
        pairs = []
        for device in range(self.lats * self.lons):
            z, x, y, core = change(*self.split(device))
            pairs.append((device, self.join(z, x, y, core)))
        return lax.ppermute(value, ("lat", "lon"), pairs)

    def core(self, value):
        return self.send(value, lambda z, x, y, c: (z, x, y, 1 - c))

    def x(self, value, step):
        return self.send(value, lambda z, x, y, c: (z, (x + step) % self.nx, y, c))

    def y(self, value, step):
        return self.send(value, lambda z, x, y, c: (z, x, (y + step) % self.ny, c))

    def z(self, value, bit):
        return self.send(value, lambda z, x, y, c: (z ^ (2 * bit - 1), x, y, c))


def part_rows(info_ref, place, step, count, rows):
    part = (info_ref[place] + step) & (count - 1)
    return pl.ds(pl.multiple_of(part * rows, 16), rows)


def pair_sum_kernel(info_ref, keep_ref, recv_ref, *outs):
    for k, ref in enumerate(outs):
        at = part_rows(info_ref, Y, k, len(outs), ref.shape[0])
        ref[...] = (keep_ref[at, :].astype(F32) + recv_ref[at, :].astype(F32)).astype(BF16)


def total_of(refs):
    total = refs[0][...].astype(F32)
    for ref in refs[1:]:
        total += ref[...].astype(F32)
    return total


def cross_sum_kernel(ny, nx, info_ref, *refs):
    outs, hold = refs[ny : ny + nx], refs[-1]
    hold[...] = total_of(refs[:ny])
    for k, ref in enumerate(outs):
        at = part_rows(info_ref, X, k, nx, ref.shape[0])
        ref[...] = hold[at, :].astype(BF16)


SMALL = 16


def put_small(ref, base, total):
    top = total.astype(BF16)
    ref[base : base + SMALL] = top
    ref[base + SMALL : base + 2 * SMALL] = (total - top.astype(F32)).astype(BF16)


def small_of(refs, base):
    total = None
    for ref in refs:
        for part in range(2):
            at = base + part * SMALL
            term = ref[at : at + SMALL].astype(F32)
            total = term if total is None else total + term
    return total


def join_sum_kernel(*refs):
    piece = refs[0].shape[0]
    small_ref, out_ref = refs[-2:]
    out_ref[0:piece] = total_of(refs[:-2]).astype(BF16)
    put_small(out_ref, piece, small_ref[...])


def z_sum_kernel(mine_ref, got_ref, out_ref):
    rows = mine_ref.shape[0] - 2 * SMALL
    out_ref[0:rows] = (mine_ref[0:rows].astype(F32) + got_ref[0:rows].astype(F32)).astype(BF16)
    put_small(out_ref, rows, small_of((mine_ref, got_ref), rows))


def gather_kernel(place, info_ref, *refs):
    ins, out_ref = refs[:-1], refs[-1]
    piece = ins[0].shape[0] - 2 * SMALL
    for k, ref in enumerate(ins):
        at = part_rows(info_ref, place, len(ins) - k, len(ins), piece)
        out_ref[at, :] = ref[0:piece]
    put_small(out_ref, len(ins) * piece, small_of(ins, piece))


def place_rows(half, value_ref, gqkv_ref, gout_ref, hold, sems):
    width = gout_ref.shape[1]
    steps = 4
    rows = width // steps

    def write(targets):
        copies = []
        for which, target in enumerate(targets):
            for step in range(steps):
                at = slice(step * rows, (step + 1) * rows)
                src = slice(which * width + step * rows, which * width + (step + 1) * rows)
                hold[src] = value_ref[src].astype(F32)
                copy = pltpu.make_async_copy(
                    hold.at[src], target.at[at], sems.at[which, step]
                )
                copy.start()
                copies.append(copy)
        for copy in copies:
            copy.wait()

    @pl.when(half == 0)
    def _():
        write((gqkv_ref.at[:, 0:width], gqkv_ref.at[:, width : 2 * width]))

    @pl.when(half == 1)
    def _():
        write((gqkv_ref.at[:, 2 * width :], gout_ref))


def place_own_kernel(info_ref, mine_ref, gqkv_ref, gout_ref, hold, sems):
    place_rows(info_ref[CORE], mine_ref, gqkv_ref, gout_ref, hold, sems)


def place_other_kernel(
    info_ref, mine_ref, got_ref, gqkv_in, gout_in, gqkv_ref, gout_ref, line_ref, gain_ref, hold, sems
):
    width = gout_ref.shape[1]
    total = small_of((mine_ref, got_ref), 2 * width)
    more = line_ref.shape[1] - width
    line_ref[:, 0:width] = total[0:8]
    line_ref[:, width:] = total[8:, 0:more]
    gain_ref[:, 0 : width - more] = total[8:9, more:]
    gain_ref[:, width - more :] = total[9:10, more:]
    place_rows(1 - info_ref[CORE], got_ref, gqkv_ref, gout_ref, hold, sems)


def per_device(tokens, norm_gain, qkv_weight, out_weight, bias_table, bias_index, cotangent):
    depth, rows_lat, cols_lon, width = tokens.shape
    entries, heads = bias_table.shape
    geo = Geometry(depth, rows_lat, cols_lon)
    win, cells = geo.win, geo.cells
    tok = tokens.reshape(cells, width)
    cot = cotangent.reshape(cells, width)

    n_rows, n_cols, n_corner = pad16(2 * geo.n_rows), pad16(2 * geo.n_cols), pad16(2 * geo.n_corner)
    rim = pl.pallas_call(
        lambda *refs: pack_kernel(geo, *refs),
        out_shape=[shape((n, width), BF16) for n in (n_rows, n_cols, n_corner)],
        in_specs=[pl.BlockSpec(memory_space=pltpu.HBM)] * 2,
        out_specs=[pl.BlockSpec(memory_space=pltpu.VMEM)] * 3,
        scratch_shapes=[
            pltpu.VMEM((2, depth, SH, cols_lon, width), BF16),
            pltpu.VMEM((2, depth, rows_lat - SH, 16, width), BF16),
            pltpu.VMEM((2, depth, SH, cols_lon, width), F32),
            pltpu.VMEM((2, depth, rows_lat - SH, 16, width), F32),
            pltpu.VMEM((n_rows + n_cols + n_corner, width), F32),
            pltpu.SemaphoreType.DMA((2, 3)),
        ],
        compiler_params=pltpu.CompilerParams(vmem_limit_bytes=60 * MIB),
    )(tokens, cotangent)
    rim = (moved(rim[0], 1, 0), moved(rim[1], 0, 1), moved(rim[2], 1, 1))

    bias, index_t = call(
        lambda *refs: lookup_kernel(heads, *refs),
        [shape((heads, win, win), F32), shape((win, win), jnp.int32)],
        [pltpu.VMEM((3 * heads * BANDS, SPAN), F32)],
        2,
        8 * MIB,
        cost=pl.CostEstimate(flops=4 * 10**9, bytes_accessed=10**6, transcendentals=0),
    )(bias_index, bias_table.T)

    chips = Chips()
    ny, nx = chips.ny, chips.nx
    lat, lon = lax.axis_index("lat"), lax.axis_index("lon")
    is_last = (lat == chips.lats - 1).astype(jnp.int32)
    info = jnp.stack([is_last, lon % 2, lon // (2 * ny) * 2 + lat % 2, lon // 2 % ny])
    half_rows = 2 * width
    big = 36 * MIB
    small_limit = 10 * MIB

    vmem, smem = pl.BlockSpec(memory_space=pltpu.VMEM), pl.BlockSpec(memory_space=pltpu.SMEM)
    hbm = pl.BlockSpec(memory_space=pltpu.HBM)
    send, keep, bias_sum, grad_proj, unit, inv, cot_win, gain_sum = pl.pallas_call(
        lambda *refs: main_kernel(geo, heads, *refs),
        in_specs=[smem] + [vmem] * 6 + [hbm, hbm, vmem],
        out_specs=[vmem] * 8,
        compiler_params=pltpu.CompilerParams(vmem_limit_bytes=big),
        out_shape=[
            shape((half_rows, width), BF16),
            shape((half_rows, width), BF16),
            shape((heads, win, win), F32),
            shape((cells, 3 * width), BF16),
            shape((cells, width), F32),
            shape((cells, 128), F32),
            shape((cells, width), BF16),
            shape((width, 128), F32),
        ],
        scratch_shapes=[
            pltpu.VMEM((cells, width), F32),
            pltpu.VMEM((n_rows, width), F32),
            pltpu.VMEM((n_cols, width), F32),
            pltpu.VMEM((n_corner, width), F32),
            pltpu.VMEM((cells, width), F32),
            pltpu.VMEM((cells, width), BF16),
            pltpu.VMEM((cells, 3 * width), BF16),
            pltpu.VMEM((cells, width), BF16),
            pltpu.VMEM((width, win), BF16),
            pltpu.VMEM((width, win), BF16),
            pltpu.VMEM((2, heads, win, win), F32),
            pltpu.VMEM((width, cells), BF16),
            pltpu.VMEM((width, width), F32),
            pltpu.VMEM((2, half_rows, width), BF16),
            pltpu.VMEM((width, 3 * width), BF16),
            pltpu.VMEM((width, width), BF16),
            pltpu.SemaphoreType.DMA((2,)),
        ],
    )(info, tok, cot, *rim, norm_gain.reshape(1, width), qkv_weight, out_weight, bias)

    got = chips.core(send)
    piece = half_rows // ny
    outs = call(
        pair_sum_kernel,
        [shape((piece, width), BF16)] * ny,
        [],
        3,
        small_limit,
        smem_first=True,
    )(info, keep, got)

    outs, bias_sum = lax.optimization_barrier((outs, bias_sum))
    got = [outs[0]] + [chips.y(outs[k], k) for k in range(1, ny)]
    gain_row = norm_gain.reshape(1, width)
    small = call(
        lambda *refs: table_kernel(heads, *refs),
        shape((SMALL, width), F32),
        [pltpu.VMEM((heads * BANDS, SPAN), F32), pltpu.VMEM((heads, BANDS * SPAN), F32)],
        4,
        small_limit,
        cost=pl.CostEstimate(flops=3 * 10**9, bytes_accessed=10**6, transcendentals=0),
    )(index_t, bias_sum, gain_sum, gain_row)
    got, small = lax.optimization_barrier((got, small))
    part = piece // nx
    outs = call(
        lambda *refs: cross_sum_kernel(ny, nx, *refs),
        [shape((part, width), BF16)] * nx,
        [pltpu.VMEM((piece, width), F32)],
        1 + ny,
        small_limit,
        smem_first=True,
    )(info, *got)

    got = [outs[0]] + [chips.x(outs[k], k) for k in range(1, nx)]
    mine = call(
        join_sum_kernel,
        shape((part + 2 * SMALL, width), BF16),
        [],
        nx + 1,
        small_limit,
    )(*got, small)
    def layer_norm_back(first, count, proj):
        return call(
            lambda *refs: back_kernel(geo, first, count, *refs),
            shape((count * win, width), BF16),
            [],
            6,
            small_limit,
            cost=pl.CostEstimate(flops=3 * 10**9, bytes_accessed=10**7, transcendentals=0),
        )(proj, unit, inv, cot_win, gain_row, qkv_weight)

    half_wins = geo.nwin // 2
    halves = []
    bit = 1
    while bit < chips.nz:
        mine, grad_proj = lax.optimization_barrier((mine, grad_proj))
        got = chips.z(mine, bit)
        if len(halves) < 2:
            halves.append(layer_norm_back(len(halves) * half_wins, half_wins, grad_proj))
            got, halves[-1] = lax.optimization_barrier((got, halves[-1]))
        mine = call(z_sum_kernel, shape(mine.shape, BF16), [], 2, small_limit)(mine, got)
        bit *= 2

    def gathered(place, count, parts):
        rows = (parts[0].shape[0] - 2 * SMALL) * count + 2 * SMALL
        return call(
            lambda *refs: gather_kernel(place, *refs),
            shape((rows, width), BF16),
            [],
            1 + count,
            small_limit,
            smem_first=True,
        )(info, *parts)

    mine, halves = lax.optimization_barrier((mine, halves))
    b_rows, b_cols, b_corner = pad16(geo.n_rows), pad16(geo.n_cols), pad16(geo.n_corner)
    back = call(
        lambda *refs: unpack_send_kernel(geo, *refs),
        [shape((n, width), BF16) for n in (b_rows, b_cols, b_corner)],
        [
            pltpu.VMEM((cells, width), F32),
            pltpu.VMEM((b_rows + b_cols + b_corner, width), F32),
        ],
        2,
        small_limit,
    )(*halves)
    back = (moved(back[0], -1, 0), moved(back[1], 0, -1), moved(back[2], -1, -1))
    parts = [mine] + [chips.x(mine, k) for k in range(1, nx)]
    parts, back = lax.optimization_barrier((parts, back))
    mine = gathered(X, nx, parts)
    ahead, behind = chips.y(mine, 1), chips.y(mine, ny - 1)
    cut = mine.shape[0] // 2
    far = jnp.concatenate([chips.y(ahead[:cut], 1), chips.y(behind[cut:], ny - 1)])
    parts = [mine, ahead, far, behind]

    grad_tokens = call(
        lambda *refs: assemble_kernel(geo, *refs),
        shape((cells, width), BF16),
        [
            pltpu.VMEM((cells, width), F32),
            pltpu.VMEM((b_rows, width), F32),
            pltpu.VMEM((b_cols, width), F32),
            pltpu.VMEM((b_corner, width), F32),
            pltpu.VMEM((cells, width), F32),
        ],
        5,
        small_limit,
    )(*halves, *back)
    parts, grad_tokens = lax.optimization_barrier((parts, grad_tokens))
    mine = gathered(Y, ny, parts)
    other = chips.core(mine)

    outputs = [shape((width, 3 * width), F32), shape((width, width), F32)]
    scratch = [pltpu.VMEM((half_rows, width), F32), pltpu.SemaphoreType.DMA((2, 4))]
    params = pltpu.CompilerParams(vmem_limit_bytes=small_limit)
    written = pl.pallas_call(
        place_own_kernel,
        out_shape=outputs,
        in_specs=[smem, vmem],
        out_specs=[hbm, hbm],
        scratch_shapes=scratch,
        compiler_params=params,
    )(info, mine)
    grad_qkv, grad_out, line, grad_gain = pl.pallas_call(
        place_other_kernel,
        out_shape=outputs + [shape((heads, BANDS * SPAN), F32), shape((1, width), F32)],
        in_specs=[smem, vmem, vmem, hbm, hbm],
        out_specs=[hbm, hbm, vmem, vmem],
        input_output_aliases={3: 0, 4: 1},
        scratch_shapes=scratch,
        compiler_params=params,
    )(info, mine, other, *written)
    grad_bias = line.T[:entries]
    return (grad_tokens.reshape(tokens.shape), grad_qkv, grad_out, grad_bias, grad_gain.reshape(width))


def solution(mesh):
    in_specs = (P(None, "lat", "lon", None), P(), P(), P(), P(), P(), P(None, "lat", "lon", None))
    out_specs = (P(None, "lat", "lon", None), P(), P(), P(), P())
    return jax.shard_map(
        per_device, mesh=mesh, in_specs=in_specs, out_specs=out_specs, check_vma=False
    )
```
